32 devices in a mesh: grp: 2 (over x), dev: 16 (over z, y, core).
Axes of the slice: x: 2, y: 2, z: 4, core: 2. Of those that a mesh axis runs over, the one named last changes fastest.
Arguments:
- diag_inverse: bfloat16 [64, 512, 512], P(('grp', 'dev')), may hold values from -1 to 1.5, as said below
- lower_block: bfloat16 [64, 512, 512], P(('grp', 'dev')), may hold values from -0.15625 to 0.15625
- upper_block: bfloat16 [64, 512, 512], P(('grp', 'dev')), may hold values from -0.15625 to 0.15625
- right_side: bfloat16 [64, 512, 128], P(('grp', 'dev')), may hold values from -6 to 6
Outputs:
- solution: bfloat16 [64, 512, 128], P(('grp', 'dev'))
The draws below stay inside these ranges and needn't reach their ends.
Inputs may be any that keep to these rules, and one draw needn't show every extreme that they name: diag_inverse holds the given inverses of the diagonal blocks.
All inputs are finite; a program needn't handle non-finite values.
Results may differ from the reference program's by a relative error of at most 0.013.
Values may be sent and summed in bfloat16 or wider, within the bound.
No kernel may reach another device: no remote copies, remote signals or barrier semaphores. Data moves between devices by JAX's collectives and lax.ppermute only.
A program may use at most 64 MiB of HBM per device.

```python
import math
import jax
import jax.numpy as jnp
from jax import lax

BLOCK = 512
NRHS = 128
NBLOCKS = 64


def draw_diag_inverse(key, part):
    first_key, second_key = jax.random.split(jax.random.fold_in(key, 17), 2)
    identity = jnp.eye(BLOCK, dtype=jnp.float32)
    offdiag = jnp.clip(jax.random.normal(first_key, (NBLOCKS, BLOCK, BLOCK), jnp.float32), -4.0, 4.0) * (0.4 / math.sqrt(BLOCK))
    diagonal = jax.random.uniform(second_key, (NBLOCKS, BLOCK), jnp.float32, 0.7, 1.3)
    whole = offdiag * (1.0 - identity)[None] + identity[None] * diagonal[:, :, None]
    return whole.astype(jnp.bfloat16)


def shard_levels(key, dims, cuts, least, high):
    level, own = 1.0, jax.random.fold_in(key, 6)
    for dim, shards_of in cuts:
        steps = jnp.exp(jax.random.uniform(jax.random.fold_in(own, dim), (shards_of,), jnp.float32, least / len(cuts), high / len(cuts)))
        level = level * jnp.repeat(steps, dims[dim] // shards_of).reshape([-1 if axis == dim else 1 for axis in range(len(dims))])
    return level


def centred(stream_key, shape, deviation, bound, shards=(), kind=jnp.bfloat16):
    result = jax.random.normal(stream_key, shape, jnp.float32) * deviation
    if len(shards) > 0:
        result = shard_levels(stream_key, shape, shards, -0.22, 0.18) * result
    return jnp.clip(result, min=-bound, max=bound).astype(kind)


def setup_inputs(seed: int = 0) -> dict:
    streams_of = jax.random.split(jax.random.key(seed), 5)
    return {
        "diag_inverse": draw_diag_inverse(jax.random.fold_in(streams_of[4], 71), 0),
        "lower_block": centred(streams_of[1], (NBLOCKS, BLOCK, BLOCK), (3 * BLOCK) ** -0.5, 0.15625, ((0, 32),)),
        "upper_block": centred(streams_of[2], (NBLOCKS, BLOCK, BLOCK), (3 * BLOCK) ** -0.5, 0.15625, ((0, 32),)),
        "right_side": centred(streams_of[3], (NBLOCKS, BLOCK, NRHS), 1.0, 6.0, ((0, 32),)),
    }


def reduce_panel(middle, left_panel, right_panel, order):
    left_spike = middle[:, :order]
    right_spike = middle[:, order:2 * order]
    own_rhs = middle[:, 2 * order:]
    from_left = jnp.dot(left_spike, left_panel, preferred_element_type=jnp.float32)
    from_right = jnp.dot(right_spike, right_panel, preferred_element_type=jnp.float32)
    coupling = from_left[:, order:2 * order] + from_right[:, :order]
    scaling = (jnp.eye(order, dtype=jnp.float32) + coupling).astype(jnp.bfloat16)
    outer_left = from_left[:, :order].astype(jnp.bfloat16)
    outer_right = from_right[:, order:2 * order].astype(jnp.bfloat16)
    remaining = (own_rhs.astype(jnp.float32) - from_left[:, 2 * order:] - from_right[:, 2 * order:]).astype(jnp.bfloat16)
    combined = jnp.concatenate([-outer_left, -outer_right, remaining], axis=1)
    return jnp.dot(scaling, combined, preferred_element_type=jnp.float32).astype(jnp.bfloat16)


def apply_panel(middle, left_values, right_values, order):
    left_spike = middle[:, :order]
    right_spike = middle[:, order:2 * order]
    own_rhs = middle[:, 2 * order:].astype(jnp.float32)
    total = own_rhs - jnp.dot(left_spike, left_values, preferred_element_type=jnp.float32)
    total = total - jnp.dot(right_spike, right_values, preferred_element_type=jnp.float32)
    return total.astype(jnp.bfloat16)


def reduce_level(panels, order):
    count = panels.shape[0]
    zero_row = jnp.zeros((1,) + panels.shape[1:], panels.dtype)
    padded = jnp.concatenate([zero_row, panels, zero_row], axis=0)
    middles = panels[0::2]
    lefts = padded[0:count:2]
    rights = padded[2:count + 2:2]
    return lax.map(lambda items: reduce_panel(items[0], items[1], items[2], order), (middles, lefts, rights))


def reduce_every(panels, order):
    count = panels.shape[0]
    zero_row = jnp.zeros((1,) + panels.shape[1:], panels.dtype)
    padded = jnp.concatenate([zero_row, panels, zero_row], axis=0)
    return lax.map(lambda items: reduce_panel(items[0], items[1], items[2], order), (panels, padded[0:count], padded[2:count + 2]))


def refine(panels, coarse, order):
    zero_row = jnp.zeros((1,) + coarse.shape[1:], coarse.dtype)
    padded = jnp.concatenate([coarse, zero_row], axis=0)
    odd_panels = panels[1::2]
    odd_values = lax.map(lambda items: apply_panel(items[0], items[1], items[2], order), (odd_panels, coarse, padded[1:]))
    return jnp.stack([coarse, odd_values], axis=1).reshape((-1,) + coarse.shape[1:])


def make_panel(items):
    stacked = jnp.concatenate([items[1], items[2], items[3]], axis=1)
    return jnp.dot(items[0], stacked, preferred_element_type=jnp.float32).astype(jnp.bfloat16)


def reference(diag_inverse, lower_block, upper_block, right_side):
    order = BLOCK
    panels = lax.map(make_panel, (diag_inverse, lower_block, upper_block, right_side))
    level_one = reduce_level(panels, order)
    level_two = reduce_every(level_one, order)
    coarse = level_two[:, :, 2 * order:]
    count = coarse.shape[0]
    zero_rows = jnp.zeros((2,) + coarse.shape[1:], coarse.dtype)
    padded = jnp.concatenate([zero_rows, coarse, zero_rows], axis=0)
    top_values = lax.map(lambda items: apply_panel(items[0], items[1], items[2], order), (level_two, padded[0:count], padded[4:count + 4]))
    return refine(panels, top_values, order)
```

```python
import functools

import jax
import jax.numpy as jnp
from jax import lax
from jax.experimental import pallas as pl
from jax.experimental.pallas import tpu as pltpu
from jax.sharding import PartitionSpec as P

AXES = ("grp", "dev")
BF16 = jnp.bfloat16
F32 = jnp.float32
EVEN, ODD = 0, 1


def dot(a, b):
    return jnp.dot(a, b, preferred_element_type=F32)


def on_parity(parity, kernel):
    def guarded(*refs):
        @pl.when(lax.rem(lax.axis_index(AXES), 2) == parity)
        def _():
            kernel(*refs)

    return guarded


def local_call(kernel, outs, ins, flops, in_hbm=0, scratch=()):
    vmem = pl.BlockSpec(memory_space=pltpu.VMEM)
    anywhere = pl.BlockSpec(memory_space=pl.ANY)
    many = len(outs) > 1
    return pl.pallas_call(
        kernel,
        out_shape=outs if many else outs[0],
        in_specs=[anywhere] * in_hbm + [vmem] * (len(ins) - in_hbm),
        out_specs=[vmem] * len(outs) if many else vmem,
        scratch_shapes=list(scratch),
        compiler_params=pltpu.CompilerParams(vmem_limit_bytes=16 * 1024 * 1024),
        cost_estimate=pl.CostEstimate(flops=flops, bytes_accessed=0, transcendentals=0),
    )(*ins)


def bf16_array(rows, columns):
    return jax.ShapeDtypeStruct((rows, columns), BF16)


def f32_array(rows, columns):
    return jax.ShapeDtypeStruct((rows, columns), F32)


def fetch(source, row, target, sem):
    copy = pltpu.make_async_copy(source.at[row], target, sem)
    copy.start()
    return copy


def second_row(order, diag, upper, right, out, diag_b, upper_b, right_b, sems):
    copies = [
        fetch(diag, 1, diag_b, sems.at[0]),
        fetch(upper, 1, upper_b, sems.at[1]),
        fetch(right, 1, right_b, sems.at[2]),
    ]
    copies[0].wait()
    copies[1].wait()
    out[:, :order] = dot(diag_b[...], upper_b[...]).astype(BF16)
    copies[2].wait()
    out[:, order:] = dot(diag_b[...], right_b[...]).astype(BF16)


def second_row_rest(order, diag, upper, right, made, out, diag_b, upper_b, right_b, sems):
    odd = lax.rem(lax.axis_index(AXES), 2) == ODD

    @pl.when(odd)
    def _():
        copy = pltpu.make_async_copy(made, out, sems.at[0])
        copy.start()
        copy.wait()

    @pl.when(jnp.logical_not(odd))
    def _():
        second_row(order, diag, upper, right, out, diag_b, upper_b, right_b, sems)


def own_products(
    order, diag, lower, upper, right, vg_b, w_a, w_b, m, n, r,
    diag_a, lower_a, upper_a, right_a, diag_b, lower_b, sems,
):
    d_a = fetch(diag, 0, diag_a, sems.at[0])
    u_a = fetch(upper, 0, upper_a, sems.at[1])
    d_b = fetch(diag, 1, diag_b, sems.at[2])
    l_b = fetch(lower, 1, lower_b, sems.at[3])
    l_a = fetch(lower, 0, lower_a, sems.at[4])
    r_a = fetch(right, 0, right_a, sems.at[5])
    d_a.wait()
    u_a.wait()
    v_a = dot(diag_a[...], upper_a[...]).astype(BF16)
    d_b.wait()
    l_b.wait()
    w_b[...] = dot(diag_b[...], lower_b[...]).astype(BF16)
    l_a.wait()
    w_a[...] = dot(diag_a[...], lower_a[...]).astype(BF16)
    r_a.wait()
    g_a = dot(diag_a[...], right_a[...]).astype(BF16)
    n[...] = dot(v_a, vg_b[:, :order]).astype(BF16)
    r[...] = g_a.astype(F32) - dot(v_a, vg_b[:, order:])
    m[...] = dot(v_a, w_b[...])


def scale_one(order, w_a, m, r, vg_left, scale, tg):
    eye = (
        lax.broadcasted_iota(jnp.int32, (order, order), 0)
        == lax.broadcasted_iota(jnp.int32, (order, order), 1)
    ).astype(F32)
    scale[...] = (eye + (dot(w_a[...], vg_left[:, :order]) + m[...])).astype(BF16)
    rest = (r[...] - dot(w_a[...], vg_left[:, order:])).astype(BF16)
    tg[:, :order] = dot(scale[...], w_a[...]).astype(BF16)
    tg[:, order:] = dot(scale[...], rest).astype(BF16)


def spikes_one(order, scale, n, w_b, tg, v_one, w_vg):
    v_one[...] = (-dot(scale[...], n[...])).astype(BF16)
    w_vg[:, :order] = dot(w_b[...], v_one[...]).astype(BF16)
    w_vg[:, order:] = dot(w_b[...], tg[:, order:]).astype(BF16)


def level_one_odd(order, w_a, m, r, vg_left, n, w_b, tg, v_one, w_vg, scale):
    scale_one(order, w_a, m, r, vg_left, scale, tg)
    spikes_one(order, scale, n, w_b, tg, v_one, w_vg)


def scaled_two(order, v, tg, v_one, w_b, w_vg_left, t_right):
    v16 = v.astype(BF16)
    t = tg[:, :order]
    from_left = dot(t, dot(w_vg_left[:, :order], v16).astype(BF16))
    own = dot(w_b[...], v16).astype(BF16)
    from_right = dot(v_one[...], dot(t_right[:, :order], own).astype(BF16))
    return v - from_left - from_right


def right_side_two(order, tg, v_one, w_vg_left, tg_right):
    return (
        tg[:, order:].astype(F32)
        + dot(tg[:, :order], w_vg_left[:, order:])
        - dot(v_one[...], tg_right[:, order:])
    )


def level_two(order, tg, v_one, w_b, w_vg_left, tg_right, g_two, w_g):
    h = right_side_two(order, tg, v_one, w_vg_left, tg_right)
    g_two[...] = scaled_two(order, h, tg, v_one, w_b, w_vg_left, tg_right).astype(BF16)
    w_g[...] = dot(w_b[...], g_two[...]).astype(BF16)


def level_two_odd(order, tg, v_one, w_b, w_vg_left, tg_right, g_right, g_v, w_g):
    h = right_side_two(order, tg, v_one, w_vg_left, tg_right)
    g_v[:, : h.shape[1]] = scaled_two(order, h, tg, v_one, w_b, w_vg_left, tg_right).astype(BF16)
    w_g[...] = dot(w_b[...], g_v[:, : h.shape[1]]).astype(BF16)
    g_v[:, h.shape[1] :] = dot(v_one[...], g_right[...]).astype(BF16)


def pass_right(order, tg, w_b, from_left, out):
    out[...] = dot(w_b[...], (-dot(tg[:, :order], from_left[...])).astype(BF16)).astype(BF16)


def pass_left(v_one, g_v, out):
    out[...] = dot(v_one[...], g_v[:, : out.shape[1]]).astype(BF16)


def top_value(order, g, tg, v_one, w_b, w_vg_left, t_right, p, q):
    h = dot(v_one[...], q) - dot(tg[:, :order], p[...])
    scaled = scaled_two(order, h, tg, v_one, w_b, w_vg_left, t_right)
    return (g.astype(F32) + scaled).astype(BF16)


def top_even(order, g_two, tg, v_one, w_b, w_vg_left, t_right, p, g_v, x):
    columns = x.shape[1]
    x[...] = top_value(
        order, g_two[...], tg, v_one, w_b, w_vg_left, t_right, p, g_v[:, columns:]
    )


def top_odd(order, g_v, tg, v_one, w_b, w_vg_left, t_right, p, q, x):
    columns = x.shape[1]
    x[...] = top_value(
        order, g_v[:, :columns], tg, v_one, w_b, w_vg_left, t_right, p, q[...]
    )


def finish(order, vg_b, w_b, x_even, x_odd, x_next_odd, x_next_even, out):
    odd = lax.rem(lax.axis_index(AXES), 2) == ODD

    def rows(x, x_next):
        out[0] = x[...]
        out[1] = (
            vg_b[:, order:].astype(F32) - dot(w_b[...], x[...]) - dot(vg_b[:, :order], x_next[...])
        ).astype(BF16)

    @pl.when(odd)
    def _():
        rows(x_odd, x_next_even)

    @pl.when(jnp.logical_not(odd))
    def _():
        rows(x_even, x_next_odd)


def body(diag, lower, upper, right):
    order, rhs = diag.shape[1], right.shape[2]
    count = lax.axis_size(AXES)
    evens, odds = range(0, count, 2), range(1, count, 2)
    pairs_right = [(i, i + 1) for i in evens if i + 1 < count]
    pairs_left = [(i + 1, i) for i in evens if i + 1 < count]
    gaps_right = [(i, i + 1) for i in odds if i + 1 < count]
    gaps_left = [(i + 1, i) for i in odds if i + 1 < count]

    def sent(block, route):
        return lax.ppermute(block, AXES, route)

    part = functools.partial
    square = 2 * order**3
    thin = 2 * order * order * rhs
    block = pltpu.VMEM((order, order), BF16)
    side = pltpu.VMEM((order, rhs), BF16)
    wide = bf16_array(order, order + rhs)
    full = bf16_array(order, order)
    slim = bf16_array(order, rhs)
    twin = bf16_array(order, 2 * rhs)

    row_scratch = (block, block, side, pltpu.SemaphoreType.DMA((3,)))
    vg_odd = local_call(
        on_parity(ODD, part(second_row, order)),
        [wide], [diag, upper, right], square + thin, 3, row_scratch,
    )
    vg_gap = sent(vg_odd, gaps_right)
    vg_b = local_call(
        part(second_row_rest, order),
        [wide], [diag, upper, right, vg_odd], square + thin, 4, row_scratch,
    )
    vg_pair = sent(vg_b, pairs_right)
    w_a, w_b, m, n, r = local_call(
        part(own_products, order),
        [full, full, f32_array(order, order), full, f32_array(order, rhs)],
        [diag, lower, upper, right, vg_b], 5 * square + 2 * thin, 4,
        (block, block, block, side, block, block, pltpu.SemaphoreType.DMA((6,))),
    )

    tg_odd, v_odd, w_vg_odd = local_call(
        on_parity(ODD, part(level_one_odd, order)),
        [wide, full, wide], [w_a, m, r, vg_pair, n, w_b], 4 * square + 3 * thin, 0, (block,),
    )
    w_vg_gap = sent(w_vg_odd, gaps_right)
    tg_pair = sent(tg_odd, pairs_left)

    scale_even, tg_even = local_call(
        on_parity(EVEN, part(scale_one, order)),
        [full, wide], [w_a, m, r, vg_gap], 2 * square + 2 * thin,
    )
    tg_gap = sent(tg_even, gaps_left)
    v_even, w_vg_even = local_call(
        on_parity(EVEN, part(spikes_one, order)),
        [full, wide], [scale_even, n, w_b, tg_even], 2 * square + thin,
    )
    w_vg_pair = sent(w_vg_even, pairs_right)

    g_even, w_g_even = local_call(
        on_parity(EVEN, part(level_two, order)),
        [slim, slim], [tg_even, v_even, w_b, w_vg_gap, tg_pair], 8 * thin,
    )
    g_gap = sent(g_even, gaps_left)
    a_pair = sent(w_g_even, pairs_right)
    p_odd = local_call(
        on_parity(ODD, part(pass_right, order)), [slim], [tg_odd, w_b, a_pair], 2 * thin
    )
    p_gap = sent(p_odd, gaps_right)

    g_v_odd, w_g_odd = local_call(
        on_parity(ODD, part(level_two_odd, order)),
        [twin, slim], [tg_odd, v_odd, w_b, w_vg_pair, tg_gap, g_gap], 9 * thin,
    )
    g_v_pair = sent(g_v_odd, pairs_left)
    a_gap = sent(w_g_odd, gaps_right)

    q_even = local_call(on_parity(EVEN, pass_left), [slim], [v_even, g_v_pair], thin)
    q_gap = sent(q_even, gaps_left)
    x_even = local_call(
        on_parity(EVEN, part(top_even, order)),
        [slim], [g_even, tg_even, v_even, w_b, w_vg_gap, tg_pair, p_gap, g_v_pair], 7 * thin,
    )
    x_gap = sent(x_even, gaps_left)
    p_even = local_call(
        on_parity(EVEN, part(pass_right, order)), [slim], [tg_even, w_b, a_gap], 2 * thin
    )
    p_pair = sent(p_even, pairs_right)
    x_odd = local_call(
        on_parity(ODD, part(top_odd, order)),
        [slim], [g_v_odd, tg_odd, v_odd, w_b, w_vg_pair, tg_gap, p_pair, q_gap], 7 * thin,
    )
    x_pair = sent(x_odd, pairs_left)
    return local_call(
        part(finish, order),
        [jax.ShapeDtypeStruct((2, order, rhs), BF16)],
        [vg_b, w_b, x_even, x_odd, x_pair, x_gap], 2 * thin,
    )


def solution(mesh):
    split = P(AXES, None, None)
    return jax.shard_map(
        body, mesh=mesh, in_specs=(split,) * 4, out_specs=split, check_vma=False
    )
```

```python
import functools

import jax
import jax.numpy as jnp
from jax import lax
from jax.experimental import pallas as pl
from jax.experimental.pallas import tpu as pltpu
from jax.sharding import PartitionSpec as P


AXES = ("grp", "dev")
BF16 = jnp.bfloat16
F32 = jnp.float32
VMEM_BYTES = 16 * 1024 * 1024


def is_odd():
    return lax.rem(lax.axis_index(AXES), 2) == 1


def if_left(value):
    return jnp.where(lax.axis_index(AXES) > 0, value, jnp.zeros_like(value))


def if_right(value):
    last = lax.axis_size(AXES) - 1
    return jnp.where(lax.axis_index(AXES) < last, value, jnp.zeros_like(value))


def dot(a, b):
    return jnp.dot(a, b, preferred_element_type=F32)


def by_parity(even, odd):
    odd_here = is_odd()
    if odd is not None:
        pl.when(odd_here)(odd)
    if even is not None:
        pl.when(jnp.logical_not(odd_here))(even)


def identity(order):
    rows = lax.broadcasted_iota(jnp.int32, (order, order), 0)
    return (rows == lax.broadcasted_iota(jnp.int32, (order, order), 1)).astype(F32)


def local_call(kernel, outs, ins, flops, in_hbm=0, scratch=(), aliases=None):
    vmem = pl.BlockSpec(memory_space=pltpu.VMEM)
    hbm = pl.BlockSpec(memory_space=pl.ANY)
    many = len(outs) > 1
    ins = [pltpu.with_memory_space_constraint(x, pltpu.HBM) for x in ins[:in_hbm]] + ins[in_hbm:]
    return pl.pallas_call(
        kernel,
        out_shape=outs if many else outs[0],
        in_specs=[hbm] * in_hbm + [vmem] * (len(ins) - in_hbm),
        out_specs=[vmem] * len(outs) if many else vmem,
        scratch_shapes=list(scratch),
        input_output_aliases=aliases or {},
        compiler_params=pltpu.CompilerParams(vmem_limit_bytes=VMEM_BYTES),
        cost_estimate=pl.CostEstimate(flops=flops // 1000, bytes_accessed=0, transcendentals=0),
    )(*ins)


def bf16_array(rows, columns):
    return jax.ShapeDtypeStruct((rows, columns), BF16)


def f32_array(rows, columns):
    return jax.ShapeDtypeStruct((rows, columns), F32)


def fetch(source, target, sem):
    copy = pltpu.make_async_copy(source, target, sem)
    copy.start()
    return copy


def load_row(order, diag, upper, right, vg, diag_b, upper_b, right_b, sems):
    d_b = fetch(diag.at[1], diag_b, sems.at[0])
    u_b = fetch(upper.at[1], upper_b, sems.at[1])
    r_b = fetch(right.at[1], right_b, sems.at[2])
    d_b.wait()
    u_b.wait()
    vg[:, :order] = dot(diag_b[...], upper_b[...]).astype(BF16)
    r_b.wait()
    vg[:, order:] = dot(diag_b[...], right_b[...]).astype(BF16)


def second_row_odd(order, *refs):
    by_parity(None, lambda: load_row(order, *refs))


def second_row(order, diag, upper, right, vg_odd, vg_b, *rest):
    *pieces, diag_b, upper_b, right_b, sems = rest

    def odd():
        vg_b[...] = vg_odd[...]

    def even():
        load_row(order, diag, upper, right, vg_b, diag_b, upper_b, right_b, sems)
        first = 0
        for piece in pieces:
            piece[...] = vg_b[:, first : first + piece.shape[1]]
            first += piece.shape[1]

    by_parity(even, odd)


def own_products(
    order, diag, lower, upper, right, vg_b, w_a, w_b, m, n, r,
    diag_a, lower_a, upper_a, right_a, diag_b, lower_b, sems,
):
    d_a = fetch(diag.at[0], diag_a, sems.at[0])
    u_a = fetch(upper.at[0], upper_a, sems.at[1])
    d_b = fetch(diag.at[1], diag_b, sems.at[2])
    l_b = fetch(lower.at[1], lower_b, sems.at[3])
    l_a = fetch(lower.at[0], lower_a, sems.at[4])
    r_a = fetch(right.at[0], right_a, sems.at[5])
    d_a.wait()
    u_a.wait()
    v_a = dot(diag_a[...], upper_a[...]).astype(BF16)
    d_b.wait()
    l_b.wait()
    w_b[...] = dot(diag_b[...], lower_b[...]).astype(BF16)
    l_a.wait()
    w_a[...] = dot(diag_a[...], lower_a[...]).astype(BF16)
    r_a.wait()
    g_a = dot(diag_a[...], right_a[...]).astype(BF16)
    n[...] = dot(v_a, vg_b[:, :order]).astype(BF16)
    r[...] = g_a.astype(F32) - dot(v_a, vg_b[:, order:])
    m[...] = dot(v_a, w_b[...])


def scale_one(order, w_a, m, r, v_left, g_left, scale, tg):
    first = 0
    eye = identity(order)
    for piece in v_left:
        at = slice(first, first + piece.shape[1])
        coupling = if_left(dot(w_a[...], piece[...])) + m[:, at]
        scale[:, at] = (eye[:, at] + coupling).astype(BF16)
        first = at.stop
    rest = (r[...] - if_left(dot(w_a[...], g_left[...]))).astype(BF16)
    tg[:, :order] = dot(scale[...], w_a[...]).astype(BF16)
    tg[:, order:] = dot(scale[...], rest).astype(BF16)


def spikes_one(scale, n, w_b, g_one, v_one, w_v, w_g):
    v_one[...] = (-dot(scale[...], n[...])).astype(BF16)
    columns = v_one.shape[1] // len(w_v)
    for i, piece in enumerate(w_v):
        piece[...] = dot(w_b[...], v_one[:, i * columns : (i + 1) * columns]).astype(BF16)
    w_g[...] = dot(w_b[...], g_one[...]).astype(BF16)


def level_one_odd(order, w_a, m, r, v0, vg1, n, w_b, tg, v_one, w_vg, scale):
    columns = order - v0.shape[1]

    def odd():
        v_left, g_left = [v0, vg1.at[:, :columns]], vg1.at[:, columns:]
        scale_one(order, w_a, m, r, v_left, g_left, scale, tg)
        spikes_one(
            scale, n, w_b, tg.at[:, order:], v_one, [w_vg.at[:, :order]], w_vg.at[:, order:]
        )

    by_parity(None, odd)


def scale_one_even(order, w_a, m, r, vg, tg_odd, tg, scale):
    v_left, g_left = [vg.at[:, :order]], vg.at[:, order:]
    by_parity(lambda: scale_one(order, w_a, m, r, v_left, g_left, scale, tg), None)


def spikes_one_even(order, scale, n, w_b, tg, v_odd, v_one, to_pair0, to_pair1, to_pair2):
    def odd():
        to_pair0[...] = tg[:, : order // 2]
        to_pair1[...] = tg[:, order // 2 : order]
        to_pair2[...] = tg[:, order:]

    by_parity(
        lambda: spikes_one(
            scale, n, w_b, tg.at[:, order:], v_one, [to_pair0, to_pair1], to_pair2
        ),
        odd,
    )


def same(value):
    return value


def left_part(order, tg, w_v_left, w_g_left, left_on, left, h):
    t = tg[:, :order]
    columns = left.shape[1] // len(w_v_left)
    for i, piece in enumerate(w_v_left):
        left[:, i * columns : (i + 1) * columns] = left_on(dot(t, piece[...])).astype(BF16)
    h[...] = tg[:, order:].astype(F32) + left_on(dot(t, w_g_left[...]))


def left_part_all(order, tg, w_vg_gap, pair0, pair1, pair2, left, h):
    by_parity(
        lambda: left_part(
            order, tg, [w_vg_gap.at[:, :order]], w_vg_gap.at[:, order:], if_left, left, h
        ),
        lambda: left_part(order, tg, [pair0, pair1], pair2, same, left, h),
    )


def times(pieces, block):
    depth = block.shape[0] // len(pieces)
    return sum(dot(piece[...], block[i * depth : (i + 1) * depth]) for i, piece in enumerate(pieces))


def level_two(v_one, w_b, left, h_left, t_right, g_right, right_on, g, w_g):
    h = h_left[...] - right_on(dot(v_one[...], g_right[...]))
    h16 = h.astype(BF16)
    own = dot(w_b[...], h16).astype(BF16)
    from_right = right_on(dot(v_one[...], times(t_right, own).astype(BF16)))
    g[...] = (h - dot(left[...], h16) - from_right).astype(BF16)
    w_g[...] = dot(w_b[...], g[...]).astype(BF16)


def level_two_all(order, v_one, w_b, left, h_left, tg_gap, pair0, pair1, pair2, y_pair, y_gap):
    own = v_one, w_b, left, h_left
    t_gap, g_gap = [tg_gap.at[:, :order]], tg_gap.at[:, order:]
    by_parity(
        lambda: level_two(*own, [pair0, pair1], pair2, same, y_gap, y_pair),
        lambda: level_two(*own, t_gap, g_gap, if_right, y_pair, y_gap),
    )


def spikes_two(order, tg, v_one, w_b, left, t_right, right_on, s_t, s_v, scale):
    right = times(t_right, w_b[...]).astype(BF16)
    coupling = left[...].astype(F32) + right_on(dot(v_one[...], right))
    scale[...] = (identity(order) - coupling).astype(BF16)
    s_t[...] = if_left(dot(scale[...], tg[:, :order])).astype(BF16)
    s_v[...] = if_right(dot(scale[...], v_one[...])).astype(BF16)


def spikes_two_all(
    order, tg, v_one, w_b, left, tg_gap, pair0, pair1, after, s_t, s_v, scale
):
    own = order, tg, v_one, w_b, left
    by_parity(
        lambda: spikes_two(*own, [pair0, pair1], same, s_t, s_v, scale),
        lambda: spikes_two(*own, [tg_gap.at[:, :order]], if_right, s_t, s_v, scale),
    )


def passed_right(tg, w_b, from_left, out):
    own = if_left(-dot(tg[:, : tg.shape[0]], from_left[...])).astype(BF16)
    out[...] = dot(w_b[...], own).astype(BF16)


def passed_left(v_one, from_right, out):
    out[...] = if_right(dot(v_one[...], from_right[...])).astype(BF16)


def pass_on_pair(tg, v_one, w_b, got, out):
    by_parity(
        lambda: passed_left(v_one, got, out), lambda: passed_right(tg, w_b, got, out)
    )


def pass_on_gap(tg, v_one, w_b, from_left, from_right, after, out):
    by_parity(
        lambda: passed_right(tg, w_b, from_left, out), lambda: passed_left(v_one, from_right, out)
    )


def top_values(y_pair, y_gap, s_t, s_v, from_pair, from_left, from_right, x):
    def top(g, p, q):
        x[...] = (g[...].astype(F32) + dot(s_v[...], q[...]) - dot(s_t[...], p[...])).astype(BF16)

    by_parity(lambda: top(y_gap, from_left, from_pair), lambda: top(y_pair, from_pair, from_right))


def start_second(order, vg_b, w_b, x, rest):
    rest[...] = vg_b[:, order:].astype(F32) - dot(w_b[...], x[...])


def finish(order, vg_b, x, rest, x_pair, x_gap, out):
    def rows(x_next):
        out[0] = x[...]
        out[1] = (rest[...] - if_right(dot(vg_b[:, :order], x_next[...]))).astype(BF16)

    by_parity(lambda: rows(x_pair), lambda: rows(x_gap))


def exchanges(slab, count):
    pairs = [(i, i ^ 1) for i in range(count)]
    after = [(i + 1) % count for i in range(count)]
    after[2], after[slab + 2], after[count - 1] = 0, 3, count - 5
    for first in range(slab + 3, count - 5, 4):
        after[first + 3] = first
    to_right = list(enumerate(after))
    to_left = [(count - 1 - i, count - 1 - j) for i, j in to_right]
    return pairs, to_right, to_left


def body(diag, lower, upper, right):
    order, rhs = diag.shape[1], right.shape[2]
    count = lax.axis_size(AXES)
    pairs, to_right, to_left = exchanges(lax.axis_size("dev"), count)

    def sent(block, route):
        return lax.ppermute(block, AXES, route)

    part = functools.partial
    square = 2 * order**3
    thin = 2 * order * order * rhs
    block = pltpu.VMEM((order, order), BF16)
    side = pltpu.VMEM((order, rhs), BF16)
    wide = bf16_array(order, order + rhs)
    full = bf16_array(order, order)
    slim = bf16_array(order, rhs)

    row_scratch = (block, block, side, pltpu.SemaphoreType.DMA((3,)))
    vg_odd = local_call(
        part(second_row_odd, order), [wide], [diag, upper, right], square + thin, 3, row_scratch
    )
    vg_gap = sent(vg_odd, to_right)
    cut = 3 * order // 4
    vg_b, *to_pair = local_call(
        part(second_row, order),
        [wide, bf16_array(order, cut), bf16_array(order, order - cut + rhs)],
        [diag, upper, right, vg_odd], square + thin, 3, row_scratch,
    )
    vg_pair = [sent(piece, pairs) for piece in to_pair]
    w_a, w_b, m, n, r = local_call(
        part(own_products, order),
        [full, full, f32_array(order, order), full, f32_array(order, rhs)],
        [diag, lower, upper, right, vg_b], 5 * square + 2 * thin, 4,
        (block, block, block, side, block, block, pltpu.SemaphoreType.DMA((6,))),
    )

    tg_odd, v_odd, w_vg_odd = local_call(
        part(level_one_odd, order),
        [wide, full, wide], [w_a, m, r, *vg_pair, n, w_b], 4 * square + 3 * thin, 0, (block,),
    )
    w_vg_gap = sent(w_vg_odd, to_right)
    tg, scale = local_call(
        part(scale_one_even, order),
        [wide, full], [w_a, m, r, vg_gap, tg_odd], 2 * square + 2 * thin, aliases={4: 0},
    )
    tg_gap = sent(tg, to_left)
    half = bf16_array(order, order // 2)
    v_one, *to_pair = local_call(
        part(spikes_one_even, order),
        [full, half, half, slim], [scale, n, w_b, tg, v_odd], 2 * square + thin, aliases={4: 0},
    )
    pair = [sent(piece, pairs) for piece in to_pair]

    left, h_left = local_call(
        part(left_part_all, order),
        [full, f32_array(order, rhs)], [tg, w_vg_gap, *pair], square + thin,
    )
    y_pair, y_gap = local_call(
        part(level_two_all, order),
        [slim, slim], [v_one, w_b, left, h_left, tg_gap, *pair], 6 * thin,
    )
    got_pair = sent(y_pair, pairs)
    got_gap = [sent(y_gap, to_right), sent(y_gap, to_left)]
    on_gap = local_call(
        pass_on_pair, [slim], [tg, v_one, w_b, got_pair], 2 * thin
    )
    from_gap = [sent(on_gap, to_right), sent(on_gap, to_left)]
    s_t, s_v = local_call(
        part(spikes_two_all, order),
        [full, full], [tg, v_one, w_b, left, tg_gap, *pair[:2], on_gap], 4 * square, 0, (block,),
    )
    on_pair = local_call(
        pass_on_gap, [slim], [tg, v_one, w_b, *got_gap, s_t], 2 * thin
    )
    from_pair = sent(on_pair, pairs)
    x = local_call(
        top_values, [slim], [y_pair, y_gap, s_t, s_v, from_pair, *from_gap], 2 * thin
    )
    x_pair, x_gap = sent(x, pairs), sent(x, to_left)
    rest = local_call(part(start_second, order), [f32_array(order, rhs)], [vg_b, w_b, x], thin)
    return local_call(
        part(finish, order),
        [jax.ShapeDtypeStruct((2, order, rhs), BF16)], [vg_b, x, rest, x_pair, x_gap], thin,
    )


def solution(mesh):
    split = P(AXES, None, None)
    return jax.shard_map(
        body, mesh=mesh, in_specs=(split,) * 4, out_specs=split, check_vma=False
    )
```

```python
import functools

import jax
import jax.numpy as jnp
from jax import lax
from jax.experimental import pallas as pl
from jax.experimental.pallas import tpu as pltpu
from jax.sharding import PartitionSpec as P


AXES = ("grp", "dev")
BF16 = jnp.bfloat16
F32 = jnp.float32
VMEM_BYTES = 12 * 1024 * 1024


def is_odd():
    return lax.rem(lax.axis_index(AXES), 2) == 1


def if_left(value):
    return jnp.where(lax.axis_index(AXES) > 0, value, jnp.zeros_like(value))


def if_right(value):
    last = lax.axis_size(AXES) - 1
    return jnp.where(lax.axis_index(AXES) < last, value, jnp.zeros_like(value))


def dot(a, b):
    return jnp.dot(a, b, preferred_element_type=F32)


def by_parity(even, odd):
    odd_here = is_odd()
    if odd is not None:
        pl.when(odd_here)(odd)
    if even is not None:
        pl.when(jnp.logical_not(odd_here))(even)


def identity(order):
    rows = lax.broadcasted_iota(jnp.int32, (order, order), 0)
    return (rows == lax.broadcasted_iota(jnp.int32, (order, order), 1)).astype(F32)


def local_call(kernel, outs, ins, flops, in_hbm=0, scratch=(), aliases=None, weight=0.001):
    vmem = pl.BlockSpec(memory_space=pltpu.VMEM)
    hbm = pl.BlockSpec(memory_space=pl.ANY)
    many = len(outs) > 1
    ins = [pltpu.with_memory_space_constraint(x, pltpu.HBM) for x in ins[:in_hbm]] + ins[in_hbm:]
    return pl.pallas_call(
        kernel,
        out_shape=outs if many else outs[0],
        in_specs=[hbm] * in_hbm + [vmem] * (len(ins) - in_hbm),
        out_specs=[vmem] * len(outs) if many else vmem,
        scratch_shapes=list(scratch),
        input_output_aliases=aliases or {},
        compiler_params=pltpu.CompilerParams(vmem_limit_bytes=VMEM_BYTES),
        cost_estimate=pl.CostEstimate(flops=int(flops * weight), bytes_accessed=0, transcendentals=0),
    )(*ins)


def bf16_array(rows, columns):
    return jax.ShapeDtypeStruct((rows, columns), BF16)


def f32_array(rows, columns):
    return jax.ShapeDtypeStruct((rows, columns), F32)


def fetch(source, target, sem):
    copy = pltpu.make_async_copy(source, target, sem)
    copy.start()
    return copy


def load_row(order, diag, upper, right, vg, diag_b, upper_b, right_b, sems):
    d_b = fetch(diag.at[1], diag_b, sems.at[0])
    u_b = fetch(upper.at[1], upper_b, sems.at[1])
    r_b = fetch(right.at[1], right_b, sems.at[2])
    d_b.wait()
    u_b.wait()
    vg[:, :order] = dot(diag_b[...], upper_b[...]).astype(BF16)
    r_b.wait()
    vg[:, order:] = dot(diag_b[...], right_b[...]).astype(BF16)


def second_row_odd(order, *refs):
    by_parity(None, lambda: load_row(order, *refs))


def second_row(order, diag, upper, right, vg_odd, vg_b, *rest):
    *pieces, diag_b, upper_b, right_b, sems = rest

    def odd():
        vg_b[...] = vg_odd[...]

    def even():
        load_row(order, diag, upper, right, vg_b, diag_b, upper_b, right_b, sems)
        first = 0
        for piece in pieces:
            piece[...] = vg_b[:, first : first + piece.shape[1]]
            first += piece.shape[1]

    by_parity(even, odd)


def own_products(
    order, diag, lower, upper, right, vg_b, w_a, w_b, m, n, r,
    diag_a, lower_a, upper_a, right_a, diag_b, lower_b, sems,
):
    d_a = fetch(diag.at[0], diag_a, sems.at[0])
    u_a = fetch(upper.at[0], upper_a, sems.at[1])
    d_b = fetch(diag.at[1], diag_b, sems.at[2])
    l_b = fetch(lower.at[1], lower_b, sems.at[3])
    l_a = fetch(lower.at[0], lower_a, sems.at[4])
    r_a = fetch(right.at[0], right_a, sems.at[5])
    d_a.wait()
    u_a.wait()
    v_a = dot(diag_a[...], upper_a[...]).astype(BF16)
    d_b.wait()
    l_b.wait()
    w_b[...] = dot(diag_b[...], lower_b[...]).astype(BF16)
    l_a.wait()
    w_a[...] = dot(diag_a[...], lower_a[...]).astype(BF16)
    r_a.wait()
    g_a = dot(diag_a[...], right_a[...]).astype(BF16)
    n[...] = dot(v_a, vg_b[:, :order]).astype(BF16)
    r[...] = g_a.astype(F32) - dot(v_a, vg_b[:, order:])
    m[...] = dot(v_a, w_b[...])


def scale_one(order, w_a, m, r, v_left, g_left, scale, tg):
    first = 0
    eye = identity(order)
    for piece in v_left:
        at = slice(first, first + piece.shape[1])
        coupling = if_left(dot(w_a[...], piece[...])) + m[:, at]
        scale[:, at] = (eye[:, at] + coupling).astype(BF16)
        first = at.stop
    rest = (r[...] - if_left(dot(w_a[...], g_left[...]))).astype(BF16)
    tg[:, :order] = dot(scale[...], w_a[...]).astype(BF16)
    tg[:, order:] = dot(scale[...], rest).astype(BF16)


def spikes_one(order, scale, n, w_b, tg, v_one, w_t, w_v, w_g):
    v_one[...] = (-dot(scale[...], n[...])).astype(BF16)
    w_v[...] = dot(w_b[...], v_one[...]).astype(BF16)
    w_g[...] = dot(w_b[...], tg[:, order:]).astype(BF16)
    w_t[...] = dot(w_b[...], tg[:, :order]).astype(BF16)


def pack(side):
    columns = side.shape[1]
    return jnp.concatenate(
        [side[i : i + columns] for i in range(0, side.shape[0], columns)], axis=1
    )


def unpack(rows, columns):
    return jnp.concatenate(
        [rows[:, i : i + columns] for i in range(0, rows.shape[1], columns)], axis=0
    )


def hand_to_pair(order, blocks, side, to_pair):
    rows, first = pack(side), 0
    for block, piece in zip(blocks, to_pair):
        last = first + piece.shape[0] - order
        piece[:order, :] = block
        piece[order:, :] = rows[first:last]
        first = last


def side_of_pair(order, got, columns):
    return unpack(jnp.concatenate([piece[order:, :] for piece in got], axis=0), columns)


def level_one_odd(order, w_a, m, r, v0, vg1, n, w_b, tg, v_one, w_vg, *rest):
    *to_pair, scale, w_t = rest
    columns = order - v0.shape[1]

    def odd():
        v_left, g_left = [v0, vg1.at[:, :columns]], vg1.at[:, columns:]
        scale_one(order, w_a, m, r, v_left, g_left, scale, tg)
        w_v, w_g = w_vg.at[:, :order], w_vg.at[:, order:]
        spikes_one(order, scale, n, w_b, tg, v_one, w_t, w_v, w_g)
        hand_to_pair(order, [tg[:, :order], w_t[...], v_one[...]], tg[:, order:], to_pair)

    by_parity(None, odd)


def scale_one_even(order, w_a, m, r, vg, tg_odd, tg, scale):
    v_left, g_left = [vg.at[:, :order]], vg.at[:, order:]
    by_parity(lambda: scale_one(order, w_a, m, r, v_left, g_left, scale, tg), None)


def spikes_one_even(order, scale, n, w_b, tg, v_odd, pair0, pair1, pair2, v_one, *rest):
    *to_pair, w_t, w_v, w_g = rest

    def even():
        spikes_one(order, scale, n, w_b, tg, v_one, w_t, w_v, w_g)
        hand_to_pair(order, [w_v[...], w_t[...], v_one[...]], w_g[...], to_pair)

    by_parity(even, None)


def pair_part(
    order, tg, v_one, w_b, to_pair1, w_vg, pair0, pair1, pair2,
    near, far, w_far, p_far, p_v, n_h, w_h, w_n_h, p_n_h,
):
    got, w_t, w_t_pair, v_pair = (x[:order, :] for x in (pair0, to_pair1, pair1, pair2))
    got_g = side_of_pair(order, [pair0, pair1, pair2], n_h.shape[1])
    t, eye = tg[:, :order], identity(order)

    def even():
        right = dot(got, w_b[...]).astype(BF16)
        near[...] = (eye - dot(v_one[...], right)).astype(BF16)
        far[...] = dot(w_b[...], near[...]).astype(BF16)
        p_far[...] = dot(w_t_pair, far[...]).astype(BF16)
        p_v[...] = dot(w_t_pair, w_t).astype(BF16)
        n_h[...] = tg[:, order:].astype(F32) - dot(v_one[...], got_g)

    def odd():
        near[...] = (eye - dot(t, got)).astype(BF16)
        far[...] = dot(near[...], v_one[...]).astype(BF16)
        w_far[...] = dot(w_b[...], far[...]).astype(BF16)
        p_far[...] = dot(v_pair, far[...]).astype(BF16)
        p_v[...] = dot(v_pair, v_one[...]).astype(BF16)
        own = (tg[:, order:].astype(F32) + dot(t, got_g)).astype(BF16)
        scaled = dot(near[...], own)
        n_h[...] = scaled
        w_h[...] = dot(w_b[...], own)
        w_n_h[...] = dot(w_b[...], scaled.astype(BF16))
        p_n_h[...] = dot(v_pair, scaled.astype(BF16))

    by_parity(even, odd)


def level_two(
    order, tg, v_one, w_vg, near, far, w_far, p_far, p_v, n_h, w_h, w_n_h, p_n_h, w_vg_gap, tg_gap,
    g, a0, a1, b,
):
    rows = order // 2
    left_of_two = lax.rem(lax.axis_index(AXES), 4) < 2

    def hand_out(right, left):
        first, second = jnp.where(left_of_two, right, left), jnp.where(left_of_two, left, right)
        a0[...] = first[:rows]
        a1[...] = first[rows:]
        b[...] = second

    def even():
        t = tg[:, :order]
        whole = (n_h[...] + if_left(dot(t, w_vg_gap[:, order:]))).astype(BF16)
        from_left = if_left(dot(w_vg_gap[:, :order], whole)).astype(BF16)
        value = (dot(near[...], whole) - dot(t, from_left)).astype(BF16)
        onward = (dot(p_v[...], from_left) - dot(p_far[...], whole)).astype(BF16)
        g[...] = value
        hand_out(onward, value)

    def odd():
        g_right, w_v = tg_gap[:, order:], w_vg[:, :order]
        own = w_h[...] - if_right(dot(w_v, g_right))
        from_right = if_right(dot(tg_gap[:, :order], own.astype(BF16))).astype(BF16)

        def whole(start, gap, further):
            return (start[...] - if_right(dot(gap[...], g_right)) - dot(further, from_right)).astype(BF16)

        g[...] = whole(n_h, far, v_one[...])
        hand_out(whole(w_n_h, w_far, w_v), whole(p_n_h, p_far, p_v[...]))

    by_parity(even, odd)


def spikes_two(
    order, tg, v_one, w_b, pair1, pair2, near, w_vg_gap, tg_gap, after, from_left, from_right, scale
):
    t = tg[:, :order]
    index, count = lax.axis_index(AXES), lax.axis_size(AXES)

    def put(left, right):
        from_left[...] = jnp.where(index > 1, left, jnp.zeros_like(left)).astype(BF16)
        from_right[...] = jnp.where(index < count - 2, right, jnp.zeros_like(right)).astype(BF16)

    def even():
        gap = if_left(dot(t, w_vg_gap[:, :order]))
        scale[...] = (near[...].astype(F32) - gap).astype(BF16)
        s_v = dot(scale[...], v_one[...]).astype(BF16)
        put(-dot(scale[...], t), dot(s_v, pair2[:order, :]))

    def odd():
        right = dot(tg_gap[:, :order], w_b[...]).astype(BF16)
        gap = if_right(dot(v_one[...], right))
        scale[...] = (near[...].astype(F32) - gap).astype(BF16)
        s_t = dot(scale[...], t).astype(BF16)
        put(dot(s_t, pair1[:order, :]), dot(scale[...], v_one[...]))

    by_parity(even, odd)


def top_values(g, from_left, from_right, a0, a1, b, x, *halves):
    def top(left, right):
        change = dot(from_left[...], left) + dot(from_right[...], right)
        x[...] = (g[...].astype(F32) + change).astype(BF16)

    first = jnp.concatenate([a0[...], a1[...]], axis=0)
    left_of_two = lax.rem(lax.axis_index(AXES), 4) < 2
    pl.when(left_of_two)(lambda: top(b[...], first))
    pl.when(jnp.logical_not(left_of_two))(lambda: top(first, b[...]))
    rows = halves[0].shape[0]
    for i, half in enumerate(halves):
        half[...] = x[i * rows : (i + 1) * rows, :]


def second_values(order, vg_b, w_b, x, x_pair0, x_pair1, rest):
    rest[...] = vg_b[:, order:].astype(F32) - dot(w_b[...], x[...])

    def even():
        x_next = jnp.concatenate([x_pair0[...], x_pair1[...]], axis=0)
        rest[...] -= dot(vg_b[:, :order], x_next)

    by_parity(even, None)


def finish(order, vg_b, x, rest, x_gap, out):
    out[0] = x[...]

    def even():
        out[1] = rest[...].astype(BF16)

    def odd():
        out[1] = (rest[...] - if_right(dot(vg_b[:, :order], x_gap[...]))).astype(BF16)

    by_parity(even, odd)


def exchanges(slab, count):
    pairs = [(i, i ^ 1) for i in range(count)]
    twos = [(i, i ^ 2) for i in range(count)]
    inner = range(2, count - 2)
    other_twos = [(i, ((i - 2) ^ 2) + 2 if i in inner else i ^ 1) for i in range(count)]
    after = [(i + 1) % count for i in range(count)]
    after[2], after[slab + 2], after[count - 1] = 0, 3, count - 5
    for first in range(slab + 3, count - 5, 4):
        after[first + 3] = first
    to_right = list(enumerate(after))
    to_left = [(count - 1 - i, count - 1 - j) for i, j in to_right]
    return pairs, twos, other_twos, to_right, to_left


def body(diag, lower, upper, right):
    order, rhs = diag.shape[1], right.shape[2]
    count = lax.axis_size(AXES)
    pairs, twos, other_twos, to_right, to_left = exchanges(lax.axis_size("dev"), count)

    def sent(block, route):
        return lax.ppermute(block, AXES, route)

    part = functools.partial
    square = 2 * order**3
    thin = 2 * order * order * rhs
    block = pltpu.VMEM((order, order), BF16)
    side = pltpu.VMEM((order, rhs), BF16)
    wide = bf16_array(order, order + rhs)
    full = bf16_array(order, order)
    slim = bf16_array(order, rhs)

    row_scratch = (block, block, side, pltpu.SemaphoreType.DMA((3,)))
    vg_odd = local_call(
        part(second_row_odd, order), [wide], [diag, upper, right], square + thin, 3, row_scratch
    )
    vg_gap = sent(vg_odd, to_right)
    cut = 3 * order // 4
    vg_b, *to_pair = local_call(
        part(second_row, order),
        [wide, bf16_array(order, cut), bf16_array(order, order - cut + rhs)],
        [diag, upper, right, vg_odd], square + thin, 3, row_scratch,
    )
    vg_pair = [sent(piece, pairs) for piece in to_pair]
    w_a, w_b, m, n, r = local_call(
        part(own_products, order),
        [full, full, f32_array(order, order), full, f32_array(order, rhs)],
        [diag, lower, upper, right, vg_b], 5 * square + 2 * thin, 4,
        (block, block, block, side, block, block, pltpu.SemaphoreType.DMA((6,))),
    )

    extra = rhs // 16 * 6
    shares = [bf16_array(order + rows, order) for rows in (extra, extra, rhs - 2 * extra)]
    tg_odd, v_odd, w_vg_odd, *to_pair = local_call(
        part(level_one_odd, order),
        [wide, full, wide, *shares], [w_a, m, r, *vg_pair, n, w_b], 5 * square, 0, (block, block),
    )
    w_vg_gap = sent(w_vg_odd, to_right)
    tg, scale = local_call(
        part(scale_one_even, order),
        [wide, full], [w_a, m, r, vg_gap, tg_odd], 2 * square + 2 * thin, aliases={4: 0},
    )
    tg_gap = sent(tg, to_left)
    v_one, *to_pair = local_call(
        part(spikes_one_even, order),
        [full, *shares], [scale, n, w_b, tg, v_odd, *to_pair], 3 * square + thin,
        0, (block, block, side), {4: 0, 5: 1, 6: 2, 7: 3},
    )
    pair = [sent(piece, pairs) for piece in to_pair]

    tall, flat = f32_array(order, rhs), bf16_array(order // 2, rhs)
    known = local_call(
        part(pair_part, order),
        [full] * 5 + [tall] * 4,
        [tg, v_one, w_b, to_pair[1], w_vg_odd, *pair], 6 * square,
    )
    g_two, *to_two = local_call(
        part(level_two, order),
        [slim, flat, flat, slim], [tg, v_one, w_vg_odd, *known, w_vg_gap, tg_gap], 8 * thin,
    )
    by_two = [sent(to_two[0], twos), sent(to_two[1], twos), sent(to_two[2], other_twos)]
    from_left, from_right = local_call(
        part(spikes_two, order),
        [full, full],
        [tg, v_one, w_b, *pair[1:], known[0], w_vg_gap, tg_gap, g_two], 5 * square,
        0, (block,),
    )
    x, *x_own = local_call(
        top_values, [slim, flat, flat], [g_two, from_left, from_right, *by_two], 2 * thin
    )
    x_gap = sent(x, to_left)
    x_pair = [sent(piece, pairs) for piece in x_own]
    rest = local_call(part(second_values, order), [tall], [vg_b, w_b, x, *x_pair], 2 * thin, weight=1)
    return local_call(
        part(finish, order),
        [jax.ShapeDtypeStruct((2, order, rhs), BF16)], [vg_b, x, rest, x_gap], thin,
    )


def solution(mesh):
    split = P(AXES, None, None)
    return jax.shard_map(
        body, mesh=mesh, in_specs=(split,) * 4, out_specs=split, check_vma=False
    )
```

```python
import functools

import jax
import jax.numpy as jnp
from jax import lax
from jax.experimental import pallas as pl
from jax.experimental.pallas import tpu as pltpu
from jax.sharding import PartitionSpec as P


AXES = ("grp", "dev")
BF16 = jnp.bfloat16
F32 = jnp.float32
VMEM_BYTES = 12 * 1024 * 1024


def is_odd():
    return lax.rem(lax.axis_index(AXES), 2) == 1


def if_left(value):
    return jnp.where(lax.axis_index(AXES) > 0, value, jnp.zeros_like(value))


def if_right(value):
    last = lax.axis_size(AXES) - 1
    return jnp.where(lax.axis_index(AXES) < last, value, jnp.zeros_like(value))


def dot(a, b):
    return jnp.dot(a, b, preferred_element_type=F32)


def by_parity(even, odd):
    odd_here = is_odd()
    if odd is not None:
        pl.when(odd_here)(odd)
    if even is not None:
        pl.when(jnp.logical_not(odd_here))(even)


def identity(order):
    rows = lax.broadcasted_iota(jnp.int32, (order, order), 0)
    return (rows == lax.broadcasted_iota(jnp.int32, (order, order), 1)).astype(F32)


def local_call(kernel, outs, ins, flops, in_hbm=0, scratch=(), aliases=None, weight=0.001):
    vmem = pl.BlockSpec(memory_space=pltpu.VMEM)
    hbm = pl.BlockSpec(memory_space=pl.ANY)
    many = len(outs) > 1
    ins = [pltpu.with_memory_space_constraint(x, pltpu.HBM) for x in ins[:in_hbm]] + ins[in_hbm:]
    return pl.pallas_call(
        kernel,
        out_shape=outs if many else outs[0],
        in_specs=[hbm] * in_hbm + [vmem] * (len(ins) - in_hbm),
        out_specs=[vmem] * len(outs) if many else vmem,
        scratch_shapes=list(scratch),
        input_output_aliases=aliases or {},
        compiler_params=pltpu.CompilerParams(vmem_limit_bytes=VMEM_BYTES),
        cost_estimate=pl.CostEstimate(flops=int(flops * weight), bytes_accessed=0, transcendentals=0),
    )(*ins)


def bf16_array(rows, columns):
    return jax.ShapeDtypeStruct((rows, columns), BF16)


def f32_array(rows, columns):
    return jax.ShapeDtypeStruct((rows, columns), F32)


def fetch(source, target, sem):
    copy = pltpu.make_async_copy(source, target, sem)
    copy.start()
    return copy


def load_row(order, diag, upper, right, vg, diag_b, upper_b, right_b, sems):
    d_b = fetch(diag.at[1], diag_b, sems.at[0])
    u_b = fetch(upper.at[1], upper_b, sems.at[1])
    r_b = fetch(right.at[1], right_b, sems.at[2])
    d_b.wait()
    u_b.wait()
    vg[:, :order] = dot(diag_b[...], upper_b[...]).astype(BF16)
    r_b.wait()
    vg[:, order:] = dot(diag_b[...], right_b[...]).astype(BF16)


def second_row_odd(order, *refs):
    by_parity(None, lambda: load_row(order, *refs))


def second_row(order, diag, upper, right, vg_odd, vg_b, *rest):
    *pieces, diag_b, upper_b, right_b, sems = rest

    def odd():
        vg_b[...] = vg_odd[...]

    def even():
        load_row(order, diag, upper, right, vg_b, diag_b, upper_b, right_b, sems)
        first = 0
        for piece in pieces:
            piece[...] = vg_b[:, first : first + piece.shape[1]]
            first += piece.shape[1]

    by_parity(even, odd)


def own_products(
    order, diag, lower, upper, right, vg_b, w_a, w_b, m, n, r,
    diag_a, lower_a, upper_a, right_a, diag_b, lower_b, sems,
):
    d_a = fetch(diag.at[0], diag_a, sems.at[0])
    u_a = fetch(upper.at[0], upper_a, sems.at[1])
    d_b = fetch(diag.at[1], diag_b, sems.at[2])
    l_b = fetch(lower.at[1], lower_b, sems.at[3])
    l_a = fetch(lower.at[0], lower_a, sems.at[4])
    r_a = fetch(right.at[0], right_a, sems.at[5])
    d_a.wait()
    u_a.wait()
    v_a = dot(diag_a[...], upper_a[...]).astype(BF16)
    d_b.wait()
    l_b.wait()
    w_b[...] = dot(diag_b[...], lower_b[...]).astype(BF16)
    l_a.wait()
    w_a[...] = dot(diag_a[...], lower_a[...]).astype(BF16)
    r_a.wait()
    g_a = dot(diag_a[...], right_a[...]).astype(BF16)
    n[...] = dot(v_a, vg_b[:, :order]).astype(BF16)
    r[...] = g_a.astype(F32) - dot(v_a, vg_b[:, order:])
    m[...] = dot(v_a, w_b[...])


def scale_one(order, w_a, m, r, v_left, g_left, scale, tg):
    first = 0
    eye = identity(order)
    for piece in v_left:
        at = slice(first, first + piece.shape[1])
        coupling = if_left(dot(w_a[...], piece[...])) + m[:, at]
        scale[:, at] = (eye[:, at] + coupling).astype(BF16)
        first = at.stop
    rest = (r[...] - if_left(dot(w_a[...], g_left[...]))).astype(BF16)
    tg[:, :order] = dot(scale[...], w_a[...]).astype(BF16)
    tg[:, order:] = dot(scale[...], rest).astype(BF16)


def spikes_one(order, scale, n, w_b, tg, v_one, w_t, w_v, w_g):
    v_one[...] = (-dot(scale[...], n[...])).astype(BF16)
    w_v[...] = dot(w_b[...], v_one[...]).astype(BF16)
    w_g[...] = dot(w_b[...], tg[:, order:]).astype(BF16)
    w_t[...] = dot(w_b[...], tg[:, :order]).astype(BF16)


def pack(side):
    columns = side.shape[1]
    return jnp.concatenate(
        [side[i : i + columns] for i in range(0, side.shape[0], columns)], axis=1
    )


def unpack(rows, columns):
    return jnp.concatenate(
        [rows[:, i : i + columns] for i in range(0, rows.shape[1], columns)], axis=0
    )


def hand_to_pair(order, blocks, side, to_pair):
    rows, first = pack(side), 0
    for block, piece in zip(blocks, to_pair):
        last = first + piece.shape[0] - order
        piece[:order, :] = block
        piece[order:, :] = rows[first:last]
        first = last


def side_of_pair(order, got, columns):
    return unpack(jnp.concatenate([piece[order:, :] for piece in got], axis=0), columns)


def level_one_odd(order, w_a, m, r, v0, vg1, n, w_b, tg, v_one, w_vg, *rest):
    *to_pair, scale, w_t = rest
    columns = order - v0.shape[1]

    def odd():
        v_left, g_left = [v0, vg1.at[:, :columns]], vg1.at[:, columns:]
        scale_one(order, w_a, m, r, v_left, g_left, scale, tg)
        w_v, w_g = w_vg.at[:, :order], w_vg.at[:, order:]
        spikes_one(order, scale, n, w_b, tg, v_one, w_t, w_v, w_g)
        hand_to_pair(order, [tg[:, :order], w_t[...], v_one[...]], tg[:, order:], to_pair)

    by_parity(None, odd)


def scale_one_even(order, w_a, m, r, vg, tg_odd, tg, scale):
    v_left, g_left = [vg.at[:, :order]], vg.at[:, order:]
    by_parity(lambda: scale_one(order, w_a, m, r, v_left, g_left, scale, tg), None)


def spikes_one_even(order, scale, n, w_b, tg, v_odd, pair0, pair1, pair2, v_one, *rest):
    *to_pair, w_t, w_v, w_g = rest

    def even():
        spikes_one(order, scale, n, w_b, tg, v_one, w_t, w_v, w_g)
        hand_to_pair(order, [w_v[...], w_t[...], v_one[...]], w_g[...], to_pair)

    by_parity(even, None)


def pair_part(
    order, tg, v_one, w_b, to_pair1, w_vg, pair0, pair1, pair2,
    near, far, w_far, p_far, p_v, n_h, w_h, w_n_h, p_n_h,
):
    got, w_t, w_t_pair, v_pair = (x[:order, :] for x in (pair0, to_pair1, pair1, pair2))
    got_g = side_of_pair(order, [pair0, pair1, pair2], n_h.shape[1])
    t, eye = tg[:, :order], identity(order)

    def even():
        right = dot(got, w_b[...]).astype(BF16)
        near[...] = (eye - dot(v_one[...], right)).astype(BF16)
        far[...] = dot(w_b[...], near[...]).astype(BF16)
        p_far[...] = dot(w_t_pair, far[...]).astype(BF16)
        p_v[...] = dot(w_t_pair, w_t).astype(BF16)
        n_h[...] = tg[:, order:].astype(F32) - dot(v_one[...], got_g)

    def odd():
        near[...] = (eye - dot(t, got)).astype(BF16)
        far[...] = dot(near[...], v_one[...]).astype(BF16)
        w_far[...] = dot(w_b[...], far[...]).astype(BF16)
        p_far[...] = dot(v_pair, far[...]).astype(BF16)
        p_v[...] = dot(v_pair, v_one[...]).astype(BF16)
        own = (tg[:, order:].astype(F32) + dot(t, got_g)).astype(BF16)
        scaled = dot(near[...], own)
        n_h[...] = scaled
        w_h[...] = dot(w_b[...], own)
        w_n_h[...] = dot(w_b[...], scaled.astype(BF16))
        p_n_h[...] = dot(v_pair, scaled.astype(BF16))

    by_parity(even, odd)


def hand_out(right, left, a, b):
    left_of_two = lax.rem(lax.axis_index(AXES), 4) < 2
    a[...] = jnp.where(left_of_two, right, left)
    b[...] = jnp.where(left_of_two, left, right)


def level_two_even(order, tg, near, far, p_far, p_v, n_h, w_vg_gap, g, a, b):
    def even():
        t = tg[:, :order]
        whole = (n_h[...] + if_left(dot(t, w_vg_gap[:, order:]))).astype(BF16)
        from_left = if_left(dot(w_vg_gap[:, :order], whole)).astype(BF16)
        value = (dot(near[...], whole) - dot(t, from_left)).astype(BF16)
        onward = (dot(p_v[...], from_left) - dot(p_far[...], whole)).astype(BF16)
        g[...] = value
        hand_out(onward, value, a, b)

    by_parity(even, None)


def level_two_odd(
    order, v_one, w_vg, far, w_far, p_far, p_v, n_h, w_h, w_n_h, p_n_h, tg_gap, after, g, a, b
):
    def odd():
        g_right, w_v = tg_gap[:, order:], w_vg[:, :order]
        own = w_h[...] - if_right(dot(w_v, g_right))
        from_right = if_right(dot(tg_gap[:, :order], own.astype(BF16))).astype(BF16)

        def whole(start, gap, further):
            gap_part = if_right(dot(gap[...], g_right)) + dot(further, from_right)
            return (start[...] - gap_part).astype(BF16)

        g[...] = whole(n_h, far, v_one[...])
        hand_out(whole(w_n_h, w_far, w_v), whole(p_n_h, p_far, p_v[...]), a, b)

    by_parity(None, odd)


def if_two_left(value):
    return jnp.where(lax.axis_index(AXES) > 1, value, jnp.zeros_like(value))


def if_two_right(value):
    last = lax.axis_size(AXES) - 2
    return jnp.where(lax.axis_index(AXES) < last, value, jnp.zeros_like(value))


def spikes_two_even(order, tg, v_one, near, pair2, w_vg_gap, after, from_left, from_right, scale):
    def even():
        t = tg[:, :order]
        gap = if_left(dot(t, w_vg_gap[:, :order]))
        scale[...] = (near[...].astype(F32) - gap).astype(BF16)
        s_v = dot(scale[...], v_one[...]).astype(BF16)
        from_left[...] = if_two_left(-dot(scale[...], t)).astype(BF16)
        from_right[...] = if_two_right(dot(s_v, pair2[:order, :])).astype(BF16)

    by_parity(even, None)


def spikes_two_odd(order, tg, v_one, w_b, near, pair1, tg_gap, after, from_left, from_right, scale):
    def odd():
        right = dot(tg_gap[:, :order], w_b[...]).astype(BF16)
        gap = if_right(dot(v_one[...], right))
        scale[...] = (near[...].astype(F32) - gap).astype(BF16)
        s_t = dot(scale[...], tg[:, :order]).astype(BF16)
        from_left[...] = if_two_left(dot(s_t, pair1[:order, :])).astype(BF16)
        from_right[...] = if_two_right(dot(scale[...], v_one[...])).astype(BF16)

    by_parity(None, odd)


def top_value(g, from_left, from_right, a, b, x):
    def top(left, right):
        change = dot(from_left[...], left[...]) + dot(from_right[...], right[...])
        x[...] = (g[...].astype(F32) + change).astype(BF16)

    left_of_two = lax.rem(lax.axis_index(AXES), 4) < 2
    pl.when(left_of_two)(lambda: top(b, a))
    pl.when(jnp.logical_not(left_of_two))(lambda: top(a, b))


def top_even(g, from_left, from_right, a, b, after, x):
    by_parity(lambda: top_value(g, from_left, from_right, a, b, x), None)


def top_odd(g, from_left, from_right, a, b, x, *halves):
    def odd():
        top_value(g, from_left, from_right, a, b, x)
        rows = halves[0].shape[0]
        for i, half in enumerate(halves):
            half[...] = x[i * rows : (i + 1) * rows, :]

    by_parity(None, odd)


def second_values(order, vg_b, w_b, x_even, x_odd, x_pair0, x_pair1, rest):
    def even():
        x_next = jnp.concatenate([x_pair0[...], x_pair1[...]], axis=0)
        own = vg_b[:, order:].astype(F32) - dot(w_b[...], x_even[...])
        rest[...] = own - dot(vg_b[:, :order], x_next)

    def odd():
        rest[...] = vg_b[:, order:].astype(F32) - dot(w_b[...], x_odd[...])

    by_parity(even, odd)


def finish(order, vg_b, x_even, x_odd, rest, x_gap, out):
    def even():
        out[0] = x_even[...]
        out[1] = rest[...].astype(BF16)

    def odd():
        out[0] = x_odd[...]
        out[1] = (rest[...] - if_right(dot(vg_b[:, :order], x_gap[...]))).astype(BF16)

    by_parity(even, odd)


def exchanges(slab, count):
    pairs = [(i, i ^ 1) for i in range(count)]
    twos, other_twos = [], []
    for parity in (0, 1):
        over = [i ^ slab for i in range(count)]
        twos.append([(i, i ^ 2 if i % 2 == parity else over[i]) for i in range(count)])
        to = [((i - 2) ^ 2) + 2 if i % 2 == parity else over[i] for i in range(count)]
        for end in (parity, count - 2 + parity):
            to[end], to[end ^ 1], to[over[end ^ 1]] = end ^ 1, over[end ^ 1], end
        other_twos.append(list(enumerate(to)))
    after = [(i + 1) % count for i in range(count)]
    after[2], after[slab + 2], after[count - 1] = 0, 3, count - 5
    for first in range(slab + 3, count - 5, 4):
        after[first + 3] = first
    to_right = list(enumerate(after))
    to_left = [(count - 1 - i, count - 1 - j) for i, j in to_right]
    return pairs, twos, other_twos, to_right, to_left


def body(diag, lower, upper, right):
    order, rhs = diag.shape[1], right.shape[2]
    count = lax.axis_size(AXES)
    pairs, twos, other_twos, to_right, to_left = exchanges(lax.axis_size("dev"), count)

    def sent(block, route):
        return lax.ppermute(block, AXES, route)

    part = functools.partial
    square = 2 * order**3
    thin = 2 * order * order * rhs
    block = pltpu.VMEM((order, order), BF16)
    side = pltpu.VMEM((order, rhs), BF16)
    wide = bf16_array(order, order + rhs)
    full = bf16_array(order, order)
    slim = bf16_array(order, rhs)

    row_scratch = (block, block, side, pltpu.SemaphoreType.DMA((3,)))
    vg_odd = local_call(
        part(second_row_odd, order), [wide], [diag, upper, right], square + thin, 3, row_scratch
    )
    vg_gap = sent(vg_odd, to_right)
    cut = 3 * order // 4
    vg_b, *to_pair = local_call(
        part(second_row, order),
        [wide, bf16_array(order, cut), bf16_array(order, order - cut + rhs)],
        [diag, upper, right, vg_odd], square + thin, 3, row_scratch,
    )
    vg_pair = [sent(piece, pairs) for piece in to_pair]
    w_a, w_b, m, n, r = local_call(
        part(own_products, order),
        [full, full, f32_array(order, order), full, f32_array(order, rhs)],
        [diag, lower, upper, right, vg_b], 5 * square + 2 * thin, 4,
        (block, block, block, side, block, block, pltpu.SemaphoreType.DMA((6,))),
    )

    extra = rhs // 16 * 6
    shares = [bf16_array(order + rows, order) for rows in (extra, extra, rhs - 2 * extra)]
    tg_odd, v_odd, w_vg_odd, *to_pair = local_call(
        part(level_one_odd, order),
        [wide, full, wide, *shares], [w_a, m, r, *vg_pair, n, w_b], 5 * square, 0, (block, block),
    )
    w_vg_gap = sent(w_vg_odd, to_right)
    tg, scale = local_call(
        part(scale_one_even, order),
        [wide, full], [w_a, m, r, vg_gap, tg_odd], 2 * square + 2 * thin, aliases={4: 0},
    )
    tg_gap = sent(tg, to_left)
    v_one, *to_pair = local_call(
        part(spikes_one_even, order),
        [full, *shares], [scale, n, w_b, tg, v_odd, *to_pair], 3 * square + thin,
        0, (block, block, side), {4: 0, 5: 1, 6: 2, 7: 3},
    )
    pair = [sent(piece, pairs) for piece in to_pair]

    tall, flat = f32_array(order, rhs), bf16_array(order // 2, rhs)
    known = local_call(
        part(pair_part, order),
        [full] * 5 + [tall] * 4,
        [tg, v_one, w_b, to_pair[1], w_vg_odd, *pair], 6 * square,
    )
    near, far, w_far, p_far, p_v, n_h, w_h, w_n_h, p_n_h = known
    g_even, a_even, b_even = local_call(
        part(level_two_even, order),
        [slim] * 3, [tg, near, far, p_far, p_v, n_h, w_vg_gap], 6 * thin,
    )
    even_a, even_b = sent(a_even, twos[0]), sent(b_even, other_twos[0])
    left_even, right_even = local_call(
        part(spikes_two_even, order),
        [full, full], [tg, v_one, near, pair[2], w_vg_gap, a_even], 4 * square, 0, (block,),
    )
    g_odd, a_odd, b_odd = local_call(
        part(level_two_odd, order),
        [slim] * 3,
        [v_one, w_vg_odd, far, w_far, p_far, p_v, n_h, w_h, w_n_h, p_n_h, tg_gap, left_even], 8 * thin,
    )
    odd_a, odd_b = sent(a_odd, twos[1]), sent(b_odd, other_twos[1])
    left_odd, right_odd = local_call(
        part(spikes_two_odd, order),
        [full, full], [tg, v_one, w_b, near, pair[1], tg_gap, a_odd], 5 * square, 0, (block,),
    )
    x_even = local_call(
        top_even, [slim], [g_even, left_even, right_even, even_a, even_b, left_odd], 2 * thin
    )
    x_gap = sent(x_even, to_left)
    x_odd, *x_own = local_call(
        top_odd,
        [slim, flat, flat], [g_odd, left_odd, right_odd, odd_a, odd_b], 2 * thin,
    )
    x_pair = [sent(piece, pairs) for piece in x_own]
    rest = local_call(
        part(second_values, order), [tall], [vg_b, w_b, x_even, x_odd, *x_pair], 2 * thin
    )
    return local_call(
        part(finish, order),
        [jax.ShapeDtypeStruct((2, order, rhs), BF16)], [vg_b, x_even, x_odd, rest, x_gap], thin,
    )


def solution(mesh):
    split = P(AXES, None, None)
    return jax.shard_map(
        body, mesh=mesh, in_specs=(split,) * 4, out_specs=split, check_vma=False
    )
```

```python
import functools

import jax
import jax.numpy as jnp
from jax import lax
from jax.experimental import pallas as pl
from jax.experimental.pallas import tpu as pltpu
from jax.sharding import PartitionSpec as P


AXES = ("grp", "dev")
BF16 = jnp.bfloat16
F32 = jnp.float32
VMEM_BYTES = 12 * 1024 * 1024


def is_odd():
    return lax.rem(lax.axis_index(AXES), 2) == 1


def if_left(value):
    return jnp.where(lax.axis_index(AXES) > 0, value, jnp.zeros_like(value))


def if_right(value):
    last = lax.axis_size(AXES) - 1
    return jnp.where(lax.axis_index(AXES) < last, value, jnp.zeros_like(value))


def dot(a, b):
    return jnp.dot(a, b, preferred_element_type=F32)


def by_parity(even, odd):
    odd_here = is_odd()
    if odd is not None:
        pl.when(odd_here)(odd)
    if even is not None:
        pl.when(jnp.logical_not(odd_here))(even)


def identity(order):
    rows = lax.broadcasted_iota(jnp.int32, (order, order), 0)
    return (rows == lax.broadcasted_iota(jnp.int32, (order, order), 1)).astype(F32)


def local_call(kernel, outs, ins, flops, in_hbm=0, scratch=(), aliases=None, weight=0.001):
    vmem = pl.BlockSpec(memory_space=pltpu.VMEM)
    hbm = pl.BlockSpec(memory_space=pl.ANY)
    many = len(outs) > 1
    ins = [pltpu.with_memory_space_constraint(x, pltpu.HBM) for x in ins[:in_hbm]] + ins[in_hbm:]
    return pl.pallas_call(
        kernel,
        out_shape=outs if many else outs[0],
        in_specs=[hbm] * in_hbm + [vmem] * (len(ins) - in_hbm),
        out_specs=[vmem] * len(outs) if many else vmem,
        scratch_shapes=list(scratch),
        input_output_aliases=aliases or {},
        compiler_params=pltpu.CompilerParams(vmem_limit_bytes=VMEM_BYTES),
        cost_estimate=pl.CostEstimate(flops=int(flops * weight), bytes_accessed=0, transcendentals=0),
    )(*ins)


def bf16_array(rows, columns):
    return jax.ShapeDtypeStruct((rows, columns), BF16)


def f32_array(rows, columns):
    return jax.ShapeDtypeStruct((rows, columns), F32)


def fetch(source, target, sem):
    copy = pltpu.make_async_copy(source, target, sem)
    copy.start()
    return copy


def load_row(order, diag, upper, right, vg, diag_b, upper_b, right_b, sems):
    d_b = fetch(diag.at[1], diag_b, sems.at[0])
    u_b = fetch(upper.at[1], upper_b, sems.at[1])
    r_b = fetch(right.at[1], right_b, sems.at[2])
    d_b.wait()
    u_b.wait()
    vg[:, :order] = dot(diag_b[...], upper_b[...]).astype(BF16)
    r_b.wait()
    vg[:, order:] = dot(diag_b[...], right_b[...]).astype(BF16)


def second_row_odd(order, *refs):
    by_parity(None, lambda: load_row(order, *refs))


def second_row(order, diag, upper, right, vg_odd, after, vg_b, *rest):
    *pieces, diag_b, upper_b, right_b, sems = rest

    def odd():
        vg_b[...] = vg_odd[...]

    def even():
        load_row(order, diag, upper, right, vg_b, diag_b, upper_b, right_b, sems)
        first = 0
        for piece in pieces:
            piece[...] = vg_b[:, first : first + piece.shape[1]]
            first += piece.shape[1]

    by_parity(even, odd)


def own_products_odd(
    order, diag, lower, upper, right, vg_odd, w_a, w_b, m, n, r, v_a, diag_a, lower_a, diag_b, lower_b,
    upper_a, right_a, sems,
):
    def odd():
        held = diag_a, lower_a, diag_b, lower_b, upper_a, right_a
        first_right_side(order, own_copies(diag, lower, upper, right, *held, sems), vg_odd, held, v_a, r)
        spikes_own(order, vg_odd, diag_a, lower_a, diag_b, lower_b, v_a, w_a, w_b, m, n)

    by_parity(None, odd)


def own_products_even(order, diag, lower, upper, right, vg_b, *rest):
    r, v_a, diag_a, lower_a, diag_b, lower_b, upper_a, right_a, sems = rest[6:]

    def even():
        held = diag_a, lower_a, diag_b, lower_b, upper_a, right_a
        first_right_side(order, own_copies(diag, lower, upper, right, *held, sems), vg_b, held, v_a, r)

    by_parity(even, None)


def spikes_own_even(order, vg_b, diag_a, lower_a, diag_b, lower_b, v_a, after, *rest):
    w_a, w_b, m, n = rest[4:]

    def even():
        spikes_own(order, vg_b, diag_a, lower_a, diag_b, lower_b, v_a, w_a, w_b, m, n)

    by_parity(even, None)


def own_copies(diag, lower, upper, right, diag_a, lower_a, diag_b, lower_b, upper_a, right_a, sems):
    pairs = (
        (diag.at[0], diag_a), (upper.at[0], upper_a), (right.at[0], right_a),
        (diag.at[1], diag_b), (lower.at[1], lower_b), (lower.at[0], lower_a),
    )
    return [pltpu.make_async_copy(x, y, sems.at[i]) for i, (x, y) in enumerate(pairs)]


def first_right_side(order, copies, vg_b, held, v_a, r):
    diag_a, lower_a, diag_b, lower_b, upper_a, right_a = held
    for copy in copies:
        copy.start()
    for copy in copies[:3]:
        copy.wait()
    v_a[...] = dot(diag_a[...], upper_a[...]).astype(BF16)
    g_a = dot(diag_a[...], right_a[...]).astype(BF16)
    r[...] = g_a.astype(F32) - dot(v_a[...], vg_b[:, order:])
    for copy in copies[3:]:
        copy.wait()


def spikes_own(order, vg_b, diag_a, lower_a, diag_b, lower_b, v_a, w_a, w_b, m, n):
    w_b[...] = dot(diag_b[...], lower_b[...]).astype(BF16)
    w_a[...] = dot(diag_a[...], lower_a[...]).astype(BF16)
    n[...] = dot(v_a[...], vg_b[:, :order]).astype(BF16)
    m[...] = dot(v_a[...], w_b[...])


def scale_one(order, w_a, m, r, v_left, g_left, scale, tg):
    first = 0
    eye = identity(order)
    for piece in v_left:
        at = slice(first, first + piece.shape[1])
        coupling = if_left(dot(w_a[...], piece[...])) + m[:, at]
        scale[:, at] = (eye[:, at] + coupling).astype(BF16)
        first = at.stop
    rest = (r[...] - if_left(dot(w_a[...], g_left[...]))).astype(BF16)
    tg[:, :order] = dot(scale[...], w_a[...]).astype(BF16)
    tg[:, order:] = dot(scale[...], rest).astype(BF16)


def spikes_one(order, scale, n, w_b, tg, v_one, w_t, w_v, w_g):
    v_one[...] = (-dot(scale[...], n[...])).astype(BF16)
    w_v[...] = dot(w_b[...], v_one[...]).astype(BF16)
    w_g[...] = dot(w_b[...], tg[:, order:]).astype(BF16)
    w_t[...] = dot(w_b[...], tg[:, :order]).astype(BF16)


def pack(side):
    columns = side.shape[1]
    return jnp.concatenate(
        [side[i : i + columns] for i in range(0, side.shape[0], columns)], axis=1
    )


def unpack(rows, columns):
    return jnp.concatenate(
        [rows[:, i : i + columns] for i in range(0, rows.shape[1], columns)], axis=0
    )


def hand_to_pair(order, blocks, side, to_pair):
    rows, first = pack(side), 0
    for block, piece in zip(blocks, to_pair):
        last = first + piece.shape[0] - order
        piece[:order, :] = block
        piece[order:, :] = rows[first:last]
        first = last


def side_of_pair(order, got, columns):
    return unpack(jnp.concatenate([piece[order:, :] for piece in got], axis=0), columns)


def level_one_odd(order, w_a, m, r, v0, vg1, n, w_b, tg, v_one, w_vg, *rest):
    *to_pair, scale, w_t = rest
    columns = order - v0.shape[1]

    def odd():
        v_left, g_left = [v0, vg1.at[:, :columns]], vg1.at[:, columns:]
        scale_one(order, w_a, m, r, v_left, g_left, scale, tg)
        w_v, w_g = w_vg.at[:, :order], w_vg.at[:, order:]
        spikes_one(order, scale, n, w_b, tg, v_one, w_t, w_v, w_g)
        hand_to_pair(order, [tg[:, :order], w_t[...], v_one[...]], tg[:, order:], to_pair)

    by_parity(None, odd)


def scale_one_even(order, w_a, m, r, vg, tg_odd, tg, scale):
    v_left, g_left = [vg.at[:, :order]], vg.at[:, order:]
    by_parity(lambda: scale_one(order, w_a, m, r, v_left, g_left, scale, tg), None)


def spikes_one_even(order, scale, n, w_b, tg, v_odd, pair0, pair1, pair2, tg_out, v_one, *rest):
    *to_pair, w_t, w_v, w_g = rest

    def even():
        spikes_one(order, scale, n, w_b, tg, v_one, w_t, w_v, w_g)
        hand_to_pair(order, [w_v[...], w_t[...], v_one[...]], w_g[...], to_pair)

    by_parity(even, None)


def pair_part(
    order, tg, v_one, w_b, to_pair1, w_vg, pair0, pair1, pair2,
    near, far, w_far, p_far, p_v, n_h, w_h, w_n_h, p_n_h,
):
    got, w_t, w_t_pair, v_pair = (x[:order, :] for x in (pair0, to_pair1, pair1, pair2))
    got_g = side_of_pair(order, [pair0, pair1, pair2], n_h.shape[1])
    t, eye = tg[:, :order], identity(order)

    def even():
        right = dot(got, w_b[...]).astype(BF16)
        near[...] = (eye - dot(v_one[...], right)).astype(BF16)
        far[...] = dot(w_b[...], near[...]).astype(BF16)
        p_far[...] = dot(w_t_pair, far[...]).astype(BF16)
        p_v[...] = dot(w_t_pair, w_t).astype(BF16)
        n_h[...] = tg[:, order:].astype(F32) - dot(v_one[...], got_g)

    def odd():
        near[...] = (eye - dot(t, got)).astype(BF16)
        far[...] = dot(near[...], v_one[...]).astype(BF16)
        w_far[...] = dot(w_b[...], far[...]).astype(BF16)
        p_far[...] = dot(v_pair, far[...]).astype(BF16)
        p_v[...] = dot(v_pair, v_one[...]).astype(BF16)
        own = (tg[:, order:].astype(F32) + dot(t, got_g)).astype(BF16)
        scaled = dot(near[...], own)
        n_h[...] = scaled
        w_h[...] = dot(w_b[...], own)
        w_n_h[...] = dot(w_b[...], scaled.astype(BF16))
        p_n_h[...] = dot(v_pair, scaled.astype(BF16))

    by_parity(even, odd)


def hand_out(right, left, a, b):
    left_of_two = lax.rem(lax.axis_index(AXES), 4) < 2
    a[...] = jnp.where(left_of_two, right, left)
    b[...] = jnp.where(left_of_two, left, right)


def level_two_even(order, tg, near, far, p_far, p_v, n_h, w_vg_gap, g, a, b):
    def even():
        t = tg[:, :order]
        whole = (n_h[...] + if_left(dot(t, w_vg_gap[:, order:]))).astype(BF16)
        from_left = if_left(dot(w_vg_gap[:, :order], whole)).astype(BF16)
        value = (dot(near[...], whole) - dot(t, from_left)).astype(BF16)
        onward = (dot(p_v[...], from_left) - dot(p_far[...], whole)).astype(BF16)
        g[...] = value
        hand_out(onward, value, a, b)

    by_parity(even, None)


def level_two_odd(
    order, v_one, w_vg, far, w_far, p_far, p_v, n_h, w_h, w_n_h, p_n_h, tg_gap, after, g, a, b
):
    def odd():
        g_right, w_v = tg_gap[:, order:], w_vg[:, :order]
        own = w_h[...] - if_right(dot(w_v, g_right))
        from_right = if_right(dot(tg_gap[:, :order], own.astype(BF16))).astype(BF16)

        def whole(start, gap, further):
            gap_part = if_right(dot(gap[...], g_right)) + dot(further, from_right)
            return (start[...] - gap_part).astype(BF16)

        g[...] = whole(n_h, far, v_one[...])
        hand_out(whole(w_n_h, w_far, w_v), whole(p_n_h, p_far, p_v[...]), a, b)

    by_parity(None, odd)


def if_two_left(value):
    return jnp.where(lax.axis_index(AXES) > 1, value, jnp.zeros_like(value))


def if_two_right(value):
    last = lax.axis_size(AXES) - 2
    return jnp.where(lax.axis_index(AXES) < last, value, jnp.zeros_like(value))


def spikes_two_even(order, tg, v_one, near, pair2, w_vg_gap, after, from_left, from_right, scale):
    def even():
        t = tg[:, :order]
        gap = if_left(dot(t, w_vg_gap[:, :order]))
        scale[...] = (near[...].astype(F32) - gap).astype(BF16)
        s_v = dot(scale[...], v_one[...]).astype(BF16)
        from_left[...] = if_two_left(-dot(scale[...], t)).astype(BF16)
        from_right[...] = if_two_right(dot(s_v, pair2[:order, :])).astype(BF16)

    by_parity(even, None)


def spikes_two_odd(order, tg, v_one, w_b, near, pair1, tg_gap, after, from_left, from_right, scale):
    def odd():
        right = dot(tg_gap[:, :order], w_b[...]).astype(BF16)
        gap = if_right(dot(v_one[...], right))
        scale[...] = (near[...].astype(F32) - gap).astype(BF16)
        s_t = dot(scale[...], tg[:, :order]).astype(BF16)
        from_left[...] = if_two_left(dot(s_t, pair1[:order, :])).astype(BF16)
        from_right[...] = if_two_right(dot(scale[...], v_one[...])).astype(BF16)

    by_parity(None, odd)


def top_value(g, from_left, from_right, a, b, x):
    def top(left, right):
        change = dot(from_left[...], left[...]) + dot(from_right[...], right[...])
        x[...] = (g[...].astype(F32) + change).astype(BF16)

    left_of_two = lax.rem(lax.axis_index(AXES), 4) < 2
    pl.when(left_of_two)(lambda: top(b, a))
    pl.when(jnp.logical_not(left_of_two))(lambda: top(a, b))


def top_even(g, from_left, from_right, a, b, after, x):
    by_parity(lambda: top_value(g, from_left, from_right, a, b, x), None)


def top_odd(g, from_left, from_right, a, b, x, *halves):
    def odd():
        top_value(g, from_left, from_right, a, b, x)
        rows = halves[0].shape[0]
        for i, half in enumerate(halves):
            half[...] = x[i * rows : (i + 1) * rows, :]

    by_parity(None, odd)


def second_values(order, vg_b, w_b, x_even, x_odd, x_pair0, x_pair1, rest):
    def even():
        x_next = jnp.concatenate([x_pair0[...], x_pair1[...]], axis=0)
        own = vg_b[:, order:].astype(F32) - dot(w_b[...], x_even[...])
        rest[...] = own - dot(vg_b[:, :order], x_next)

    def odd():
        rest[...] = vg_b[:, order:].astype(F32) - dot(w_b[...], x_odd[...])

    by_parity(even, odd)


def finish(order, vg_b, x_even, x_odd, rest, x_gap, out):
    def even():
        out[0] = x_even[...]
        out[1] = rest[...].astype(BF16)

    def odd():
        out[0] = x_odd[...]
        out[1] = (rest[...] - if_right(dot(vg_b[:, :order], x_gap[...]))).astype(BF16)

    by_parity(even, odd)


def exchanges(slab, count):
    pairs = [(i, i ^ 1) for i in range(count)]
    twos, other_twos = [], []
    for parity in (0, 1):
        over = [i ^ slab for i in range(count)]
        twos.append([(i, i ^ 2 if i % 2 == parity else over[i]) for i in range(count)])
        to = [((i - 2) ^ 2) + 2 if i % 2 == parity else over[i] for i in range(count)]
        for end in (parity, count - 2 + parity):
            to[end], to[end ^ 1], to[over[end ^ 1]] = end ^ 1, over[end ^ 1], end
        other_twos.append(list(enumerate(to)))
    after = [(i + 1) % count for i in range(count)]
    after[2], after[slab + 2], after[count - 1] = 0, 3, count - 5
    for first in range(slab + 3, count - 5, 4):
        after[first + 3] = first
    to_right = list(enumerate(after))
    to_left = [(count - 1 - i, count - 1 - j) for i, j in to_right]
    return pairs, twos, other_twos, to_right, to_left


def body(diag, lower, upper, right):
    order, rhs = diag.shape[1], right.shape[2]
    count = lax.axis_size(AXES)
    pairs, twos, other_twos, to_right, to_left = exchanges(lax.axis_size("dev"), count)

    def sent(block, route):
        return lax.ppermute(block, AXES, route)

    part = functools.partial
    square = 2 * order**3
    thin = 2 * order * order * rhs
    block = pltpu.VMEM((order, order), BF16)
    side = pltpu.VMEM((order, rhs), BF16)
    wide = bf16_array(order, order + rhs)
    full = bf16_array(order, order)
    slim = bf16_array(order, rhs)

    row_scratch = (block, block, side, pltpu.SemaphoreType.DMA((3,)))
    vg_odd = local_call(
        part(second_row_odd, order), [wide], [diag, upper, right], square + thin, 3, row_scratch
    )
    vg_gap = sent(vg_odd, to_right)
    own_arrays = [f32_array(order, rhs)] + [full] * 5
    spike_arrays = [full, full, f32_array(order, order), full]
    own_scratch = (block, side, pltpu.SemaphoreType.DMA((6,)))
    spikes = local_call(
        part(own_products_odd, order),
        spike_arrays + own_arrays, [diag, lower, upper, right, vg_odd], 5 * square + 2 * thin,
        4, own_scratch,
    )
    spikes, own = spikes[:4], spikes[4:]
    cut = 3 * order // 4
    vg_b, *to_pair = local_call(
        part(second_row, order),
        [wide, bf16_array(order, cut), bf16_array(order, order - cut + rhs)],
        [diag, upper, right, vg_odd, own[0]], square + thin, 3, row_scratch,
    )
    vg_pair = [sent(piece, pairs) for piece in to_pair]
    r, v_a, *held = local_call(
        part(own_products_even, order),
        own_arrays, [diag, lower, upper, right, vg_b, *own], square + 2 * thin,
        4, own_scratch, {5 + i: i for i in range(6)},
    )
    w_a, w_b, m, n = spikes
    extra = rhs // 16 * 6
    shares = [bf16_array(order + rows, order) for rows in (extra, extra, rhs - 2 * extra)]
    tg_odd, v_odd, w_vg_odd, *to_pair = local_call(
        part(level_one_odd, order),
        [wide, full, wide, *shares], [w_a, m, r, *vg_pair, n, w_b], 5 * square, 0, (block, block),
    )
    w_vg_gap = sent(w_vg_odd, to_right)
    w_a, w_b, m, n = local_call(
        part(spikes_own_even, order),
        spike_arrays, [vg_b, *held, v_a, vg_gap, *spikes], 4 * square,
        aliases={7 + i: i for i in range(4)},
    )
    tg, scale = local_call(
        part(scale_one_even, order),
        [wide, full], [w_a, m, r, vg_gap, tg_odd], 2 * square + 2 * thin, aliases={4: 0},
    )
    tg, v_one, *to_pair = local_call(
        part(spikes_one_even, order),
        [wide, full, *shares], [scale, n, w_b, tg, v_odd, *to_pair], 3 * square + thin,
        0, (block, block, side), {3: 0, 4: 1, 5: 2, 6: 3, 7: 4},
    )
    tg_gap = sent(tg, to_left)
    pair = [sent(piece, pairs) for piece in to_pair]

    tall, flat = f32_array(order, rhs), bf16_array(order // 2, rhs)
    known = local_call(
        part(pair_part, order),
        [full] * 5 + [tall] * 4,
        [tg, v_one, w_b, to_pair[1], w_vg_odd, *pair], 6 * square,
    )
    near, far, w_far, p_far, p_v, n_h, w_h, w_n_h, p_n_h = known
    g_even, a_even, b_even = local_call(
        part(level_two_even, order),
        [slim] * 3, [tg, near, far, p_far, p_v, n_h, w_vg_gap], 6 * thin,
    )
    even_a, even_b = sent(a_even, twos[0]), sent(b_even, other_twos[0])
    left_even, right_even = local_call(
        part(spikes_two_even, order),
        [full, full], [tg, v_one, near, pair[2], w_vg_gap, a_even], 4 * square, 0, (block,),
    )
    g_odd, a_odd, b_odd = local_call(
        part(level_two_odd, order),
        [slim] * 3,
        [v_one, w_vg_odd, far, w_far, p_far, p_v, n_h, w_h, w_n_h, p_n_h, tg_gap, left_even], 8 * thin,
    )
    odd_a, odd_b = sent(a_odd, twos[1]), sent(b_odd, other_twos[1])
    left_odd, right_odd = local_call(
        part(spikes_two_odd, order),
        [full, full], [tg, v_one, w_b, near, pair[1], tg_gap, a_odd], 5 * square, 0, (block,),
    )
    x_even = local_call(
        top_even, [slim], [g_even, left_even, right_even, even_a, even_b, left_odd], 2 * thin
    )
    x_gap = sent(x_even, to_left)
    x_odd, *x_own = local_call(
        top_odd,
        [slim, flat, flat], [g_odd, left_odd, right_odd, odd_a, odd_b], 2 * thin,
    )
    x_pair = [sent(piece, pairs) for piece in x_own]
    rest = local_call(
        part(second_values, order), [tall], [vg_b, w_b, x_even, x_odd, *x_pair], 2 * thin
    )
    return local_call(
        part(finish, order),
        [jax.ShapeDtypeStruct((2, order, rhs), BF16)], [vg_b, x_even, x_odd, rest, x_gap], thin,
    )


def solution(mesh):
    split = P(AXES, None, None)
    return jax.shard_map(
        body, mesh=mesh, in_specs=(split,) * 4, out_specs=split, check_vma=False
    )
```

```python
import functools

import jax
import jax.numpy as jnp
from jax import lax
from jax.experimental import pallas as pl
from jax.experimental.pallas import tpu as pltpu
from jax.sharding import PartitionSpec as P


AXES = ("grp", "dev")
BF16 = jnp.bfloat16
F32 = jnp.float32
VMEM_BYTES = 12 * 1024 * 1024


def is_odd():
    return lax.rem(lax.axis_index(AXES), 2) == 1


def if_left(value):
    return jnp.where(lax.axis_index(AXES) > 0, value, jnp.zeros_like(value))


def if_right(value):
    last = lax.axis_size(AXES) - 1
    return jnp.where(lax.axis_index(AXES) < last, value, jnp.zeros_like(value))


def dot(a, b):
    return jnp.dot(a, b, preferred_element_type=F32)


def by_parity(even, odd):
    odd_here = is_odd()
    if odd is not None:
        pl.when(odd_here)(odd)
    if even is not None:
        pl.when(jnp.logical_not(odd_here))(even)


def identity(order):
    rows = lax.broadcasted_iota(jnp.int32, (order, order), 0)
    return (rows == lax.broadcasted_iota(jnp.int32, (order, order), 1)).astype(F32)


def local_call(kernel, outs, ins, flops, in_hbm=0, scratch=(), aliases=None, weight=0.001):
    vmem = pl.BlockSpec(memory_space=pltpu.VMEM)
    hbm = pl.BlockSpec(memory_space=pl.ANY)
    many = len(outs) > 1
    ins = [pltpu.with_memory_space_constraint(x, pltpu.HBM) for x in ins[:in_hbm]] + ins[in_hbm:]
    return pl.pallas_call(
        kernel,
        out_shape=outs if many else outs[0],
        in_specs=[hbm] * in_hbm + [vmem] * (len(ins) - in_hbm),
        out_specs=[vmem] * len(outs) if many else vmem,
        scratch_shapes=list(scratch),
        input_output_aliases=aliases or {},
        compiler_params=pltpu.CompilerParams(vmem_limit_bytes=VMEM_BYTES),
        cost_estimate=pl.CostEstimate(flops=int(flops * weight), bytes_accessed=0, transcendentals=0),
    )(*ins)


def bf16_array(rows, columns):
    return jax.ShapeDtypeStruct((rows, columns), BF16)


def f32_array(rows, columns):
    return jax.ShapeDtypeStruct((rows, columns), F32)


def fetch(source, target, sem):
    copy = pltpu.make_async_copy(source, target, sem)
    copy.start()
    return copy


def load_row(order, diag, upper, right, vg, diag_b, sides, sems, later=()):
    copies = [
        fetch(diag.at[1], diag_b, sems.at[0]),
        fetch(upper.at[1], sides.at[:, :order], sems.at[1]),
        fetch(right.at[1], sides.at[:, order:], sems.at[2]),
    ]
    for copy in later:
        copy.start()
    for copy in copies:
        copy.wait()
    vg[...] = dot(diag_b[...], sides[...]).astype(BF16)


def second_row_odd(order, diag, upper, right, lower, vg, diag_b, lower_b, sides, sems):
    def odd():
        later = pltpu.make_async_copy(lower.at[1], lower_b, sems.at[3])
        load_row(order, diag, upper, right, vg, diag_b, sides, sems, [later])
        later.wait()

    by_parity(None, odd)


def second_row(order, diag, upper, right, vg_odd, after, vg_b, *rest):
    *pieces, diag_b, sides, sems = rest

    def odd():
        vg_b[...] = vg_odd[...]

    def even():
        load_row(order, diag, upper, right, vg_b, diag_b, sides, sems)
        first = 0
        for piece in pieces:
            piece[...] = vg_b[:, first : first + piece.shape[1]]
            first += piece.shape[1]

    by_parity(even, odd)


def own_products_odd(
    order, diag, lower, upper, right, vg_odd, diag_b, lower_b,
    w_a, w_b, m, n, r, v_a, diag_a, lower_a, upper_a, right_a, sems,
):
    def odd():
        copies = first_row_copies(diag, lower, upper, right, diag_a, lower_a, upper_a, right_a, sems)
        for copy in copies:
            copy.start()
        w_b[...] = dot(diag_b[...], lower_b[...]).astype(BF16)
        first_right_side(order, copies, vg_odd, diag_a, upper_a, right_a, v_a, r)
        first_spikes(order, vg_odd, diag_a, lower_a, v_a, w_a, w_b, m, n)

    by_parity(None, odd)


def own_products_even(order, diag, lower, upper, right, vg_b, *rest):
    r, v_a, diag_a, lower_a, diag_b, lower_b, upper_a, right_a, sems = rest[6:]

    def even():
        copies = first_row_copies(diag, lower, upper, right, diag_a, lower_a, upper_a, right_a, sems)
        copies += [
            pltpu.make_async_copy(diag.at[1], diag_b, sems.at[4]),
            pltpu.make_async_copy(lower.at[1], lower_b, sems.at[5]),
        ]
        for copy in copies:
            copy.start()
        first_right_side(order, copies, vg_b, diag_a, upper_a, right_a, v_a, r)

    by_parity(even, None)


def spikes_own_even(order, vg_b, diag_a, lower_a, diag_b, lower_b, v_a, after, *rest):
    w_a, w_b, m, n = rest[4:]

    def even():
        w_b[...] = dot(diag_b[...], lower_b[...]).astype(BF16)
        first_spikes(order, vg_b, diag_a, lower_a, v_a, w_a, w_b, m, n)

    by_parity(even, None)


def first_row_copies(diag, lower, upper, right, diag_a, lower_a, upper_a, right_a, sems):
    pairs = (diag, diag_a), (upper, upper_a), (right, right_a), (lower, lower_a)
    return [pltpu.make_async_copy(x.at[0], y, sems.at[i]) for i, (x, y) in enumerate(pairs)]


def first_right_side(order, copies, vg_b, diag_a, upper_a, right_a, v_a, r):
    for copy in copies[:3]:
        copy.wait()
    v_a[...] = dot(diag_a[...], upper_a[...]).astype(BF16)
    g_a = dot(diag_a[...], right_a[...]).astype(BF16)
    r[...] = g_a.astype(F32) - dot(v_a[...], vg_b[:, order:])
    for copy in copies[3:]:
        copy.wait()


def first_spikes(order, vg_b, diag_a, lower_a, v_a, w_a, w_b, m, n):
    w_a[...] = dot(diag_a[...], lower_a[...]).astype(BF16)
    n[...] = dot(v_a[...], vg_b[:, :order]).astype(BF16)
    m[...] = dot(v_a[...], w_b[...])


def scale_one(order, w_a, m, r, v_left, g_left, scale, tg):
    first = 0
    eye = identity(order)
    for piece in v_left:
        at = slice(first, first + piece.shape[1])
        coupling = if_left(dot(w_a[...], piece[...])) + m[:, at]
        scale[:, at] = (eye[:, at] + coupling).astype(BF16)
        first = at.stop
    rest = (r[...] - if_left(dot(w_a[...], g_left[...]))).astype(BF16)
    tg[:, :order] = dot(scale[...], w_a[...]).astype(BF16)
    tg[:, order:] = dot(scale[...], rest).astype(BF16)


def spikes_one(order, scale, n, w_b, tg, v_one, w_t, w_v, w_g):
    v_one[...] = (-dot(scale[...], n[...])).astype(BF16)
    w_v[...] = dot(w_b[...], v_one[...]).astype(BF16)
    w_g[...] = dot(w_b[...], tg[:, order:]).astype(BF16)
    w_t[...] = dot(w_b[...], tg[:, :order]).astype(BF16)


def pack(side):
    columns = side.shape[1]
    return jnp.concatenate(
        [side[i : i + columns] for i in range(0, side.shape[0], columns)], axis=1
    )


def unpack(rows, columns):
    return jnp.concatenate(
        [rows[:, i : i + columns] for i in range(0, rows.shape[1], columns)], axis=0
    )


def hand_to_pair(order, blocks, side, to_pair):
    rows, first = pack(side), 0
    for block, piece in zip(blocks, to_pair):
        last = first + piece.shape[0] - order
        piece[:order, :] = block
        if last > first:
            piece[order:, :] = rows[first:last]
        first = last


def side_of_pair(order, got, columns):
    return unpack(jnp.concatenate([piece[order:, :] for piece in got], axis=0), columns)


def level_one_odd(order, w_a, m, r, v0, vg1, n, w_b, tg, v_one, w_vg, *rest):
    *to_pair, scale, w_t = rest
    columns = order - v0.shape[1]

    def odd():
        v_left, g_left = [v0, vg1.at[:, :columns]], vg1.at[:, columns:]
        scale_one(order, w_a, m, r, v_left, g_left, scale, tg)
        w_v, w_g = w_vg.at[:, :order], w_vg.at[:, order:]
        spikes_one(order, scale, n, w_b, tg, v_one, w_t, w_v, w_g)
        hand_to_pair(order, [tg[:, :order], w_t[...], v_one[...]], tg[:, order:], to_pair)

    by_parity(None, odd)


def scale_one_even(order, w_a, m, r, vg, tg_odd, tg, scale):
    v_left, g_left = [vg.at[:, :order]], vg.at[:, order:]
    by_parity(lambda: scale_one(order, w_a, m, r, v_left, g_left, scale, tg), None)


def spikes_one_even(order, scale, n, w_b, tg, v_odd, pair0, pair1, pair2, tg_out, v_one, *rest):
    *to_pair, w_t, w_v, w_g = rest

    def even():
        spikes_one(order, scale, n, w_b, tg, v_one, w_t, w_v, w_g)
        hand_to_pair(order, [w_v[...], w_t[...], v_one[...]], w_g[...], to_pair)

    by_parity(even, None)


def same(value):
    return value


def pair_part_even(order, tg, v_one, w_b, pair0, pair1, near, n_h):
    def even():
        right = dot(pair0[:order, :], w_b[...]).astype(BF16)
        near[...] = (identity(order) - dot(v_one[...], right)).astype(BF16)
        side = side_of_pair(order, [pair0, pair1], n_h.shape[1])
        n_h[...] = tg[:, order:].astype(F32) - dot(v_one[...], side)

    by_parity(even, None)


def pair_part_odd(
    order, tg, v_one, w_b, pair0, pair1, pair2, near, far, w_far, p_far, p_v, n_h, w_h, w_n_h, p_n_h
):
    def odd():
        t, v_pair = tg[:, :order], pair2[...]
        near[...] = (identity(order) - dot(t, pair0[:order, :])).astype(BF16)
        far[...] = dot(near[...], v_one[...]).astype(BF16)
        w_far[...] = dot(w_b[...], far[...]).astype(BF16)
        p_far[...] = dot(v_pair, far[...]).astype(BF16)
        p_v[...] = dot(v_pair, v_one[...]).astype(BF16)
        side = side_of_pair(order, [pair0, pair1], n_h.shape[1])
        own = (tg[:, order:].astype(F32) + dot(t, side)).astype(BF16)
        scaled = dot(near[...], own)
        n_h[...] = scaled
        w_h[...] = dot(w_b[...], own)
        w_n_h[...] = dot(w_b[...], scaled.astype(BF16))
        p_n_h[...] = dot(v_pair, scaled.astype(BF16))

    by_parity(None, odd)


def hand_over(block, out):
    rows = block.shape[0]
    out[:rows, :] = block[...]
    if out.shape[0] > rows:
        out[rows:, :] = jnp.zeros((out.shape[0] - rows, out.shape[1]), BF16)


def hand_out(right, left, a, b):
    left_of_two = lax.rem(lax.axis_index(AXES), 4) < 2
    hand_over(jnp.where(left_of_two, right, left), a)
    b[...] = jnp.where(left_of_two, left, right)


def level_two_even(order, tg, w_b, near, n_h, pair1, w_vg_gap, g, a, b):
    def even():
        t = tg[:, :order]
        whole = (n_h[...] + if_left(dot(t, w_vg_gap[:, order:]))).astype(BF16)
        from_left = if_left(dot(w_vg_gap[:, :order], whole)).astype(BF16)
        value = (dot(near[...], whole) - dot(t, from_left)).astype(BF16)
        onward = (-dot(pair1[:order, :], dot(w_b[...], value).astype(BF16))).astype(BF16)
        g[...] = value
        hand_out(onward, value, a, b)

    by_parity(even, None)


def level_two_odd(
    order, v_one, w_vg, far, w_far, p_far, p_v, n_h, w_h, w_n_h, p_n_h, tg_gap, after, g, a, b
):
    def odd():
        g_right, w_v = tg_gap[:, order:], w_vg[:, :order]
        own = w_h[...] - if_right(dot(w_v, g_right))
        from_right = if_right(dot(tg_gap[:, :order], own.astype(BF16))).astype(BF16)

        def whole(start, gap, further):
            gap_part = if_right(dot(gap[...], g_right)) + dot(further, from_right)
            return (start[...] - gap_part).astype(BF16)

        g[...] = whole(n_h, far, v_one[...])
        hand_out(whole(w_n_h, w_far, w_v), whole(p_n_h, p_far, p_v[...]), a, b)

    by_parity(None, odd)


def if_two_left(value):
    return jnp.where(lax.axis_index(AXES) > 1, value, jnp.zeros_like(value))


def if_two_right(value):
    last = lax.axis_size(AXES) - 2
    return jnp.where(lax.axis_index(AXES) < last, value, jnp.zeros_like(value))


def spikes_two_even(order, tg, v_one, near, pair2, w_vg_gap, after, from_left, from_right, scale):
    def even():
        t = tg[:, :order]
        gap = if_left(dot(t, w_vg_gap[:, :order]))
        scale[...] = (near[...].astype(F32) - gap).astype(BF16)
        s_v = dot(scale[...], v_one[...]).astype(BF16)
        from_left[...] = if_two_left(-dot(scale[...], t)).astype(BF16)
        from_right[...] = if_two_right(dot(s_v, pair2[:order, :])).astype(BF16)

    by_parity(even, None)


def spikes_two_odd(order, tg, v_one, w_b, near, pair1, tg_gap, after, from_left, from_right, scale):
    def odd():
        right = dot(tg_gap[:, :order], w_b[...]).astype(BF16)
        gap = if_right(dot(v_one[...], right))
        scale[...] = (near[...].astype(F32) - gap).astype(BF16)
        s_t = dot(scale[...], tg[:, :order]).astype(BF16)
        from_left[...] = if_two_left(dot(s_t, pair1[:order, :])).astype(BF16)
        from_right[...] = if_two_right(dot(scale[...], v_one[...])).astype(BF16)

    by_parity(None, odd)


def top_value(g, from_left, from_right, a, b, x):
    def top(left, right):
        rows = g.shape[0]
        change = dot(from_left[...], left[:rows, :]) + dot(from_right[...], right[:rows, :])
        x[...] = (g[...].astype(F32) + change).astype(BF16)

    left_of_two = lax.rem(lax.axis_index(AXES), 4) < 2
    pl.when(left_of_two)(lambda: top(b, a))
    pl.when(jnp.logical_not(left_of_two))(lambda: top(a, b))


def top_even(g, from_left, from_right, a, b, x, x_out):
    def even():
        top_value(g, from_left, from_right, a, b, x)
        hand_over(x, x_out)

    by_parity(even, None)


def top_odd(g, from_left, from_right, a, b, x):
    by_parity(None, lambda: top_value(g, from_left, from_right, a, b, x))


def start_second(order, vg_b, w_b, x_even, x_odd, rest):
    def start(x):
        rest[...] = vg_b[:, order:].astype(F32) - dot(w_b[...], x[...])

    by_parity(lambda: start(x_even), lambda: start(x_odd))


def finish(order, vg_b, x_even, x_odd, rest, x_pair, x_gap, out):
    def rows(x, x_next, right_on):
        out[0] = x[...]
        out[1] = (rest[...] - right_on(dot(vg_b[:, :order], x_next[:order, :]))).astype(BF16)

    by_parity(lambda: rows(x_even, x_pair, same), lambda: rows(x_odd, x_gap, if_right))


def exchanges(slab, count):
    pairs = [(i, i ^ 1) for i in range(count)]
    twos, other_twos = [], []
    for parity in (0, 1):
        over = [i ^ slab for i in range(count)]
        twos.append([(i, i ^ 2 if i % 2 == parity else over[i]) for i in range(count)])
        to = [((i - 2) ^ 2) + 2 if i % 2 == parity else over[i] for i in range(count)]
        for end in (parity, count - 2 + parity):
            to[end], to[end ^ 1], to[over[end ^ 1]] = end ^ 1, over[end ^ 1], end
        other_twos.append(list(enumerate(to)))
    after = [(i + 1) % count for i in range(count)]
    after[2], after[slab + 2], after[count - 1] = 0, 3, count - 5
    for first in range(slab + 3, count - 5, 4):
        after[first + 3] = first
    to_right = list(enumerate(after))
    to_left = [(count - 1 - i, count - 1 - j) for i, j in to_right]
    return pairs, twos, other_twos, to_right, to_left


def body(diag, lower, upper, right):
    order, rhs = diag.shape[1], right.shape[2]
    count = lax.axis_size(AXES)
    pairs, twos, other_twos, to_right, to_left = exchanges(lax.axis_size("dev"), count)

    def sent(block, route):
        return lax.ppermute(block, AXES, route)

    part = functools.partial
    square = 2 * order**3
    thin = 2 * order * order * rhs
    block = pltpu.VMEM((order, order), BF16)
    side = pltpu.VMEM((order, rhs), BF16)
    wide = bf16_array(order, order + rhs)
    full = bf16_array(order, order)
    slim = bf16_array(order, rhs)

    row_scratch = (pltpu.VMEM((order, order + rhs), BF16), pltpu.SemaphoreType.DMA((4,)))
    vg_odd, diag_b, lower_b = local_call(
        part(second_row_odd, order),
        [wide, full, full], [diag, upper, right, lower], square + thin, 4, row_scratch,
    )
    vg_gap = sent(vg_odd, to_right)
    own_arrays = [f32_array(order, rhs)] + [full] * 3
    spike_arrays = [full, full, f32_array(order, order), full]
    own_scratch = (block, side, pltpu.SemaphoreType.DMA((6,)))
    spikes = local_call(
        part(own_products_odd, order),
        spike_arrays + own_arrays, [diag, lower, upper, right, vg_odd, diag_b, lower_b],
        5 * square + 2 * thin, 4, own_scratch,
    )
    spikes, own = spikes[:4], [*spikes[4:], diag_b, lower_b]
    cut = 3 * order // 4
    vg_b, *to_pair = local_call(
        part(second_row, order),
        [wide, bf16_array(order, cut), bf16_array(order, order - cut + rhs)],
        [diag, upper, right, vg_odd, own[0]], square + thin, 3, (block, *row_scratch),
    )
    vg_pair = [sent(piece, pairs) for piece in to_pair]
    r, v_a, *held = local_call(
        part(own_products_even, order),
        own_arrays + [full] * 2, [diag, lower, upper, right, vg_b, *own], square + 2 * thin,
        4, own_scratch, {5 + i: i for i in range(6)},
    )
    w_a, w_b, m, n = spikes
    shares = [bf16_array(order + rows, order) for rows in (rhs // 2, rhs // 2, 0)]
    tg_odd, v_odd, w_vg_odd, *to_pair = local_call(
        part(level_one_odd, order),
        [wide, full, wide, *shares], [w_a, m, r, *vg_pair, n, w_b], 5 * square, 0, (block, block),
    )
    w_vg_gap = sent(w_vg_odd, to_right)
    w_a, w_b, m, n = local_call(
        part(spikes_own_even, order),
        spike_arrays, [vg_b, *held, v_a, vg_gap, *spikes], 4 * square,
        aliases={7 + i: i for i in range(4)},
    )
    tg, scale = local_call(
        part(scale_one_even, order),
        [wide, full], [w_a, m, r, vg_gap, tg_odd], 2 * square + 2 * thin, aliases={4: 0},
    )
    tg, v_one, *to_pair = local_call(
        part(spikes_one_even, order),
        [wide, full, *shares], [scale, n, w_b, tg, v_odd, *to_pair], 3 * square + thin,
        0, (block, block, side), {3: 0, 4: 1, 5: 2, 6: 3, 7: 4},
    )
    tg_gap = sent(tg, to_left)
    pair = [sent(piece, pairs) for piece in to_pair]

    tall, tall_slim = f32_array(order, rhs), bf16_array(order + 16, rhs)
    near_even, n_h_even = local_call(
        part(pair_part_even, order), [full, tall], [tg, v_one, w_b, *pair[:2]], 2 * square + thin
    )
    near, far, w_far, p_far, p_v, n_h, w_h, w_n_h, p_n_h = local_call(
        part(pair_part_odd, order),
        [full] * 5 + [tall] * 4, [tg, v_one, w_b, *pair], 5 * square + 5 * thin,
    )
    g_even, a_even, b_even = local_call(
        part(level_two_even, order),
        [slim] * 3, [tg, w_b, near_even, n_h_even, pair[1], w_vg_gap], 6 * thin,
    )
    even_a, even_b = sent(a_even, twos[0]), sent(b_even, other_twos[0])
    left_even, right_even = local_call(
        part(spikes_two_even, order),
        [full, full], [tg, v_one, near_even, pair[2], w_vg_gap, a_even], 4 * square, 0, (block,),
    )
    g_odd, a_odd, b_odd = local_call(
        part(level_two_odd, order),
        [slim, tall_slim, slim],
        [v_one, w_vg_odd, far, w_far, p_far, p_v, n_h, w_h, w_n_h, p_n_h, tg_gap, left_even], 8 * thin,
    )
    odd_a, odd_b = sent(a_odd, twos[1]), sent(b_odd, other_twos[1])
    left_odd, right_odd = local_call(
        part(spikes_two_odd, order),
        [full, full], [tg, v_one, w_b, near, pair[1], tg_gap, a_odd], 5 * square, 0, (block,),
    )
    x_even, x_out = local_call(
        top_even, [slim, tall_slim], [g_even, left_even, right_even, even_a, even_b], 2 * thin
    )
    x_gap = sent(x_out, to_left)
    x_odd = local_call(top_odd, [slim], [g_odd, left_odd, right_odd, odd_a, odd_b], 2 * thin)
    x_pair = sent(x_odd, pairs)
    rest = local_call(part(start_second, order), [tall], [vg_b, w_b, x_even, x_odd], thin)
    return local_call(
        part(finish, order),
        [jax.ShapeDtypeStruct((2, order, rhs), BF16)],
        [vg_b, x_even, x_odd, rest, x_pair, x_gap], thin,
    )


def solution(mesh):
    split = P(AXES, None, None)
    return jax.shard_map(
        body, mesh=mesh, in_specs=(split,) * 4, out_specs=split, check_vma=False
    )
```

```python
import functools

import jax
import jax.numpy as jnp
from jax import lax
from jax.experimental import pallas as pl
from jax.experimental.pallas import tpu as pltpu
from jax.sharding import PartitionSpec as P


AXES = ("grp", "dev")
BF16 = jnp.bfloat16
F32 = jnp.float32
VMEM_BYTES = 12 * 1024 * 1024


def is_odd():
    return lax.rem(lax.axis_index(AXES), 2) == 1


def if_left(value):
    return jnp.where(lax.axis_index(AXES) > 0, value, jnp.zeros_like(value))


def if_right(value):
    last = lax.axis_size(AXES) - 1
    return jnp.where(lax.axis_index(AXES) < last, value, jnp.zeros_like(value))


def dot(a, b):
    return jnp.dot(a, b, preferred_element_type=F32)


def by_parity(even, odd):
    odd_here = is_odd()
    if odd is not None:
        pl.when(odd_here)(odd)
    if even is not None:
        pl.when(jnp.logical_not(odd_here))(even)


def identity(order):
    rows = lax.broadcasted_iota(jnp.int32, (order, order), 0)
    return (rows == lax.broadcasted_iota(jnp.int32, (order, order), 1)).astype(F32)


def local_call(
    kernel, outs, ins, flops, in_hbm=0, scratch=(), aliases=None, weight=0.001, out_in_hbm=False
):
    vmem = pl.BlockSpec(memory_space=pltpu.VMEM)
    hbm = pl.BlockSpec(memory_space=pl.ANY)
    many = len(outs) > 1
    ins = [pltpu.with_memory_space_constraint(x, pltpu.HBM) for x in ins[:in_hbm]] + ins[in_hbm:]
    return pl.pallas_call(
        kernel,
        out_shape=outs if many else outs[0],
        in_specs=[hbm] * in_hbm + [vmem] * (len(ins) - in_hbm),
        out_specs=[vmem] * len(outs) if many else pl.BlockSpec(memory_space=pltpu.HBM) if out_in_hbm else vmem,
        scratch_shapes=list(scratch),
        input_output_aliases=aliases or {},
        compiler_params=pltpu.CompilerParams(vmem_limit_bytes=VMEM_BYTES),
        cost_estimate=pl.CostEstimate(flops=int(flops * weight), bytes_accessed=0, transcendentals=0),
    )(*ins)


def bf16_array(rows, columns):
    return jax.ShapeDtypeStruct((rows, columns), BF16)


def f32_array(rows, columns):
    return jax.ShapeDtypeStruct((rows, columns), F32)


def fetch(source, target, sem):
    copy = pltpu.make_async_copy(source, target, sem)
    copy.start()
    return copy


def load_row(order, diag, upper, right, vg, diag_b, sides, sems, later=()):
    copies = [
        fetch(diag.at[1], diag_b, sems.at[0]),
        fetch(upper.at[1], sides.at[:, :order], sems.at[1]),
        fetch(right.at[1], sides.at[:, order:], sems.at[2]),
    ]
    for copy in later:
        copy.start()
    for copy in copies:
        copy.wait()
    vg[...] = dot(diag_b[...], sides[...]).astype(BF16)


def second_row_odd(order, diag, upper, right, lower, vg, diag_b, lower_b, sides, sems):
    def odd():
        later = pltpu.make_async_copy(lower.at[1], lower_b, sems.at[3])
        load_row(order, diag, upper, right, vg, diag_b, sides, sems, [later])
        later.wait()

    by_parity(None, odd)


def second_row(order, diag, upper, right, vg_odd, after, vg_b, *rest):
    *pieces, diag_b, sides, sems = rest

    def odd():
        vg_b[...] = vg_odd[...]

    def even():
        load_row(order, diag, upper, right, vg_b, diag_b, sides, sems)
        first = 0
        for piece in pieces:
            piece[...] = vg_b[:, first : first + piece.shape[1]]
            first += piece.shape[1]

    by_parity(even, odd)


def own_products_odd(
    order, diag, lower, upper, right, vg_odd, diag_b, lower_b,
    w_a, w_b, m, n, r, v_a, diag_a, lower_a, upper_a, right_a, sems,
):
    def odd():
        copies = first_row_copies(diag, lower, upper, right, diag_a, lower_a, upper_a, right_a, sems)
        for copy in copies:
            copy.start()
        w_b[...] = dot(diag_b[...], lower_b[...]).astype(BF16)
        first_right_side(order, copies, vg_odd, diag_a, upper_a, right_a, v_a, r)
        first_spikes(order, vg_odd, diag_a, lower_a, v_a, w_a, w_b, m, n)

    by_parity(None, odd)


def own_products_even(order, diag, lower, upper, right, vg_b, *rest):
    r, v_a, diag_a, lower_a, diag_b, lower_b, upper_a, right_a, sems = rest[6:]

    def even():
        copies = first_row_copies(diag, lower, upper, right, diag_a, lower_a, upper_a, right_a, sems)
        copies += [
            pltpu.make_async_copy(diag.at[1], diag_b, sems.at[4]),
            pltpu.make_async_copy(lower.at[1], lower_b, sems.at[5]),
        ]
        for copy in copies:
            copy.start()
        first_right_side(order, copies, vg_b, diag_a, upper_a, right_a, v_a, r)

    by_parity(even, None)


def spikes_own_even(order, vg_b, diag_a, lower_a, diag_b, lower_b, v_a, after, *rest):
    w_a, w_b, m, n = rest[4:]

    def even():
        w_b[...] = dot(diag_b[...], lower_b[...]).astype(BF16)
        first_spikes(order, vg_b, diag_a, lower_a, v_a, w_a, w_b, m, n)

    by_parity(even, None)


def first_row_copies(diag, lower, upper, right, diag_a, lower_a, upper_a, right_a, sems):
    pairs = (diag, diag_a), (upper, upper_a), (right, right_a), (lower, lower_a)
    return [pltpu.make_async_copy(x.at[0], y, sems.at[i]) for i, (x, y) in enumerate(pairs)]


def first_right_side(order, copies, vg_b, diag_a, upper_a, right_a, v_a, r):
    for copy in copies[:3]:
        copy.wait()
    v_a[...] = dot(diag_a[...], upper_a[...]).astype(BF16)
    g_a = dot(diag_a[...], right_a[...]).astype(BF16)
    r[...] = g_a.astype(F32) - dot(v_a[...], vg_b[:, order:])
    for copy in copies[3:]:
        copy.wait()


def first_spikes(order, vg_b, diag_a, lower_a, v_a, w_a, w_b, m, n):
    w_a[...] = dot(diag_a[...], lower_a[...]).astype(BF16)
    n[...] = dot(v_a[...], vg_b[:, :order]).astype(BF16)
    m[...] = dot(v_a[...], w_b[...])


def scale_one(order, w_a, m, r, v_left, g_left, scale, tg):
    first = 0
    eye = identity(order)
    for piece in v_left:
        at = slice(first, first + piece.shape[1])
        coupling = if_left(dot(w_a[...], piece[...])) + m[:, at]
        scale[:, at] = (eye[:, at] + coupling).astype(BF16)
        first = at.stop
    rest = (r[...] - if_left(dot(w_a[...], g_left[...]))).astype(BF16)
    tg[:, :order] = dot(scale[...], w_a[...]).astype(BF16)
    tg[:, order:] = dot(scale[...], rest).astype(BF16)


def spikes_one(order, scale, n, w_b, tg, v_one, w_t, w_v, w_g):
    v_one[...] = (-dot(scale[...], n[...])).astype(BF16)
    w_v[...] = dot(w_b[...], v_one[...]).astype(BF16)
    w_g[...] = dot(w_b[...], tg[:, order:]).astype(BF16)
    w_t[...] = dot(w_b[...], tg[:, :order]).astype(BF16)


def pack(side):
    columns = side.shape[1]
    return jnp.concatenate(
        [side[i : i + columns] for i in range(0, side.shape[0], columns)], axis=1
    )


def unpack(rows, columns):
    return jnp.concatenate(
        [rows[:, i : i + columns] for i in range(0, rows.shape[1], columns)], axis=0
    )


def hand_to_pair(order, blocks, side, to_pair):
    rows, first = pack(side), 0
    for block, piece in zip(blocks, to_pair):
        last = first + piece.shape[0] - order
        piece[:order, :] = block
        if last > first:
            piece[order:, :] = rows[first:last]
        first = last


def side_of_pair(order, got, columns):
    return unpack(jnp.concatenate([piece[order:, :] for piece in got], axis=0), columns)


def level_one_odd(order, w_a, m, r, v0, vg1, n, w_b, tg, v_one, w_vg, *rest):
    *to_pair, scale, w_t = rest
    columns = order - v0.shape[1]

    def odd():
        v_left, g_left = [v0, vg1.at[:, :columns]], vg1.at[:, columns:]
        scale_one(order, w_a, m, r, v_left, g_left, scale, tg)
        w_v, w_g = w_vg.at[:, :order], w_vg.at[:, order:]
        spikes_one(order, scale, n, w_b, tg, v_one, w_t, w_v, w_g)
        hand_to_pair(order, [tg[:, :order], w_t[...], v_one[...]], tg[:, order:], to_pair)

    by_parity(None, odd)


def scale_one_even(order, w_a, m, r, vg, tg_odd, tg, scale):
    v_left, g_left = [vg.at[:, :order]], vg.at[:, order:]
    by_parity(lambda: scale_one(order, w_a, m, r, v_left, g_left, scale, tg), None)


def spikes_one_even(order, scale, n, w_b, tg, v_odd, pair0, pair1, pair2, tg_out, v_one, *rest):
    *to_pair, w_t, w_v, w_g = rest

    def even():
        spikes_one(order, scale, n, w_b, tg, v_one, w_t, w_v, w_g)
        hand_to_pair(order, [w_v[...], w_t[...], v_one[...]], w_g[...], to_pair)

    by_parity(even, None)


def same(value):
    return value


def pair_part_even(order, tg, v_one, w_b, pair0, pair1, near, n_h):
    def even():
        right = dot(pair0[:order, :], w_b[...]).astype(BF16)
        near[...] = (identity(order) - dot(v_one[...], right)).astype(BF16)
        side = side_of_pair(order, [pair0, pair1], n_h.shape[1])
        n_h[...] = tg[:, order:].astype(F32) - dot(v_one[...], side)

    by_parity(even, None)


def pair_part_odd(
    order, tg, v_one, w_b, pair0, pair1, pair2, near, far, w_far, p_far, p_v, n_h, w_h, w_n_h, p_n_h
):
    def odd():
        t, v_pair = tg[:, :order], pair2[...]
        near[...] = (identity(order) - dot(t, pair0[:order, :])).astype(BF16)
        far[...] = dot(near[...], v_one[...]).astype(BF16)
        w_far[...] = dot(w_b[...], far[...]).astype(BF16)
        p_far[...] = dot(v_pair, far[...]).astype(BF16)
        p_v[...] = dot(v_pair, v_one[...]).astype(BF16)
        side = side_of_pair(order, [pair0, pair1], n_h.shape[1])
        own = (tg[:, order:].astype(F32) + dot(t, side)).astype(BF16)
        scaled = dot(near[...], own)
        n_h[...] = scaled
        w_h[...] = dot(w_b[...], own)
        w_n_h[...] = dot(w_b[...], scaled.astype(BF16))
        p_n_h[...] = dot(v_pair, scaled.astype(BF16))

    by_parity(None, odd)


def hand_over(block, out):
    rows = block.shape[0]
    out[:rows, :] = block[...]
    if out.shape[0] > rows:
        out[rows:, :] = jnp.zeros((out.shape[0] - rows, out.shape[1]), BF16)


def hand_out(right, left, a, b):
    left_of_two = lax.rem(lax.axis_index(AXES), 4) < 2
    hand_over(jnp.where(left_of_two, right, left), a)
    b[...] = jnp.where(left_of_two, left, right)


def level_two_even(order, tg, w_b, near, n_h, pair1, w_vg_gap, g, a, b):
    def even():
        t = tg[:, :order]
        whole = (n_h[...] + if_left(dot(t, w_vg_gap[:, order:]))).astype(BF16)
        from_left = if_left(dot(w_vg_gap[:, :order], whole)).astype(BF16)
        value = (dot(near[...], whole) - dot(t, from_left)).astype(BF16)
        onward = (-dot(pair1[:order, :], dot(w_b[...], value).astype(BF16))).astype(BF16)
        g[...] = value
        hand_out(onward, value, a, b)

    by_parity(even, None)


def level_two_odd(
    order, v_one, w_vg, far, w_far, p_far, p_v, n_h, w_h, w_n_h, p_n_h, tg_gap, after, g, a, b
):
    def odd():
        g_right, w_v = tg_gap[:, order:], w_vg[:, :order]
        own = w_h[...] - if_right(dot(w_v, g_right))
        from_right = if_right(dot(tg_gap[:, :order], own.astype(BF16))).astype(BF16)

        def whole(start, gap, further):
            gap_part = if_right(dot(gap[...], g_right)) + dot(further, from_right)
            return (start[...] - gap_part).astype(BF16)

        g[...] = whole(n_h, far, v_one[...])
        hand_out(whole(w_n_h, w_far, w_v), whole(p_n_h, p_far, p_v[...]), a, b)

    by_parity(None, odd)


def if_two_left(value):
    return jnp.where(lax.axis_index(AXES) > 1, value, jnp.zeros_like(value))


def if_two_right(value):
    last = lax.axis_size(AXES) - 2
    return jnp.where(lax.axis_index(AXES) < last, value, jnp.zeros_like(value))


def spikes_two_even(order, tg, v_one, near, pair2, w_vg_gap, after, from_left, from_right, scale):
    def even():
        t = tg[:, :order]
        gap = if_left(dot(t, w_vg_gap[:, :order]))
        scale[...] = (near[...].astype(F32) - gap).astype(BF16)
        s_v = dot(scale[...], v_one[...]).astype(BF16)
        from_left[...] = (-dot(scale[...], t)).astype(BF16)
        from_right[...] = dot(s_v, pair2[:order, :]).astype(BF16)

    by_parity(even, None)


def spikes_two_odd(order, tg, v_one, w_b, near, pair1, tg_gap, after, from_left, from_right, scale):
    def odd():
        right = dot(tg_gap[:, :order], w_b[...]).astype(BF16)
        gap = if_right(dot(v_one[...], right))
        scale[...] = (near[...].astype(F32) - gap).astype(BF16)
        s_t = dot(scale[...], tg[:, :order]).astype(BF16)
        from_left[...] = dot(s_t, pair1[:order, :]).astype(BF16)
        from_right[...] = dot(scale[...], v_one[...]).astype(BF16)

    by_parity(None, odd)


def top_value(g, from_left, from_right, a, b, x):
    def top(left, right):
        rows = g.shape[0]
        change = if_two_left(dot(from_left[...], left[:rows, :]))
        change += if_two_right(dot(from_right[...], right[:rows, :]))
        x[...] = (g[...].astype(F32) + change).astype(BF16)

    left_of_two = lax.rem(lax.axis_index(AXES), 4) < 2
    pl.when(left_of_two)(lambda: top(b, a))
    pl.when(jnp.logical_not(left_of_two))(lambda: top(a, b))


def top_even(g, from_left, from_right, a, b, x, x_out):
    def even():
        top_value(g, from_left, from_right, a, b, x)
        hand_over(x, x_out)

    by_parity(even, None)


def top_odd(g, from_left, from_right, a, b, x):
    by_parity(None, lambda: top_value(g, from_left, from_right, a, b, x))


def start_second(order, vg_b, w_b, x_even, x_odd, rest):
    def start(x):
        rest[...] = vg_b[:, order:].astype(F32) - dot(w_b[...], x[...])

    by_parity(lambda: start(x_even), lambda: start(x_odd))


def write_rows(order, vg_b, x, rest, x_next, right_on, out, rows, sem):
    rows[0] = x[...]
    rows[1] = (rest[...] - right_on(dot(vg_b[:, :order], x_next[:order, :]))).astype(BF16)
    copy = pltpu.make_async_copy(rows, out, sem)
    copy.start()
    copy.wait()


def finish_odd(order, vg_b, x, rest, x_gap, out, rows, sem):
    by_parity(None, lambda: write_rows(order, vg_b, x, rest, x_gap, if_right, out, rows, sem))


def finish_even(order, made, vg_b, x, rest, x_pair, out, rows, sem):
    by_parity(lambda: write_rows(order, vg_b, x, rest, x_pair, same, out, rows, sem), None)


def exchanges(slab, count):
    pairs = [(i, i ^ 1) for i in range(count)]
    twos, other_twos = [], []
    for parity in (0, 1):
        over = [i ^ slab for i in range(count)]
        twos.append([(i, i ^ 2 if i % 2 == parity else over[i]) for i in range(count)])
        to = [((i - 2) ^ 2) + 2 if i % 2 == parity else over[i] for i in range(count)]
        for end in (parity, count - 2 + parity):
            to[end], to[end ^ 1], to[over[end ^ 1]] = end ^ 1, over[end ^ 1], end
        other_twos.append(list(enumerate(to)))
    after = [(i + 1) % count for i in range(count)]
    after[2], after[slab + 2], after[count - 1] = 0, 3, count - 5
    for first in range(slab + 3, count - 5, 4):
        after[first + 3] = first
    to_right = list(enumerate(after))
    to_left = [(count - 1 - i, count - 1 - j) for i, j in to_right]
    return pairs, twos, other_twos, to_right, to_left


def body(diag, lower, upper, right):
    order, rhs = diag.shape[1], right.shape[2]
    count = lax.axis_size(AXES)
    pairs, twos, other_twos, to_right, to_left = exchanges(lax.axis_size("dev"), count)

    def sent(block, route):
        return lax.ppermute(block, AXES, route)

    part = functools.partial
    square = 2 * order**3
    thin = 2 * order * order * rhs
    block = pltpu.VMEM((order, order), BF16)
    side = pltpu.VMEM((order, rhs), BF16)
    wide = bf16_array(order, order + rhs)
    full = bf16_array(order, order)
    slim = bf16_array(order, rhs)

    row_scratch = (pltpu.VMEM((order, order + rhs), BF16), pltpu.SemaphoreType.DMA((4,)))
    vg_odd, diag_b, lower_b = local_call(
        part(second_row_odd, order),
        [wide, full, full], [diag, upper, right, lower], square + thin, 4, row_scratch,
    )
    vg_gap = sent(vg_odd, to_right)
    own_arrays = [f32_array(order, rhs)] + [full] * 3
    spike_arrays = [full, full, f32_array(order, order), full]
    own_scratch = (block, side, pltpu.SemaphoreType.DMA((6,)))
    spikes = local_call(
        part(own_products_odd, order),
        spike_arrays + own_arrays, [diag, lower, upper, right, vg_odd, diag_b, lower_b],
        5 * square + 2 * thin, 4, own_scratch,
    )
    spikes, own = spikes[:4], [*spikes[4:], diag_b, lower_b]
    cut = 3 * order // 4
    vg_b, *to_pair = local_call(
        part(second_row, order),
        [wide, bf16_array(order, cut), bf16_array(order, order - cut + rhs)],
        [diag, upper, right, vg_odd, own[0]], square + thin, 3, (block, *row_scratch),
    )
    vg_pair = [sent(piece, pairs) for piece in to_pair]
    r, v_a, *held = local_call(
        part(own_products_even, order),
        own_arrays + [full] * 2, [diag, lower, upper, right, vg_b, *own], square + 2 * thin,
        4, own_scratch, {5 + i: i for i in range(6)},
    )
    w_a, w_b, m, n = spikes
    shares = [bf16_array(order + rows, order) for rows in (rhs // 2, rhs // 2, 0)]
    tg_odd, v_odd, w_vg_odd, *to_pair = local_call(
        part(level_one_odd, order),
        [wide, full, wide, *shares], [w_a, m, r, *vg_pair, n, w_b], 5 * square, 0, (block, block),
    )
    w_vg_gap = sent(w_vg_odd, to_right)
    w_a, w_b, m, n = local_call(
        part(spikes_own_even, order),
        spike_arrays, [vg_b, *held, v_a, vg_gap, *spikes], 4 * square,
        aliases={7 + i: i for i in range(4)},
    )
    tg, scale = local_call(
        part(scale_one_even, order),
        [wide, full], [w_a, m, r, vg_gap, tg_odd], 2 * square + 2 * thin, aliases={4: 0},
    )
    tg, v_one, *to_pair = local_call(
        part(spikes_one_even, order),
        [wide, full, *shares], [scale, n, w_b, tg, v_odd, *to_pair], 3 * square + thin,
        0, (block, block, side), {3: 0, 4: 1, 5: 2, 6: 3, 7: 4},
    )
    tg_gap = sent(tg, to_left)
    pair = [sent(piece, pairs) for piece in to_pair]

    tall, tall_slim = f32_array(order, rhs), bf16_array(order + 16, rhs)
    near_even, n_h_even = local_call(
        part(pair_part_even, order), [full, tall], [tg, v_one, w_b, *pair[:2]], 2 * square + thin
    )
    near, far, w_far, p_far, p_v, n_h, w_h, w_n_h, p_n_h = local_call(
        part(pair_part_odd, order),
        [full] * 5 + [tall] * 4, [tg, v_one, w_b, *pair], 5 * square + 5 * thin,
    )
    g_even, a_even, b_even = local_call(
        part(level_two_even, order),
        [slim] * 3, [tg, w_b, near_even, n_h_even, pair[1], w_vg_gap], 6 * thin,
    )
    even_a, even_b = sent(a_even, twos[0]), sent(b_even, other_twos[0])
    left_even, right_even = local_call(
        part(spikes_two_even, order),
        [full, full], [tg, v_one, near_even, pair[2], w_vg_gap, a_even], 4 * square, 0, (block,),
    )
    g_odd, a_odd, b_odd = local_call(
        part(level_two_odd, order),
        [slim, tall_slim, slim],
        [v_one, w_vg_odd, far, w_far, p_far, p_v, n_h, w_h, w_n_h, p_n_h, tg_gap, left_even], 8 * thin,
    )
    odd_a, odd_b = sent(a_odd, twos[1]), sent(b_odd, other_twos[1])
    left_odd, right_odd = local_call(
        part(spikes_two_odd, order),
        [full, full], [tg, v_one, w_b, near, pair[1], tg_gap, a_odd], 5 * square, 0, (block,),
    )
    x_even, x_out = local_call(
        top_even, [slim, tall_slim], [g_even, left_even, right_even, even_a, even_b], 2 * thin
    )
    x_gap = sent(x_out, to_left)
    x_odd = local_call(top_odd, [slim], [g_odd, left_odd, right_odd, odd_a, odd_b], 2 * thin)
    x_pair = sent(x_odd, pairs)
    rest = local_call(part(start_second, order), [tall], [vg_b, w_b, x_even, x_odd], thin)
    values = jax.ShapeDtypeStruct((2, order, rhs), BF16)
    scratch = (pltpu.VMEM(values.shape, BF16), pltpu.SemaphoreType.DMA)
    made = local_call(
        part(finish_odd, order),
        [values], [vg_b, x_odd, rest, x_gap], thin, 0, scratch, out_in_hbm=True,
    )
    return local_call(
        part(finish_even, order),
        [values], [made, vg_b, x_even, rest, x_pair], thin, 1, scratch, {0: 0}, out_in_hbm=True,
    )


def solution(mesh):
    split = P(AXES, None, None)
    return jax.shard_map(
        body, mesh=mesh, in_specs=(split,) * 4, out_specs=split, check_vma=False
    )
```

```python
import functools

import jax
import jax.numpy as jnp
from jax import lax
from jax.experimental import pallas as pl
from jax.experimental.pallas import tpu as pltpu
from jax.sharding import PartitionSpec as P


AXES = ("grp", "dev")
BF16 = jnp.bfloat16
F32 = jnp.float32
VMEM_BYTES = 12 * 1024 * 1024


def is_odd():
    return lax.rem(lax.axis_index(AXES), 2) == 1


def if_left(value):
    return jnp.where(lax.axis_index(AXES) > 0, value, jnp.zeros_like(value))


def if_right(value):
    last = lax.axis_size(AXES) - 1
    return jnp.where(lax.axis_index(AXES) < last, value, jnp.zeros_like(value))


def dot(a, b):
    return jnp.dot(a, b, preferred_element_type=F32)


def by_parity(even, odd):
    odd_here = is_odd()
    if odd is not None:
        pl.when(odd_here)(odd)
    if even is not None:
        pl.when(jnp.logical_not(odd_here))(even)


def identity(order):
    rows = lax.broadcasted_iota(jnp.int32, (order, order), 0)
    return (rows == lax.broadcasted_iota(jnp.int32, (order, order), 1)).astype(F32)


def local_call(
    kernel, outs, ins, flops, in_hbm=0, scratch=(), aliases=None, out_in_hbm=False
):
    vmem = pl.BlockSpec(memory_space=pltpu.VMEM)
    hbm = pl.BlockSpec(memory_space=pl.ANY)
    many = len(outs) > 1
    ins = [pltpu.with_memory_space_constraint(x, pltpu.HBM) for x in ins[:in_hbm]] + ins[in_hbm:]
    return pl.pallas_call(
        kernel,
        out_shape=outs if many else outs[0],
        in_specs=[hbm] * in_hbm + [vmem] * (len(ins) - in_hbm),
        out_specs=[vmem] * len(outs) if many else pl.BlockSpec(memory_space=pltpu.HBM) if out_in_hbm else vmem,
        scratch_shapes=list(scratch),
        input_output_aliases=aliases or {},
        compiler_params=pltpu.CompilerParams(vmem_limit_bytes=VMEM_BYTES),
        cost_estimate=pl.CostEstimate(flops=flops // 1000, bytes_accessed=0, transcendentals=0),
    )(*ins)


def bf16_array(rows, columns):
    return jax.ShapeDtypeStruct((rows, columns), BF16)


def f32_array(rows, columns):
    return jax.ShapeDtypeStruct((rows, columns), F32)


def fetch(source, target, sem):
    copy = pltpu.make_async_copy(source, target, sem)
    copy.start()
    return copy


def load_row(order, diag, upper, right, vg, diag_b, sides, sems, later=()):
    copies = [
        fetch(diag.at[1], diag_b, sems.at[0]),
        fetch(upper.at[1], sides.at[:, :order], sems.at[1]),
        fetch(right.at[1], sides.at[:, order:], sems.at[2]),
    ]
    for copy in later:
        copy.start()
    for copy in copies:
        copy.wait()
    vg[...] = dot(diag_b[...], sides[...]).astype(BF16)


def second_row_odd(order, diag, upper, right, lower, vg, diag_b, lower_b, sides, sems):
    def odd():
        later = pltpu.make_async_copy(lower.at[1], lower_b, sems.at[3])
        load_row(order, diag, upper, right, vg, diag_b, sides, sems, [later])
        later.wait()

    by_parity(None, odd)


def second_row(order, diag, upper, right, vg_odd, after, vg_b, *rest):
    *pieces, diag_b, sides, sems = rest

    def odd():
        vg_b[...] = vg_odd[...]

    def even():
        load_row(order, diag, upper, right, vg_b, diag_b, sides, sems)
        first = 0
        for piece in pieces:
            piece[...] = vg_b[:, first : first + piece.shape[1]]
            first += piece.shape[1]

    by_parity(even, odd)


def own_products_odd(
    order, diag, lower, upper, right, vg_odd, diag_b, lower_b,
    w_a, w_b, m, n, r, v_a, diag_a, lower_a, upper_a, right_a, sems,
):
    def odd():
        copies = first_row_copies(diag, lower, upper, right, diag_a, lower_a, upper_a, right_a, sems)
        for copy in copies:
            copy.start()
        w_b[...] = dot(diag_b[...], lower_b[...]).astype(BF16)
        first_right_side(order, copies, vg_odd, diag_a, upper_a, right_a, v_a, r)
        first_spikes(order, vg_odd, diag_a, lower_a, v_a, w_a, w_b, m, n)

    by_parity(None, odd)


def own_products_even(order, diag, lower, upper, right, vg_b, *rest):
    r, v_a, diag_a, lower_a, diag_b, lower_b, upper_a, right_a, sems = rest[6:]

    def even():
        copies = first_row_copies(diag, lower, upper, right, diag_a, lower_a, upper_a, right_a, sems)
        copies += [
            pltpu.make_async_copy(diag.at[1], diag_b, sems.at[4]),
            pltpu.make_async_copy(lower.at[1], lower_b, sems.at[5]),
        ]
        for copy in copies:
            copy.start()
        first_right_side(order, copies, vg_b, diag_a, upper_a, right_a, v_a, r)

    by_parity(even, None)


def spikes_own_even(order, vg_b, diag_a, lower_a, diag_b, lower_b, v_a, after, *rest):
    w_a, w_b, m, n = rest[4:]

    def even():
        w_b[...] = dot(diag_b[...], lower_b[...]).astype(BF16)
        first_spikes(order, vg_b, diag_a, lower_a, v_a, w_a, w_b, m, n)

    by_parity(even, None)


def first_row_copies(diag, lower, upper, right, diag_a, lower_a, upper_a, right_a, sems):
    pairs = (diag, diag_a), (upper, upper_a), (right, right_a), (lower, lower_a)
    return [pltpu.make_async_copy(x.at[0], y, sems.at[i]) for i, (x, y) in enumerate(pairs)]


def first_right_side(order, copies, vg_b, diag_a, upper_a, right_a, v_a, r):
    for copy in copies[:3]:
        copy.wait()
    v_a[...] = dot(diag_a[...], upper_a[...]).astype(BF16)
    g_a = dot(diag_a[...], right_a[...]).astype(BF16)
    r[...] = g_a.astype(F32) - dot(v_a[...], vg_b[:, order:])
    for copy in copies[3:]:
        copy.wait()


def first_spikes(order, vg_b, diag_a, lower_a, v_a, w_a, w_b, m, n):
    w_a[...] = dot(diag_a[...], lower_a[...]).astype(BF16)
    n[...] = dot(v_a[...], vg_b[:, :order]).astype(BF16)
    m[...] = dot(v_a[...], w_b[...])


def scale_one(order, w_a, m, r, v_left, g_left, scale, tg):
    first = 0
    eye = identity(order)
    for piece in v_left:
        at = slice(first, first + piece.shape[1])
        coupling = if_left(dot(w_a[...], piece[...])) + m[:, at]
        scale[:, at] = (eye[:, at] + coupling).astype(BF16)
        first = at.stop
    rest = (r[...] - if_left(dot(w_a[...], g_left[...]))).astype(BF16)
    tg[:, :order] = dot(scale[...], w_a[...]).astype(BF16)
    tg[:, order:] = dot(scale[...], rest).astype(BF16)


def spikes_one(order, scale, n, w_b, tg, v_one, w_t, w_v, w_g):
    v_one[...] = (-dot(scale[...], n[...])).astype(BF16)
    w_v[...] = dot(w_b[...], v_one[...]).astype(BF16)
    w_g[...] = dot(w_b[...], tg[:, order:]).astype(BF16)
    w_t[...] = dot(w_b[...], tg[:, :order]).astype(BF16)


def pack(side):
    columns = side.shape[1]
    return jnp.concatenate(
        [side[i : i + columns] for i in range(0, side.shape[0], columns)], axis=1
    )


def unpack(rows, columns):
    return jnp.concatenate(
        [rows[:, i : i + columns] for i in range(0, rows.shape[1], columns)], axis=0
    )


def hand_to_pair(order, blocks, side, to_pair):
    rows, first = pack(side), 0
    for block, piece in zip(blocks, to_pair):
        last = first + piece.shape[0] - order
        piece[:order, :] = block
        if last > first:
            piece[order:, :] = rows[first:last]
        first = last


def side_of_pair(order, got, columns):
    return unpack(jnp.concatenate([piece[order:, :] for piece in got], axis=0), columns)


def level_one_odd(order, w_a, m, r, v0, vg1, n, w_b, tg, v_one, w_vg, *rest):
    *to_pair, scale, w_t = rest
    columns = order - v0.shape[1]

    def odd():
        v_left, g_left = [v0, vg1.at[:, :columns]], vg1.at[:, columns:]
        scale_one(order, w_a, m, r, v_left, g_left, scale, tg)
        w_v, w_g = w_vg.at[:, :order], w_vg.at[:, order:]
        spikes_one(order, scale, n, w_b, tg, v_one, w_t, w_v, w_g)
        hand_to_pair(order, [tg[:, :order], w_t[...], v_one[...]], tg[:, order:], to_pair)

    by_parity(None, odd)


def scale_one_even(order, w_a, m, r, vg, tg_odd, tg, scale):
    v_left, g_left = [vg.at[:, :order]], vg.at[:, order:]
    by_parity(lambda: scale_one(order, w_a, m, r, v_left, g_left, scale, tg), None)


def spikes_one_even(order, scale, n, w_b, tg, v_odd, pair0, pair1, pair2, tg_out, v_one, *rest):
    *to_pair, w_t, w_v, w_g = rest

    def even():
        spikes_one(order, scale, n, w_b, tg, v_one, w_t, w_v, w_g)
        hand_to_pair(order, [w_v[...], w_t[...], v_one[...]], w_g[...], to_pair)

    by_parity(even, None)


def same(value):
    return value


def pair_part_even(order, tg, v_one, w_b, pair0, pair1, near, n_h):
    def even():
        right = dot(pair0[:order, :], w_b[...]).astype(BF16)
        near[...] = (identity(order) - dot(v_one[...], right)).astype(BF16)
        side = side_of_pair(order, [pair0, pair1], n_h.shape[1])
        n_h[...] = tg[:, order:].astype(F32) - dot(v_one[...], side)

    by_parity(even, None)


def pair_part_odd(
    order, tg, v_one, w_b, pair0, pair1, pair2, near, far, w_far, p_far, p_v, n_h, w_h, w_n_h, p_n_h
):
    def odd():
        t, v_pair = tg[:, :order], pair2[...]
        near[...] = (identity(order) - dot(t, pair0[:order, :])).astype(BF16)
        far[...] = dot(near[...], v_one[...]).astype(BF16)
        w_far[...] = dot(w_b[...], far[...]).astype(BF16)
        p_far[...] = dot(v_pair, far[...]).astype(BF16)
        p_v[...] = dot(v_pair, v_one[...]).astype(BF16)
        side = side_of_pair(order, [pair0, pair1], n_h.shape[1])
        own = (tg[:, order:].astype(F32) + dot(t, side)).astype(BF16)
        scaled = dot(near[...], own)
        n_h[...] = scaled
        w_h[...] = dot(w_b[...], own)
        w_n_h[...] = dot(w_b[...], scaled.astype(BF16))
        p_n_h[...] = dot(v_pair, scaled.astype(BF16))

    by_parity(None, odd)


def hand_over(block, out):
    rows = block.shape[0]
    out[:rows, :] = block[...]
    if out.shape[0] > rows:
        out[rows:, :] = jnp.zeros((out.shape[0] - rows, out.shape[1]), BF16)


def hand_out(right, left, a, b):
    left_of_two = lax.rem(lax.axis_index(AXES), 4) < 2
    hand_over(jnp.where(left_of_two, right, left), a)
    b[...] = jnp.where(left_of_two, left, right)


def level_two_even(order, tg, w_b, near, n_h, pair1, w_vg_gap, g, a, b):
    def even():
        t = tg[:, :order]
        whole = (n_h[...] + if_left(dot(t, w_vg_gap[:, order:]))).astype(BF16)
        from_left = if_left(dot(w_vg_gap[:, :order], whole)).astype(BF16)
        value = (dot(near[...], whole) - dot(t, from_left)).astype(BF16)
        onward = (-dot(pair1[:order, :], dot(w_b[...], value).astype(BF16))).astype(BF16)
        g[...] = value
        hand_out(onward, value, a, b)

    by_parity(even, None)


def less_gap(start, gap, g_right, further, from_right):
    return (start[...] - if_right(dot(gap[...], g_right)) - dot(further, from_right)).astype(BF16)


def level_two_odd(
    order, w_vg, w_far, p_far, p_v, w_h, w_n_h, p_n_h, tg_gap, after, from_right, a, b
):
    def odd():
        g_right, w_v = tg_gap[:, order:], w_vg[:, :order]
        own = (w_h[...] - if_right(dot(w_v, g_right))).astype(BF16)
        gap = if_right(dot(tg_gap[:, :order], own)).astype(BF16)
        from_right[...] = gap
        to_right = less_gap(w_n_h, w_far, g_right, w_v, gap)
        hand_out(to_right, less_gap(p_n_h, p_far, g_right, p_v[...], gap), a, b)

    by_parity(None, odd)


def if_two_left(value):
    return jnp.where(lax.axis_index(AXES) > 1, value, jnp.zeros_like(value))


def if_two_right(value):
    last = lax.axis_size(AXES) - 2
    return jnp.where(lax.axis_index(AXES) < last, value, jnp.zeros_like(value))


def spikes_two_even(order, tg, v_one, near, pair2, w_vg_gap, after, from_left, from_right, scale):
    def even():
        t = tg[:, :order]
        gap = if_left(dot(t, w_vg_gap[:, :order]))
        scale[...] = (near[...].astype(F32) - gap).astype(BF16)
        s_v = dot(scale[...], v_one[...]).astype(BF16)
        from_left[...] = (-dot(scale[...], t)).astype(BF16)
        from_right[...] = dot(s_v, pair2[:order, :]).astype(BF16)

    by_parity(even, None)


def spikes_two_odd(
    order, tg, v_one, w_b, near, far, n_h, pair1, tg_gap, from_right, after, g, left, right, scale
):
    def odd():
        g[...] = less_gap(n_h, far, tg_gap[:, order:], v_one[...], from_right[...])
        through = dot(tg_gap[:, :order], w_b[...]).astype(BF16)
        gap = if_right(dot(v_one[...], through))
        scale[...] = (near[...].astype(F32) - gap).astype(BF16)
        s_t = dot(scale[...], tg[:, :order]).astype(BF16)
        left[...] = dot(s_t, pair1[:order, :]).astype(BF16)
        right[...] = dot(scale[...], v_one[...]).astype(BF16)

    by_parity(None, odd)


def top_value(g, from_left, from_right, a, b, x):
    def top(left, right):
        rows = g.shape[0]
        change = if_two_left(dot(from_left[...], left[:rows, :]))
        change += if_two_right(dot(from_right[...], right[:rows, :]))
        x[...] = (g[...].astype(F32) + change).astype(BF16)

    left_of_two = lax.rem(lax.axis_index(AXES), 4) < 2
    pl.when(left_of_two)(lambda: top(b, a))
    pl.when(jnp.logical_not(left_of_two))(lambda: top(a, b))


def top_even(g, from_left, from_right, a, b, x, x_out):
    def even():
        top_value(g, from_left, from_right, a, b, x)
        hand_over(x, x_out)

    by_parity(even, None)


def top_odd(g, from_left, from_right, a, b, x):
    by_parity(None, lambda: top_value(g, from_left, from_right, a, b, x))


def start_second(order, vg_b, w_b, x_even, x_odd, rest):
    def start(x):
        rest[...] = vg_b[:, order:].astype(F32) - dot(w_b[...], x[...])

    by_parity(lambda: start(x_even), lambda: start(x_odd))


def write_rows(order, vg_b, x, rest, x_next, right_on, out, rows, sems):
    rows[0] = x[...]
    copies = [fetch(rows.at[0], out.at[0], sems.at[0])]
    half = order // 2
    for k in range(2):
        at = pl.ds(k * half, half)
        next_part = right_on(dot(vg_b[at, :order], x_next[:order, :]))
        rows[1, at] = (rest[at, :] - next_part).astype(BF16)
        copies.append(fetch(rows.at[1, at], out.at[1, at], sems.at[k + 1]))
    for copy in copies:
        copy.wait()


def finish_odd(order, vg_b, x, rest, x_gap, out, rows, sems):
    by_parity(None, lambda: write_rows(order, vg_b, x, rest, x_gap, if_right, out, rows, sems))


def finish_even(order, made, vg_b, x, rest, x_pair, out, rows, sems):
    by_parity(lambda: write_rows(order, vg_b, x, rest, x_pair, same, out, rows, sems), None)


def exchanges(slab, count):
    pairs = [(i, i ^ 1) for i in range(count)]
    twos, other_twos = [], []
    for parity in (0, 1):
        over = [i ^ slab for i in range(count)]
        twos.append([(i, i ^ 2 if i % 2 == parity else over[i]) for i in range(count)])
        to = [((i - 2) ^ 2) + 2 if i % 2 == parity else over[i] for i in range(count)]
        for end in (parity, count - 2 + parity):
            to[end], to[end ^ 1], to[over[end ^ 1]] = end ^ 1, over[end ^ 1], end
        other_twos.append(list(enumerate(to)))
    after = [(i + 1) % count for i in range(count)]
    after[2], after[slab + 2], after[count - 1] = 0, 3, count - 5
    for first in range(slab + 3, count - 5, 4):
        after[first + 3] = first
    to_right = list(enumerate(after))
    to_left = [(count - 1 - i, count - 1 - j) for i, j in to_right]
    return pairs, twos, other_twos, to_right, to_left


def body(diag, lower, upper, right):
    order, rhs = diag.shape[1], right.shape[2]
    count = lax.axis_size(AXES)
    pairs, twos, other_twos, to_right, to_left = exchanges(lax.axis_size("dev"), count)

    def sent(block, route):
        return lax.ppermute(block, AXES, route)

    part = functools.partial
    square = 2 * order**3
    thin = 2 * order * order * rhs
    block = pltpu.VMEM((order, order), BF16)
    side = pltpu.VMEM((order, rhs), BF16)
    wide = bf16_array(order, order + rhs)
    full = bf16_array(order, order)
    slim = bf16_array(order, rhs)

    row_scratch = (pltpu.VMEM((order, order + rhs), BF16), pltpu.SemaphoreType.DMA((4,)))
    vg_odd, diag_b, lower_b = local_call(
        part(second_row_odd, order),
        [wide, full, full], [diag, upper, right, lower], square + thin, 4, row_scratch,
    )
    vg_gap = sent(vg_odd, to_right)
    own_arrays = [f32_array(order, rhs)] + [full] * 3
    spike_arrays = [full, full, f32_array(order, order), full]
    own_scratch = (block, side, pltpu.SemaphoreType.DMA((6,)))
    spikes = local_call(
        part(own_products_odd, order),
        spike_arrays + own_arrays, [diag, lower, upper, right, vg_odd, diag_b, lower_b],
        5 * square + 2 * thin, 4, own_scratch,
    )
    spikes, own = spikes[:4], [*spikes[4:], diag_b, lower_b]
    cut = 3 * order // 4
    vg_b, *to_pair = local_call(
        part(second_row, order),
        [wide, bf16_array(order, cut), bf16_array(order, order - cut + rhs)],
        [diag, upper, right, vg_odd, own[0]], square + thin, 3, (block, *row_scratch),
    )
    vg_pair = [sent(piece, pairs) for piece in to_pair]
    r, v_a, *held = local_call(
        part(own_products_even, order),
        own_arrays + [full] * 2, [diag, lower, upper, right, vg_b, *own], square + 2 * thin,
        4, own_scratch, {5 + i: i for i in range(6)},
    )
    w_a, w_b, m, n = spikes
    shares = [bf16_array(order + rows, order) for rows in (rhs // 2, rhs // 2, 0)]
    tg_odd, v_odd, w_vg_odd, *to_pair = local_call(
        part(level_one_odd, order),
        [wide, full, wide, *shares], [w_a, m, r, *vg_pair, n, w_b], 5 * square, 0, (block, block),
    )
    w_vg_gap = sent(w_vg_odd, to_right)
    w_a, w_b, m, n = local_call(
        part(spikes_own_even, order),
        spike_arrays, [vg_b, *held, v_a, vg_gap, *spikes], 4 * square,
        aliases={7 + i: i for i in range(4)},
    )
    tg, scale = local_call(
        part(scale_one_even, order),
        [wide, full], [w_a, m, r, vg_gap, tg_odd], 2 * square + 2 * thin, aliases={4: 0},
    )
    tg, v_one, *to_pair = local_call(
        part(spikes_one_even, order),
        [wide, full, *shares], [scale, n, w_b, tg, v_odd, *to_pair], 3 * square + thin,
        0, (block, block, side), {3: 0, 4: 1, 5: 2, 6: 3, 7: 4},
    )
    tg_gap = sent(tg, to_left)
    pair = [sent(piece, pairs) for piece in to_pair]

    tall, tall_slim = f32_array(order, rhs), bf16_array(order + 16, rhs)
    near_even, n_h_even = local_call(
        part(pair_part_even, order), [full, tall], [tg, v_one, w_b, *pair[:2]], 2 * square + thin
    )
    near, far, w_far, p_far, p_v, n_h, w_h, w_n_h, p_n_h = local_call(
        part(pair_part_odd, order),
        [full] * 5 + [tall] * 4, [tg, v_one, w_b, *pair], 5 * square + 5 * thin,
    )
    g_even, a_even, b_even = local_call(
        part(level_two_even, order),
        [slim] * 3, [tg, w_b, near_even, n_h_even, pair[1], w_vg_gap], 6 * thin,
    )
    even_a, even_b = sent(a_even, twos[0]), sent(b_even, other_twos[0])
    left_even, right_even = local_call(
        part(spikes_two_even, order),
        [full, full], [tg, v_one, near_even, pair[2], w_vg_gap, a_even], 4 * square, 0, (block,),
    )
    from_right, a_odd, b_odd = local_call(
        part(level_two_odd, order),
        [slim, tall_slim, slim],
        [w_vg_odd, w_far, p_far, p_v, w_h, w_n_h, p_n_h, tg_gap, left_even], 6 * thin,
    )
    odd_a, odd_b = sent(a_odd, twos[1]), sent(b_odd, other_twos[1])
    g_odd, left_odd, right_odd = local_call(
        part(spikes_two_odd, order),
        [slim, full, full],
        [tg, v_one, w_b, near, far, n_h, pair[1], tg_gap, from_right, a_odd], 5 * square, 0, (block,),
    )
    x_even, x_out = local_call(
        top_even, [slim, tall_slim], [g_even, left_even, right_even, even_a, even_b], 2 * thin
    )
    x_gap = sent(x_out, to_left)
    x_odd = local_call(top_odd, [slim], [g_odd, left_odd, right_odd, odd_a, odd_b], 2 * thin)
    x_pair = sent(x_odd, pairs)
    rest = local_call(part(start_second, order), [tall], [vg_b, w_b, x_even, x_odd], thin)
    values = jax.ShapeDtypeStruct((2, order, rhs), BF16)
    scratch = (pltpu.VMEM(values.shape, BF16), pltpu.SemaphoreType.DMA((3,)))
    made = local_call(
        part(finish_odd, order),
        [values], [vg_b, x_odd, rest, x_gap], thin, 0, scratch, out_in_hbm=True,
    )
    return local_call(
        part(finish_even, order),
        [values], [made, vg_b, x_even, rest, x_pair], thin, 1, scratch, {0: 0}, out_in_hbm=True,
    )


def solution(mesh):
    split = P(AXES, None, None)
    return jax.shard_map(
        body, mesh=mesh, in_specs=(split,) * 4, out_specs=split, check_vma=False
    )
```

```python
import functools

import jax
import jax.numpy as jnp
from jax import lax
from jax.experimental import pallas as pl
from jax.experimental.pallas import tpu as pltpu
from jax.sharding import PartitionSpec as P


AXES = ("grp", "dev")
BF16 = jnp.bfloat16
F32 = jnp.float32
VMEM_BYTES = 12 * 1024 * 1024


def is_odd():
    return lax.rem(lax.axis_index(AXES), 2) == 1


def if_left(value):
    return jnp.where(lax.axis_index(AXES) > 0, value, jnp.zeros_like(value))


def if_right(value):
    last = lax.axis_size(AXES) - 1
    return jnp.where(lax.axis_index(AXES) < last, value, jnp.zeros_like(value))


def dot(a, b):
    return jnp.dot(a, b, preferred_element_type=F32)


def by_parity(even, odd):
    odd_here = is_odd()
    if odd is not None:
        pl.when(odd_here)(odd)
    if even is not None:
        pl.when(jnp.logical_not(odd_here))(even)


def identity(order):
    rows = lax.broadcasted_iota(jnp.int32, (order, order), 0)
    return (rows == lax.broadcasted_iota(jnp.int32, (order, order), 1)).astype(F32)


def local_call(
    kernel, outs, ins, flops, in_hbm=0, scratch=(), aliases=None, out_in_hbm=False
):
    vmem = pl.BlockSpec(memory_space=pltpu.VMEM)
    hbm = pl.BlockSpec(memory_space=pl.ANY)
    many = len(outs) > 1
    places = [vmem] * len(outs)
    if out_in_hbm:
        places[-1] = pl.BlockSpec(memory_space=pltpu.HBM)
    ins = [pltpu.with_memory_space_constraint(x, pltpu.HBM) for x in ins[:in_hbm]] + ins[in_hbm:]
    return pl.pallas_call(
        kernel,
        out_shape=outs if many else outs[0],
        in_specs=[hbm] * in_hbm + [vmem] * (len(ins) - in_hbm),
        out_specs=places if many else places[0],
        scratch_shapes=list(scratch),
        input_output_aliases=aliases or {},
        compiler_params=pltpu.CompilerParams(vmem_limit_bytes=VMEM_BYTES),
        cost_estimate=pl.CostEstimate(flops=flops // 1000, bytes_accessed=0, transcendentals=0),
    )(*ins)


def bf16_array(rows, columns):
    return jax.ShapeDtypeStruct((rows, columns), BF16)


def f32_array(rows, columns):
    return jax.ShapeDtypeStruct((rows, columns), F32)


def fetch(source, target, sem):
    copy = pltpu.make_async_copy(source, target, sem)
    copy.start()
    return copy


def load_row(order, diag, upper, right, vg, diag_b, sides, sems, later=()):
    copies = [
        fetch(diag.at[1], diag_b, sems.at[0]),
        fetch(upper.at[1], sides.at[:, :order], sems.at[1]),
        fetch(right.at[1], sides.at[:, order:], sems.at[2]),
    ]
    for copy in later:
        copy.start()
    for copy in copies:
        copy.wait()
    vg[...] = dot(diag_b[...], sides[...]).astype(BF16)


def second_row_odd(order, diag, upper, right, lower, vg, diag_b, lower_b, sides, sems):
    def odd():
        later = pltpu.make_async_copy(lower.at[1], lower_b, sems.at[3])
        load_row(order, diag, upper, right, vg, diag_b, sides, sems, [later])
        later.wait()

    by_parity(None, odd)


def second_row(order, diag, upper, right, vg_odd, after, vg_b, *rest):
    *pieces, diag_b, sides, sems = rest

    def odd():
        vg_b[...] = vg_odd[...]

    def even():
        load_row(order, diag, upper, right, vg_b, diag_b, sides, sems)
        first = 0
        for piece in pieces:
            piece[...] = vg_b[:, first : first + piece.shape[1]]
            first += piece.shape[1]

    by_parity(even, odd)


def own_products_odd(
    order, diag, lower, upper, right, vg_odd, diag_b, lower_b,
    w_a, w_b, m, n, r, v_a, diag_a, lower_a, upper_a, right_a, sems,
):
    def odd():
        copies = first_row_copies(diag, lower, upper, right, diag_a, lower_a, upper_a, right_a, sems)
        for copy in copies:
            copy.start()
        w_b[...] = dot(diag_b[...], lower_b[...]).astype(BF16)
        first_right_side(order, copies, vg_odd, diag_a, upper_a, right_a, v_a, r)
        first_spikes(order, vg_odd, diag_a, lower_a, v_a, w_a, w_b, m, n)

    by_parity(None, odd)


def own_products_even(order, diag, lower, upper, right, vg_b, *rest):
    r, v_a, diag_a, lower_a, diag_b, lower_b, upper_a, right_a, sems = rest[6:]

    def even():
        copies = first_row_copies(diag, lower, upper, right, diag_a, lower_a, upper_a, right_a, sems)
        copies += [
            pltpu.make_async_copy(diag.at[1], diag_b, sems.at[4]),
            pltpu.make_async_copy(lower.at[1], lower_b, sems.at[5]),
        ]
        for copy in copies:
            copy.start()
        first_right_side(order, copies, vg_b, diag_a, upper_a, right_a, v_a, r)

    by_parity(even, None)


def spikes_own_even(order, vg_b, diag_a, lower_a, diag_b, lower_b, v_a, after, *rest):
    w_a, w_b, m, n = rest[4:]

    def even():
        w_b[...] = dot(diag_b[...], lower_b[...]).astype(BF16)
        first_spikes(order, vg_b, diag_a, lower_a, v_a, w_a, w_b, m, n)

    by_parity(even, None)


def first_row_copies(diag, lower, upper, right, diag_a, lower_a, upper_a, right_a, sems):
    pairs = (diag, diag_a), (upper, upper_a), (right, right_a), (lower, lower_a)
    return [pltpu.make_async_copy(x.at[0], y, sems.at[i]) for i, (x, y) in enumerate(pairs)]


def first_right_side(order, copies, vg_b, diag_a, upper_a, right_a, v_a, r):
    for copy in copies[:3]:
        copy.wait()
    v_a[...] = dot(diag_a[...], upper_a[...]).astype(BF16)
    g_a = dot(diag_a[...], right_a[...]).astype(BF16)
    r[...] = g_a.astype(F32) - dot(v_a[...], vg_b[:, order:])
    for copy in copies[3:]:
        copy.wait()


def first_spikes(order, vg_b, diag_a, lower_a, v_a, w_a, w_b, m, n):
    w_a[...] = dot(diag_a[...], lower_a[...]).astype(BF16)
    n[...] = dot(v_a[...], vg_b[:, :order]).astype(BF16)
    m[...] = dot(v_a[...], w_b[...])


def scale_one(order, w_a, m, r, v_left, g_left, scale, tg):
    first = 0
    eye = identity(order)
    for piece in v_left:
        at = slice(first, first + piece.shape[1])
        coupling = if_left(dot(w_a[...], piece[...])) + m[:, at]
        scale[:, at] = (eye[:, at] + coupling).astype(BF16)
        first = at.stop
    rest = (r[...] - if_left(dot(w_a[...], g_left[...]))).astype(BF16)
    tg[:, :order] = dot(scale[...], w_a[...]).astype(BF16)
    tg[:, order:] = dot(scale[...], rest).astype(BF16)


def spikes_one(order, scale, n, w_b, tg, v_one, w_t, w_v, w_g):
    v_one[...] = (-dot(scale[...], n[...])).astype(BF16)
    w_v[...] = dot(w_b[...], v_one[...]).astype(BF16)
    w_g[...] = dot(w_b[...], tg[:, order:]).astype(BF16)
    w_t[...] = dot(w_b[...], tg[:, :order]).astype(BF16)


def pack(side):
    columns = side.shape[1]
    return jnp.concatenate(
        [side[i : i + columns] for i in range(0, side.shape[0], columns)], axis=1
    )


def unpack(rows, columns):
    return jnp.concatenate(
        [rows[:, i : i + columns] for i in range(0, rows.shape[1], columns)], axis=0
    )


def hand_to_pair(order, blocks, side, to_pair):
    rows, first = pack(side), 0
    for block, piece in zip(blocks, to_pair):
        last = first + piece.shape[0] - order
        piece[:order, :] = block
        if last > first:
            piece[order:, :] = rows[first:last]
        first = last


def side_of_pair(order, got, columns):
    return unpack(jnp.concatenate([piece[order:, :] for piece in got], axis=0), columns)


def level_one_odd(order, w_a, m, r, v0, vg1, n, w_b, tg, v_one, w_vg, *rest):
    *to_pair, scale, w_t = rest
    columns = order - v0.shape[1]

    def odd():
        v_left, g_left = [v0, vg1.at[:, :columns]], vg1.at[:, columns:]
        scale_one(order, w_a, m, r, v_left, g_left, scale, tg)
        w_v, w_g = w_vg.at[:, :order], w_vg.at[:, order:]
        spikes_one(order, scale, n, w_b, tg, v_one, w_t, w_v, w_g)
        hand_to_pair(order, [tg[:, :order], w_t[...], v_one[...]], tg[:, order:], to_pair)

    by_parity(None, odd)


def scale_one_even(order, w_a, m, r, vg, tg_odd, tg, scale):
    v_left, g_left = [vg.at[:, :order]], vg.at[:, order:]
    by_parity(lambda: scale_one(order, w_a, m, r, v_left, g_left, scale, tg), None)


def spikes_one_even(order, place, scale, n, w_b, tg, *refs):
    v_one, *to_pair, w_t, w_v, w_g = refs[-7:]

    @pl.when(lax.rem(lax.axis_index(AXES), 4) == place)
    def _():
        spikes_one(order, scale, n, w_b, tg, v_one, w_t, w_v, w_g)
        hand_to_pair(order, [w_v[...], w_t[...], v_one[...]], w_g[...], to_pair)


def same(value):
    return value


def pair_part_even(order, tg, v_one, w_b, pair0, pair1, near, n_h):
    def even():
        right = dot(pair0[:order, :], w_b[...]).astype(BF16)
        near[...] = (identity(order) - dot(v_one[...], right)).astype(BF16)
        side = side_of_pair(order, [pair0, pair1], n_h.shape[1])
        n_h[...] = tg[:, order:].astype(F32) - dot(v_one[...], side)

    by_parity(even, None)


def pair_part_odd(
    order, tg, v_one, w_b, pair0, pair1, pair2, near, far, w_far, p_far, p_v, n_h, w_h, w_n_h, p_n_h
):
    def odd():
        t, v_pair = tg[:, :order], pair2[...]
        near[...] = (identity(order) - dot(t, pair0[:order, :])).astype(BF16)
        far[...] = dot(near[...], v_one[...]).astype(BF16)
        w_far[...] = dot(w_b[...], far[...]).astype(BF16)
        p_far[...] = dot(v_pair, far[...]).astype(BF16)
        p_v[...] = dot(v_pair, v_one[...]).astype(BF16)
        side = side_of_pair(order, [pair0, pair1], n_h.shape[1])
        own = (tg[:, order:].astype(F32) + dot(t, side)).astype(BF16)
        scaled = dot(near[...], own)
        n_h[...] = scaled
        w_h[...] = dot(w_b[...], own)
        w_n_h[...] = dot(w_b[...], scaled.astype(BF16))
        p_n_h[...] = dot(v_pair, scaled.astype(BF16))

    by_parity(None, odd)


def hand_over(block, out):
    rows = block.shape[0]
    out[:rows, :] = block[...]
    if out.shape[0] > rows:
        out[rows:, :] = jnp.zeros((out.shape[0] - rows, out.shape[1]), BF16)


def hand_out(right, left, a, b):
    left_of_two = lax.rem(lax.axis_index(AXES), 4) < 2
    hand_over(jnp.where(left_of_two, right, left), a)
    b[...] = jnp.where(left_of_two, left, right)


def level_two_even(order, tg, w_b, near, n_h, pair1, w_vg_gap, g, a, b):
    def even():
        t = tg[:, :order]
        whole = (n_h[...] + if_left(dot(t, w_vg_gap[:, order:]))).astype(BF16)
        from_left = if_left(dot(w_vg_gap[:, :order], whole)).astype(BF16)
        value = (dot(near[...], whole) - dot(t, from_left)).astype(BF16)
        onward = (-dot(pair1[:order, :], dot(w_b[...], value).astype(BF16))).astype(BF16)
        g[...] = value
        hand_out(onward, value, a, b)

    by_parity(even, None)


def less_gap(start, gap, g_right, further, from_right):
    return (start[...] - if_right(dot(gap[...], g_right)) - dot(further, from_right)).astype(BF16)


def level_two_odd(
    order, w_vg, w_far, p_far, p_v, w_h, w_n_h, p_n_h, tg_gap, after, from_right, a, b
):
    def odd():
        g_right, w_v = tg_gap[:, order:], w_vg[:, :order]
        own = (w_h[...] - if_right(dot(w_v, g_right))).astype(BF16)
        gap = if_right(dot(tg_gap[:, :order], own)).astype(BF16)
        from_right[...] = gap
        to_right = less_gap(w_n_h, w_far, g_right, w_v, gap)
        hand_out(to_right, less_gap(p_n_h, p_far, g_right, p_v[...], gap), a, b)

    by_parity(None, odd)


def if_two_left(value):
    return jnp.where(lax.axis_index(AXES) > 1, value, jnp.zeros_like(value))


def if_two_right(value):
    last = lax.axis_size(AXES) - 2
    return jnp.where(lax.axis_index(AXES) < last, value, jnp.zeros_like(value))


def spikes_two_even(order, tg, v_one, near, pair2, w_vg_gap, after, from_left, from_right, scale):
    def even():
        t = tg[:, :order]
        gap = if_left(dot(t, w_vg_gap[:, :order]))
        scale[...] = (near[...].astype(F32) - gap).astype(BF16)
        s_v = dot(scale[...], v_one[...]).astype(BF16)
        from_left[...] = (-dot(scale[...], t)).astype(BF16)
        from_right[...] = dot(s_v, pair2[:order, :]).astype(BF16)

    by_parity(even, None)


def spikes_two_odd(
    order, tg, v_one, w_b, near, far, n_h, pair1, tg_gap, from_right, after, g, left, right, scale
):
    def odd():
        g[...] = less_gap(n_h, far, tg_gap[:, order:], v_one[...], from_right[...])
        through = dot(tg_gap[:, :order], w_b[...]).astype(BF16)
        gap = if_right(dot(v_one[...], through))
        scale[...] = (near[...].astype(F32) - gap).astype(BF16)
        s_t = dot(scale[...], tg[:, :order]).astype(BF16)
        left[...] = dot(s_t, pair1[:order, :]).astype(BF16)
        right[...] = dot(scale[...], v_one[...]).astype(BF16)

    by_parity(None, odd)


def top_value(g, from_left, from_right, a, b, x):
    def top(left, right):
        rows = g.shape[0]
        change = if_two_left(dot(from_left[...], left[:rows, :]))
        change += if_two_right(dot(from_right[...], right[:rows, :]))
        x[...] = (g[...].astype(F32) + change).astype(BF16)

    left_of_two = lax.rem(lax.axis_index(AXES), 4) < 2
    pl.when(left_of_two)(lambda: top(b, a))
    pl.when(jnp.logical_not(left_of_two))(lambda: top(a, b))


def top_even(g, from_left, from_right, a, b, x, x_out):
    def even():
        top_value(g, from_left, from_right, a, b, x)
        hand_over(x, x_out)

    by_parity(even, None)


def top_odd(g, from_left, from_right, a, b, x):
    by_parity(None, lambda: top_value(g, from_left, from_right, a, b, x))


def start_second(order, vg_b, w_b, x_even, x_odd, rest, out, sem):
    def start(x):
        copy = fetch(x, out.at[0], sem)
        rest[...] = vg_b[:, order:].astype(F32) - dot(w_b[...], x[...])
        copy.wait()

    by_parity(lambda: start(x_even), lambda: start(x_odd))


def write_second(order, vg_b, rest, x_next, right_on, out, row, sems):
    half, copies = order // 2, []
    for k in range(2):
        at = pl.ds(k * half, half)
        next_part = right_on(dot(vg_b[at, :order], x_next[:order, :]))
        row[at, :] = (rest[at, :] - next_part).astype(BF16)
        copies.append(fetch(row.at[at], out.at[1, at], sems.at[k]))
    for copy in copies:
        copy.wait()


def finish_odd(order, made, vg_b, rest, x_gap, out, row, sems):
    by_parity(None, lambda: write_second(order, vg_b, rest, x_gap, if_right, out, row, sems))


def finish_even(order, made, vg_b, rest, x_pair, out, row, sems):
    by_parity(lambda: write_second(order, vg_b, rest, x_pair, same, out, row, sems), None)


def exchanges(slab, count):
    pairs = [(i, i ^ 1) for i in range(count)]
    twos, other_twos = [], []
    for parity in (0, 1):
        over = [i ^ slab for i in range(count)]
        twos.append([(i, i ^ 2 if i % 2 == parity else over[i]) for i in range(count)])
        to = [((i - 2) ^ 2) + 2 if i % 2 == parity else over[i] for i in range(count)]
        for end in (parity, count - 2 + parity):
            to[end], to[end ^ 1], to[over[end ^ 1]] = end ^ 1, over[end ^ 1], end
        other_twos.append(list(enumerate(to)))
    after = [(i + 1) % count for i in range(count)]
    after[2], after[slab + 2], after[count - 1] = 0, 3, count - 5
    for first in range(slab + 3, count - 5, 4):
        after[first + 3] = first
    to_right = list(enumerate(after))
    to_left = [(count - 1 - i, count - 1 - j) for i, j in to_right]
    return pairs, twos, other_twos, to_right, to_left


def body(diag, lower, upper, right):
    order, rhs = diag.shape[1], right.shape[2]
    count = lax.axis_size(AXES)
    pairs, twos, other_twos, to_right, to_left = exchanges(lax.axis_size("dev"), count)

    def sent(block, route):
        return lax.ppermute(block, AXES, route)

    part = functools.partial
    square = 2 * order**3
    thin = 2 * order * order * rhs
    block = pltpu.VMEM((order, order), BF16)
    side = pltpu.VMEM((order, rhs), BF16)
    wide = bf16_array(order, order + rhs)
    full = bf16_array(order, order)
    slim = bf16_array(order, rhs)

    row_scratch = (pltpu.VMEM((order, order + rhs), BF16), pltpu.SemaphoreType.DMA((4,)))
    vg_odd, diag_b, lower_b = local_call(
        part(second_row_odd, order),
        [wide, full, full], [diag, upper, right, lower], square + thin, 4, row_scratch,
    )
    vg_gap = sent(vg_odd, to_right)
    own_arrays = [f32_array(order, rhs)] + [full] * 3
    spike_arrays = [full, full, f32_array(order, order), full]
    own_scratch = (block, side, pltpu.SemaphoreType.DMA((6,)))
    spikes = local_call(
        part(own_products_odd, order),
        spike_arrays + own_arrays, [diag, lower, upper, right, vg_odd, diag_b, lower_b],
        5 * square + 2 * thin, 4, own_scratch,
    )
    spikes, own = spikes[:4], [*spikes[4:], diag_b, lower_b]
    cut = 3 * order // 4
    vg_b, *to_pair = local_call(
        part(second_row, order),
        [wide, bf16_array(order, cut), bf16_array(order, order - cut + rhs)],
        [diag, upper, right, vg_odd, own[0]], square + thin, 3, (block, *row_scratch),
    )
    vg_pair = [sent(piece, pairs) for piece in to_pair]
    r, v_a, *held = local_call(
        part(own_products_even, order),
        own_arrays + [full] * 2, [diag, lower, upper, right, vg_b, *own], square + 2 * thin,
        4, own_scratch, {5 + i: i for i in range(6)},
    )
    w_a, w_b, m, n = spikes
    shares = [bf16_array(order + rows, order) for rows in (rhs // 2, rhs // 2, 0)]
    tg_odd, v_odd, w_vg_odd, *to_pair = local_call(
        part(level_one_odd, order),
        [wide, full, wide, *shares], [w_a, m, r, *vg_pair, n, w_b], 5 * square, 0, (block, block),
    )
    w_vg_gap = sent(w_vg_odd, to_right)
    w_a, w_b, m, n = local_call(
        part(spikes_own_even, order),
        spike_arrays, [vg_b, *held, v_a, vg_gap, *spikes], 4 * square,
        aliases={7 + i: i for i in range(4)},
    )
    tg, scale = local_call(
        part(scale_one_even, order),
        [wide, full], [w_a, m, r, vg_gap, tg_odd], 2 * square + 2 * thin, aliases={4: 0},
    )
    tg, v_one, *to_pair = local_call(
        part(spikes_one_even, order, 0),
        [wide, full, *shares], [scale, n, w_b, tg, v_odd, *to_pair], 3 * square + thin,
        0, (block, block, side), {3: 0, 4: 1, 5: 2, 6: 3, 7: 4},
    )
    tg_gap = sent(tg, to_left)
    v_one, *to_pair = local_call(
        part(spikes_one_even, order, 2),
        [full, *shares], [scale, n, w_b, tg, v_one, *to_pair], 3 * square + thin,
        0, (block, block, side), {4: 0, 5: 1, 6: 2, 7: 3},
    )
    pair = [sent(piece, pairs) for piece in to_pair]

    tall, tall_slim = f32_array(order, rhs), bf16_array(order + 16, rhs)
    near_even, n_h_even = local_call(
        part(pair_part_even, order), [full, tall], [tg, v_one, w_b, *pair[:2]], 2 * square + thin
    )
    near, far, w_far, p_far, p_v, n_h, w_h, w_n_h, p_n_h = local_call(
        part(pair_part_odd, order),
        [full] * 5 + [tall] * 4, [tg, v_one, w_b, *pair], 5 * square + 5 * thin,
    )
    g_even, a_even, b_even = local_call(
        part(level_two_even, order),
        [slim] * 3, [tg, w_b, near_even, n_h_even, pair[1], w_vg_gap], 6 * thin,
    )
    even_a, even_b = sent(a_even, twos[0]), sent(b_even, other_twos[0])
    left_even, right_even = local_call(
        part(spikes_two_even, order),
        [full, full], [tg, v_one, near_even, pair[2], w_vg_gap, a_even], 4 * square, 0, (block,),
    )
    from_right, a_odd, b_odd = local_call(
        part(level_two_odd, order),
        [slim, tall_slim, slim],
        [w_vg_odd, w_far, p_far, p_v, w_h, w_n_h, p_n_h, tg_gap, left_even], 6 * thin,
    )
    odd_a, odd_b = sent(a_odd, twos[1]), sent(b_odd, other_twos[1])
    g_odd, left_odd, right_odd = local_call(
        part(spikes_two_odd, order),
        [slim, full, full],
        [tg, v_one, w_b, near, far, n_h, pair[1], tg_gap, from_right, a_odd], 5 * square, 0, (block,),
    )
    x_even, x_out = local_call(
        top_even, [slim, tall_slim], [g_even, left_even, right_even, even_a, even_b], 2 * thin
    )
    x_gap = sent(x_out, to_left)
    x_odd = local_call(top_odd, [slim], [g_odd, left_odd, right_odd, odd_a, odd_b], 2 * thin)
    x_pair = sent(x_odd, pairs)
    values = jax.ShapeDtypeStruct((2, order, rhs), BF16)
    rest, made = local_call(
        part(start_second, order),
        [tall, values], [vg_b, w_b, x_even, x_odd], thin, 0, (pltpu.SemaphoreType.DMA,), None, True,
    )
    scratch = (side, pltpu.SemaphoreType.DMA((2,)))
    for kernel, x_next in ((finish_odd, x_gap), (finish_even, x_pair)):
        made = local_call(
            part(kernel, order), [values], [made, vg_b, rest, x_next], thin, 1, scratch, {0: 0}, True
        )
    return made


def solution(mesh):
    split = P(AXES, None, None)
    return jax.shard_map(
        body, mesh=mesh, in_specs=(split,) * 4, out_specs=split, check_vma=False
    )
```

```python
import functools

import jax
import jax.numpy as jnp
from jax import lax
from jax.experimental import pallas as pl
from jax.experimental.pallas import tpu as pltpu
from jax.sharding import PartitionSpec as P


AXES = ("grp", "dev")
BF16 = jnp.bfloat16
F32 = jnp.float32
VMEM_BYTES = 12 * 1024 * 1024


def is_odd():
    return lax.rem(lax.axis_index(AXES), 2) == 1


def if_left(value):
    return jnp.where(lax.axis_index(AXES) > 0, value, jnp.zeros_like(value))


def if_right(value):
    last = lax.axis_size(AXES) - 1
    return jnp.where(lax.axis_index(AXES) < last, value, jnp.zeros_like(value))


def dot(a, b):
    return jnp.dot(a, b, preferred_element_type=F32)


def by_parity(even, odd):
    odd_here = is_odd()
    if odd is not None:
        pl.when(odd_here)(odd)
    if even is not None:
        pl.when(jnp.logical_not(odd_here))(even)


def identity(order):
    rows = lax.broadcasted_iota(jnp.int32, (order, order), 0)
    return (rows == lax.broadcasted_iota(jnp.int32, (order, order), 1)).astype(F32)


def local_call(
    kernel, outs, ins, flops, in_hbm=0, scratch=(), aliases=None, out_in_hbm=False
):
    vmem = pl.BlockSpec(memory_space=pltpu.VMEM)
    hbm = pl.BlockSpec(memory_space=pl.ANY)
    many = len(outs) > 1
    places = [vmem] * len(outs)
    if out_in_hbm:
        places[-1] = pl.BlockSpec(memory_space=pltpu.HBM)
    ins = [pltpu.with_memory_space_constraint(x, pltpu.HBM) for x in ins[:in_hbm]] + ins[in_hbm:]
    return pl.pallas_call(
        kernel,
        out_shape=outs if many else outs[0],
        in_specs=[hbm] * in_hbm + [vmem] * (len(ins) - in_hbm),
        out_specs=places if many else places[0],
        scratch_shapes=list(scratch),
        input_output_aliases=aliases or {},
        compiler_params=pltpu.CompilerParams(vmem_limit_bytes=VMEM_BYTES),
        cost_estimate=pl.CostEstimate(flops=flops // 1000, bytes_accessed=0, transcendentals=0),
    )(*ins)


def bf16_array(rows, columns):
    return jax.ShapeDtypeStruct((rows, columns), BF16)


def f32_array(rows, columns):
    return jax.ShapeDtypeStruct((rows, columns), F32)


def fetch(source, target, sem):
    copy = pltpu.make_async_copy(source, target, sem)
    copy.start()
    return copy


def load_row(order, diag, upper, right, vg, diag_b, sides, sems, later=()):
    copies = [
        fetch(diag.at[1], diag_b, sems.at[0]),
        fetch(upper.at[1], sides.at[:, :order], sems.at[1]),
        fetch(right.at[1], sides.at[:, order:], sems.at[2]),
    ]
    for copy in later:
        copy.start()
    for copy in copies:
        copy.wait()
    vg[...] = dot(diag_b[...], sides[...]).astype(BF16)


def second_row_odd(order, diag, upper, right, lower, vg, diag_b, lower_b, sides, sems):
    def odd():
        later = pltpu.make_async_copy(lower.at[1], lower_b, sems.at[3])
        load_row(order, diag, upper, right, vg, diag_b, sides, sems, [later])
        later.wait()

    by_parity(None, odd)


def second_row(order, diag, upper, right, vg_odd, after, vg_b, *rest):
    *pieces, diag_b, sides, sems = rest

    def odd():
        vg_b[...] = vg_odd[...]

    def even():
        load_row(order, diag, upper, right, vg_b, diag_b, sides, sems)
        first = 0
        for piece in pieces:
            piece[...] = vg_b[:, first : first + piece.shape[1]]
            first += piece.shape[1]

    by_parity(even, odd)


def own_products_odd(
    order, diag, lower, upper, right, vg_odd, diag_b, lower_b,
    w_a, w_b, m, n, r, v_a, diag_a, lower_a, upper_a, right_a, sems,
):
    def odd():
        copies = first_row_copies(diag, lower, upper, right, diag_a, lower_a, upper_a, right_a, sems)
        for copy in copies:
            copy.start()
        w_b[...] = dot(diag_b[...], lower_b[...]).astype(BF16)
        first_right_side(order, copies, vg_odd, diag_a, upper_a, right_a, v_a, r)
        first_spikes(order, vg_odd, diag_a, lower_a, v_a, w_a, w_b, m, n)

    by_parity(None, odd)


def own_products_even(order, diag, lower, upper, right, vg_b, *rest):
    r, v_a, diag_a, lower_a, diag_b, lower_b, upper_a, right_a, sems = rest[6:]

    def even():
        copies = first_row_copies(diag, lower, upper, right, diag_a, lower_a, upper_a, right_a, sems)
        copies += [
            pltpu.make_async_copy(diag.at[1], diag_b, sems.at[4]),
            pltpu.make_async_copy(lower.at[1], lower_b, sems.at[5]),
        ]
        for copy in copies:
            copy.start()
        first_right_side(order, copies, vg_b, diag_a, upper_a, right_a, v_a, r)

    by_parity(even, None)


def spikes_own_even(order, vg_b, diag_a, lower_a, diag_b, lower_b, v_a, after, *rest):
    w_a, w_b, m, n = rest[4:]

    def even():
        w_b[...] = dot(diag_b[...], lower_b[...]).astype(BF16)
        first_spikes(order, vg_b, diag_a, lower_a, v_a, w_a, w_b, m, n)

    by_parity(even, None)


def first_row_copies(diag, lower, upper, right, diag_a, lower_a, upper_a, right_a, sems):
    pairs = (diag, diag_a), (upper, upper_a), (right, right_a), (lower, lower_a)
    return [pltpu.make_async_copy(x.at[0], y, sems.at[i]) for i, (x, y) in enumerate(pairs)]


def first_right_side(order, copies, vg_b, diag_a, upper_a, right_a, v_a, r):
    for copy in copies[:3]:
        copy.wait()
    v_a[...] = dot(diag_a[...], upper_a[...]).astype(BF16)
    g_a = dot(diag_a[...], right_a[...]).astype(BF16)
    r[...] = g_a.astype(F32) - dot(v_a[...], vg_b[:, order:])
    for copy in copies[3:]:
        copy.wait()


def first_spikes(order, vg_b, diag_a, lower_a, v_a, w_a, w_b, m, n):
    w_a[...] = dot(diag_a[...], lower_a[...]).astype(BF16)
    n[...] = dot(v_a[...], vg_b[:, :order]).astype(BF16)
    m[...] = dot(v_a[...], w_b[...])


def scale_one(order, w_a, m, r, v_left, g_left, scale, tg):
    first = 0
    eye = identity(order)
    for piece in v_left:
        at = slice(first, first + piece.shape[1])
        coupling = if_left(dot(w_a[...], piece[...])) + m[:, at]
        scale[:, at] = (eye[:, at] + coupling).astype(BF16)
        first = at.stop
    rest = (r[...] - if_left(dot(w_a[...], g_left[...]))).astype(BF16)
    tg[:, :order] = dot(scale[...], w_a[...]).astype(BF16)
    tg[:, order:] = dot(scale[...], rest).astype(BF16)


def spikes_one(order, scale, n, w_b, tg, v_one, w_t, w_v, w_g):
    v_one[...] = (-dot(scale[...], n[...])).astype(BF16)
    w_v[...] = dot(w_b[...], v_one[...]).astype(BF16)
    w_g[...] = dot(w_b[...], tg[:, order:]).astype(BF16)
    w_t[...] = dot(w_b[...], tg[:, :order]).astype(BF16)


def pack(side):
    columns = side.shape[1]
    return jnp.concatenate(
        [side[i : i + columns] for i in range(0, side.shape[0], columns)], axis=1
    )


def unpack(rows, columns):
    return jnp.concatenate(
        [rows[:, i : i + columns] for i in range(0, rows.shape[1], columns)], axis=0
    )


def hand_to_pair(order, blocks, side, to_pair):
    rows, first = pack(side), 0
    for block, piece in zip(blocks, to_pair):
        last = first + piece.shape[0] - order
        piece[:order, :] = block
        if last > first:
            piece[order:, :] = rows[first:last]
        first = last


def side_of_pair(order, got, columns):
    return unpack(jnp.concatenate([piece[order:, :] for piece in got], axis=0), columns)


def level_one_odd(order, w_a, m, r, v0, vg1, n, w_b, tg, v_one, w_vg, scale):
    columns = order - v0.shape[1]

    def odd():
        v_left, g_left = [v0, vg1.at[:, :columns]], vg1.at[:, columns:]
        scale_one(order, w_a, m, r, v_left, g_left, scale, tg)
        v_one[...] = (-dot(scale[...], n[...])).astype(BF16)
        w_vg[:, :order] = dot(w_b[...], v_one[...]).astype(BF16)
        w_vg[:, order:] = dot(w_b[...], tg[:, order:]).astype(BF16)

    by_parity(None, odd)


def scale_one_even(order, w_a, m, r, vg, tg_odd, tg, scale):
    v_left, g_left = [vg.at[:, :order]], vg.at[:, order:]
    by_parity(lambda: scale_one(order, w_a, m, r, v_left, g_left, scale, tg), None)


def spikes_one_even(order, place, scale, n, w_b, tg, *refs):
    v_one, *to_pair, w_t, w_v, w_g = refs[-7:]

    @pl.when(lax.rem(lax.axis_index(AXES), 4) == place)
    def _():
        spikes_one(order, scale, n, w_b, tg, v_one, w_t, w_v, w_g)
        hand_to_pair(order, [w_v[...], w_t[...], v_one[...]], w_g[...], to_pair)


def spikes_one_first(order, scale, n, w_b, tg, v_odd, tg_out, v_one, *rest):
    *to_pair, w_t, w_v, w_g = rest
    spikes_one_even(order, 0, scale, n, w_b, tg, v_one, *rest)

    def odd():
        w_t[...] = dot(w_b[...], tg[:, :order]).astype(BF16)
        hand_to_pair(order, [tg[:, :order], w_t[...], v_odd[...]], tg[:, order:], to_pair)

    by_parity(None, odd)


def same(value):
    return value


def pair_part_even(order, tg, v_one, w_b, pair0, pair1, near, n_h):
    def even():
        right = dot(pair0[:order, :], w_b[...]).astype(BF16)
        near[...] = (identity(order) - dot(v_one[...], right)).astype(BF16)
        side = side_of_pair(order, [pair0, pair1], n_h.shape[1])
        n_h[...] = tg[:, order:].astype(F32) - dot(v_one[...], side)

    by_parity(even, None)


def pair_part_odd(
    order, tg, v_one, w_b, pair0, pair1, pair2, near, far, w_far, p_far, p_v, n_h, w_h, w_n_h, p_n_h
):
    def odd():
        t, v_pair = tg[:, :order], pair2[...]
        near[...] = (identity(order) - dot(t, pair0[:order, :])).astype(BF16)
        far[...] = dot(near[...], v_one[...]).astype(BF16)
        w_far[...] = dot(w_b[...], far[...]).astype(BF16)
        p_far[...] = dot(v_pair, far[...]).astype(BF16)
        p_v[...] = dot(v_pair, v_one[...]).astype(BF16)
        side = side_of_pair(order, [pair0, pair1], n_h.shape[1])
        own = (tg[:, order:].astype(F32) + dot(t, side)).astype(BF16)
        scaled = dot(near[...], own)
        n_h[...] = scaled
        w_h[...] = dot(w_b[...], own)
        w_n_h[...] = dot(w_b[...], scaled.astype(BF16))
        p_n_h[...] = dot(v_pair, scaled.astype(BF16))

    by_parity(None, odd)


def hand_over(block, out):
    rows = block.shape[0]
    out[:rows, :] = block[...]
    if out.shape[0] > rows:
        out[rows:, :] = jnp.zeros((out.shape[0] - rows, out.shape[1]), BF16)


def hand_out(right, left, a, b):
    left_of_two = lax.rem(lax.axis_index(AXES), 4) < 2
    hand_over(jnp.where(left_of_two, right, left), a)
    b[...] = jnp.where(left_of_two, left, right)


def level_two_even(order, tg, w_b, near, n_h, pair1, w_vg_gap, g, a, b):
    def even():
        t = tg[:, :order]
        whole = (n_h[...] + if_left(dot(t, w_vg_gap[:, order:]))).astype(BF16)
        from_left = if_left(dot(w_vg_gap[:, :order], whole)).astype(BF16)
        value = (dot(near[...], whole) - dot(t, from_left)).astype(BF16)
        onward = (-dot(pair1[:order, :], dot(w_b[...], value).astype(BF16))).astype(BF16)
        g[...] = value
        hand_out(onward, value, a, b)

    by_parity(even, None)


def less_gap(start, gap, g_right, further, from_right):
    return (start[...] - if_right(dot(gap[...], g_right)) - dot(further, from_right)).astype(BF16)


def level_two_odd(
    order, w_vg, w_far, p_far, p_v, w_h, w_n_h, p_n_h, tg_gap, after, from_right, a, b
):
    def odd():
        g_right, w_v = tg_gap[:, order:], w_vg[:, :order]
        own = (w_h[...] - if_right(dot(w_v, g_right))).astype(BF16)
        gap = if_right(dot(tg_gap[:, :order], own)).astype(BF16)
        from_right[...] = gap
        to_right = less_gap(w_n_h, w_far, g_right, w_v, gap)
        hand_out(to_right, less_gap(p_n_h, p_far, g_right, p_v[...], gap), a, b)

    by_parity(None, odd)


def if_two_left(value):
    return jnp.where(lax.axis_index(AXES) > 1, value, jnp.zeros_like(value))


def if_two_right(value):
    last = lax.axis_size(AXES) - 2
    return jnp.where(lax.axis_index(AXES) < last, value, jnp.zeros_like(value))


def spikes_two_even(order, tg, v_one, near, pair2, w_vg_gap, after, from_left, from_right, scale):
    def even():
        t = tg[:, :order]
        gap = if_left(dot(t, w_vg_gap[:, :order]))
        scale[...] = (near[...].astype(F32) - gap).astype(BF16)
        s_v = dot(scale[...], v_one[...]).astype(BF16)
        from_left[...] = (-dot(scale[...], t)).astype(BF16)
        from_right[...] = dot(s_v, pair2[:order, :]).astype(BF16)

    by_parity(even, None)


def spikes_two_odd(
    order, tg, v_one, w_b, near, far, n_h, pair1, tg_gap, from_right, after, g, left, right, scale
):
    def odd():
        g[...] = less_gap(n_h, far, tg_gap[:, order:], v_one[...], from_right[...])
        through = dot(tg_gap[:, :order], w_b[...]).astype(BF16)
        gap = if_right(dot(v_one[...], through))
        scale[...] = (near[...].astype(F32) - gap).astype(BF16)
        s_t = dot(scale[...], tg[:, :order]).astype(BF16)
        left[...] = dot(s_t, pair1[:order, :]).astype(BF16)
        right[...] = dot(scale[...], v_one[...]).astype(BF16)

    by_parity(None, odd)


def top_value(g, from_left, from_right, a, b, x):
    def top(left, right):
        rows = g.shape[0]
        change = if_two_left(dot(from_left[...], left[:rows, :]))
        change += if_two_right(dot(from_right[...], right[:rows, :]))
        x[...] = (g[...].astype(F32) + change).astype(BF16)

    left_of_two = lax.rem(lax.axis_index(AXES), 4) < 2
    pl.when(left_of_two)(lambda: top(b, a))
    pl.when(jnp.logical_not(left_of_two))(lambda: top(a, b))


def top_even(g, from_left, from_right, a, b, x, x_out):
    def even():
        top_value(g, from_left, from_right, a, b, x)
        hand_over(x, x_out)

    by_parity(even, None)


def top_odd(g, from_left, from_right, a, b, x):
    by_parity(None, lambda: top_value(g, from_left, from_right, a, b, x))


def start_second(order, vg_b, w_b, x_even, x_odd, rest, out, sem):
    def start(x):
        copy = fetch(x, out.at[0], sem)
        rest[...] = vg_b[:, order:].astype(F32) - dot(w_b[...], x[...])
        copy.wait()

    by_parity(lambda: start(x_even), lambda: start(x_odd))


def write_second(order, vg_b, rest, x_next, right_on, out, row, sems):
    half, copies = order // 2, []
    for k in range(2):
        at = pl.ds(k * half, half)
        next_part = right_on(dot(vg_b[at, :order], x_next[:order, :]))
        row[at, :] = (rest[at, :] - next_part).astype(BF16)
        copies.append(fetch(row.at[at], out.at[1, at], sems.at[k]))
    for copy in copies:
        copy.wait()


def finish_odd(order, made, vg_b, rest, x_gap, out, row, sems):
    by_parity(None, lambda: write_second(order, vg_b, rest, x_gap, if_right, out, row, sems))


def finish_even(order, made, vg_b, rest, x_pair, out, row, sems):
    by_parity(lambda: write_second(order, vg_b, rest, x_pair, same, out, row, sems), None)


def exchanges(slab, count):
    pairs = [(i, i ^ 1) for i in range(count)]
    twos, other_twos = [], []
    for parity in (0, 1):
        over = [i ^ slab for i in range(count)]
        twos.append([(i, i ^ 2 if i % 2 == parity else over[i]) for i in range(count)])
        to = [((i - 2) ^ 2) + 2 if i % 2 == parity else over[i] for i in range(count)]
        for end in (parity, count - 2 + parity):
            to[end], to[end ^ 1], to[over[end ^ 1]] = end ^ 1, over[end ^ 1], end
        other_twos.append(list(enumerate(to)))
    after = [(i + 1) % count for i in range(count)]
    after[2], after[slab + 2], after[count - 1] = 0, 3, count - 5
    for first in range(slab + 3, count - 5, 4):
        after[first + 3] = first
    to_right = list(enumerate(after))
    to_left = [(count - 1 - i, count - 1 - j) for i, j in to_right]
    return pairs, twos, other_twos, to_right, to_left


def body(diag, lower, upper, right):
    order, rhs = diag.shape[1], right.shape[2]
    count = lax.axis_size(AXES)
    pairs, twos, other_twos, to_right, to_left = exchanges(lax.axis_size("dev"), count)

    def sent(block, route):
        return lax.ppermute(block, AXES, route)

    part = functools.partial
    square = 2 * order**3
    thin = 2 * order * order * rhs
    block = pltpu.VMEM((order, order), BF16)
    side = pltpu.VMEM((order, rhs), BF16)
    wide = bf16_array(order, order + rhs)
    full = bf16_array(order, order)
    slim = bf16_array(order, rhs)

    row_scratch = (pltpu.VMEM((order, order + rhs), BF16), pltpu.SemaphoreType.DMA((4,)))
    vg_odd, diag_b, lower_b = local_call(
        part(second_row_odd, order),
        [wide, full, full], [diag, upper, right, lower], square + thin, 4, row_scratch,
    )
    vg_gap = sent(vg_odd, to_right)
    own_arrays = [f32_array(order, rhs)] + [full] * 3
    spike_arrays = [full, full, f32_array(order, order), full]
    own_scratch = (block, side, pltpu.SemaphoreType.DMA((6,)))
    spikes = local_call(
        part(own_products_odd, order),
        spike_arrays + own_arrays, [diag, lower, upper, right, vg_odd, diag_b, lower_b],
        5 * square + 2 * thin, 4, own_scratch,
    )
    spikes, own = spikes[:4], [*spikes[4:], diag_b, lower_b]
    cut = 3 * order // 4
    vg_b, *to_pair = local_call(
        part(second_row, order),
        [wide, bf16_array(order, cut), bf16_array(order, order - cut + rhs)],
        [diag, upper, right, vg_odd, own[0]], square + thin, 3, (block, *row_scratch),
    )
    vg_pair = [sent(piece, pairs) for piece in to_pair]
    r, v_a, *held = local_call(
        part(own_products_even, order),
        own_arrays + [full] * 2, [diag, lower, upper, right, vg_b, *own], square + 2 * thin,
        4, own_scratch, {5 + i: i for i in range(6)},
    )
    w_a, w_b, m, n = spikes
    shares = [bf16_array(order + rows, order) for rows in (rhs // 2, rhs // 2, 0)]
    tg_odd, v_odd, w_vg_odd = local_call(
        part(level_one_odd, order),
        [wide, full, wide], [w_a, m, r, *vg_pair, n, w_b], 4 * square, 0, (block,),
    )
    w_vg_gap = sent(w_vg_odd, to_right)
    w_a, w_b, m, n = local_call(
        part(spikes_own_even, order),
        spike_arrays, [vg_b, *held, v_a, vg_gap, *spikes], 4 * square,
        aliases={7 + i: i for i in range(4)},
    )
    tg, scale = local_call(
        part(scale_one_even, order),
        [wide, full], [w_a, m, r, vg_gap, tg_odd], 2 * square + 2 * thin, aliases={4: 0},
    )
    tg, v_one, *to_pair = local_call(
        part(spikes_one_first, order),
        [wide, full, *shares], [scale, n, w_b, tg, v_odd], 3 * square + thin,
        0, (block, block, side), {3: 0, 4: 1},
    )
    tg_gap = sent(tg, to_left)
    v_one, *to_pair = local_call(
        part(spikes_one_even, order, 2),
        [full, *shares], [scale, n, w_b, tg, v_one, *to_pair], 3 * square + thin,
        0, (block, block, side), {4: 0, 5: 1, 6: 2, 7: 3},
    )
    pair = [sent(piece, pairs) for piece in to_pair]

    tall, tall_slim = f32_array(order, rhs), bf16_array(order + 16, rhs)
    near_even, n_h_even = local_call(
        part(pair_part_even, order), [full, tall], [tg, v_one, w_b, *pair[:2]], 2 * square + thin
    )
    near, far, w_far, p_far, p_v, n_h, w_h, w_n_h, p_n_h = local_call(
        part(pair_part_odd, order),
        [full] * 5 + [tall] * 4, [tg, v_one, w_b, *pair], 5 * square + 5 * thin,
    )
    g_even, a_even, b_even = local_call(
        part(level_two_even, order),
        [slim] * 3, [tg, w_b, near_even, n_h_even, pair[1], w_vg_gap], 6 * thin,
    )
    even_a, even_b = sent(a_even, twos[0]), sent(b_even, other_twos[0])
    left_even, right_even = local_call(
        part(spikes_two_even, order),
        [full, full], [tg, v_one, near_even, pair[2], w_vg_gap, a_even], 4 * square, 0, (block,),
    )
    from_right, a_odd, b_odd = local_call(
        part(level_two_odd, order),
        [slim, tall_slim, slim],
        [w_vg_odd, w_far, p_far, p_v, w_h, w_n_h, p_n_h, tg_gap, left_even], 6 * thin,
    )
    odd_a, odd_b = sent(a_odd, twos[1]), sent(b_odd, other_twos[1])
    g_odd, left_odd, right_odd = local_call(
        part(spikes_two_odd, order),
        [slim, full, full],
        [tg, v_one, w_b, near, far, n_h, pair[1], tg_gap, from_right, a_odd], 5 * square, 0, (block,),
    )
    x_even, x_out = local_call(
        top_even, [slim, tall_slim], [g_even, left_even, right_even, even_a, even_b], 2 * thin
    )
    x_gap = sent(x_out, to_left)
    x_odd = local_call(top_odd, [slim], [g_odd, left_odd, right_odd, odd_a, odd_b], 2 * thin)
    x_pair = sent(x_odd, pairs)
    values = jax.ShapeDtypeStruct((2, order, rhs), BF16)
    rest, made = local_call(
        part(start_second, order),
        [tall, values], [vg_b, w_b, x_even, x_odd], thin, 0, (pltpu.SemaphoreType.DMA,), None, True,
    )
    scratch = (side, pltpu.SemaphoreType.DMA((2,)))
    for kernel, x_next in ((finish_odd, x_gap), (finish_even, x_pair)):
        made = local_call(
            part(kernel, order), [values], [made, vg_b, rest, x_next], thin, 1, scratch, {0: 0}, True
        )
    return made


def solution(mesh):
    split = P(AXES, None, None)
    return jax.shard_map(
        body, mesh=mesh, in_specs=(split,) * 4, out_specs=split, check_vma=False
    )
```
